32 devices in a mesh: dp: 8 (over z, x), fsdp: 4 (over y, core).
Axes of the slice: x: 2, y: 2, z: 4, core: 2. Of those that a mesh axis runs over, the one named last changes fastest.
Arguments:
- act: bfloat16 [8192, 1536], P(('dp', 'fsdp')), may hold values from -6 to 6
- cotangent: bfloat16 [8192, 1536], P(('dp', 'fsdp')), may hold values from -6 to 6
- item_counts: int32 [32], P(('dp', 'fsdp')), may hold values from 0 to 1
- item_lengths: int32 [32], P(('dp', 'fsdp')), may hold values from 128 to 256, as said below
- time_steps: int32 [32], P(('dp', 'fsdp')), may hold values from 0 to 999
- ada_weight: float32 [1536, 4608], P(None, ('dp', 'fsdp')), may hold values from -0.15625 to 0.15625
- ada_first: float32 [1536, 4608], P(None, ('dp', 'fsdp')), may hold values from -0.00015258789 to 0.00015258789
- ada_second: float32 [1536, 4608], P(None, ('dp', 'fsdp')), may hold values from 4.5470155e-11 to 1.8188062e-10
- ada_average: float32 [1536, 4608], P(None, ('dp', 'fsdp')), may hold values from -0.15625 to 0.15625
- in_weight: float32 [1536, 6144], P(None, ('dp', 'fsdp')), may hold values from -0.25515518 to 0.25515518
- in_first: float32 [1536, 6144], P(None, ('dp', 'fsdp')), may hold values from -0.00015258789 to 0.00015258789
- in_second: float32 [1536, 6144], P(None, ('dp', 'fsdp')), may hold values from 4.5470155e-11 to 1.8188062e-10
- in_average: float32 [1536, 6144], P(None, ('dp', 'fsdp')), may hold values from -0.15625 to 0.15625
- x_weight: float32 [3072, 128], P(('dp', 'fsdp')), may hold values from -0.109375 to 0.109375
- x_first: float32 [3072, 128], P(('dp', 'fsdp')), may hold values from -0.00015258789 to 0.00015258789
- x_second: float32 [3072, 128], P(('dp', 'fsdp')), may hold values from 4.5470155e-11 to 1.8188062e-10
- x_average: float32 [3072, 128], P(('dp', 'fsdp')), may hold values from -0.109375 to 0.109375
- dt_weight: float32 [96, 3072], P(None, ('dp', 'fsdp')), may hold values from -0.625 to 0.625
- dt_first: float32 [96, 3072], P(None, ('dp', 'fsdp')), may hold values from -0.00015258789 to 0.00015258789
- dt_second: float32 [96, 3072], P(None, ('dp', 'fsdp')), may hold values from 4.5470155e-11 to 1.8188062e-10
- dt_average: float32 [96, 3072], P(None, ('dp', 'fsdp')), may hold values from -0.625 to 0.625
- chan_table: float32 [23, 3072], P(None, ('dp', 'fsdp')), may hold values from -7 to 3
- chan_first: float32 [23, 3072], P(None, ('dp', 'fsdp')), may hold values from -0.00015258789 to 0.00015258789
- chan_second: float32 [23, 3072], P(None, ('dp', 'fsdp')), may hold values from 4.5470155e-11 to 1.8188062e-10
- chan_average: float32 [23, 3072], P(None, ('dp', 'fsdp')), may hold values from -7 to 3
- out_weight: float32 [3072, 1536], P(('dp', 'fsdp')), may hold values from -0.4375 to 0.4375
- out_first: float32 [3072, 1536], P(('dp', 'fsdp')), may hold values from -0.00015258789 to 0.00015258789
- out_second: float32 [3072, 1536], P(('dp', 'fsdp')), may hold values from 4.5470155e-11 to 1.8188062e-10
- out_average: float32 [3072, 1536], P(('dp', 'fsdp')), may hold values from -0.4375 to 0.4375
Outputs:
- final: float32 [8192, 1536], P(('dp', 'fsdp'))
- act_grad: float32 [8192, 1536], P(('dp', 'fsdp'))
- grad_norm: float32 [], replicated
- ada_first_new: float32 [1536, 4608], P(None, ('dp', 'fsdp'))
- ada_second_new: float32 [1536, 4608], P(None, ('dp', 'fsdp'))
- ada_weight_new: float32 [1536, 4608], P(None, ('dp', 'fsdp'))
- ada_average_new: float32 [1536, 4608], P(None, ('dp', 'fsdp'))
- in_first_new: float32 [1536, 6144], P(None, ('dp', 'fsdp'))
- in_second_new: float32 [1536, 6144], P(None, ('dp', 'fsdp'))
- in_weight_new: float32 [1536, 6144], P(None, ('dp', 'fsdp'))
- in_average_new: float32 [1536, 6144], P(None, ('dp', 'fsdp'))
- x_first_new: float32 [3072, 128], P(('dp', 'fsdp'))
- x_second_new: float32 [3072, 128], P(('dp', 'fsdp'))
- x_weight_new: float32 [3072, 128], P(('dp', 'fsdp'))
- x_average_new: float32 [3072, 128], P(('dp', 'fsdp'))
- dt_first_new: float32 [96, 3072], P(None, ('dp', 'fsdp'))
- dt_second_new: float32 [96, 3072], P(None, ('dp', 'fsdp'))
- dt_weight_new: float32 [96, 3072], P(None, ('dp', 'fsdp'))
- dt_average_new: float32 [96, 3072], P(None, ('dp', 'fsdp'))
- chan_first_new: float32 [23, 3072], P(None, ('dp', 'fsdp'))
- chan_second_new: float32 [23, 3072], P(None, ('dp', 'fsdp'))
- chan_table_new: float32 [23, 3072], P(None, ('dp', 'fsdp'))
- chan_average_new: float32 [23, 3072], P(None, ('dp', 'fsdp'))
- out_first_new: float32 [3072, 1536], P(('dp', 'fsdp'))
- out_second_new: float32 [3072, 1536], P(('dp', 'fsdp'))
- out_weight_new: float32 [3072, 1536], P(('dp', 'fsdp'))
- out_average_new: float32 [3072, 1536], P(('dp', 'fsdp'))
The draws below stay inside these ranges and needn't reach their ends.
Inputs may be any that keep to these rules, and one draw needn't show every extreme that they name: `item_lengths`: the first item slot of the whole batch is full.
All inputs are finite; a program needn't handle non-finite values.
Results may differ from the reference program's by a relative error of at most 0.012.
The reference program's roundings to bfloat16 on the way count: a program that leaves them out, or rounds other values in their place, can miss the bound.
Values may be sent and summed in bfloat16 or wider, within the bound.
No kernel may reach another device: no remote copies, remote signals or barrier semaphores. Data moves between devices by JAX's collectives and lax.ppermute only.
A program may use at most 320 MiB of HBM per device.

```python
import math
import jax
import jax.numpy as jnp
from jax import lax

D = 1536
E = 3072
N = 16
R = 96
CONV = 4
ITEM = 256
BLOCK = 32
SLOTS = 1
STEP = 10
CH = 23
TOKENS = 8192
ITEMS = 32
PARAMS = 21992448
N_DP = 8
N_FSDP = 4


def draw_item_counts(key, part):
    key = jax.random.fold_in(key, 11)
    values = jax.random.randint(key, (N_DP * N_FSDP,), 0, SLOTS + 1)
    return values.at[0].set(SLOTS).astype(jnp.int32)


def draw_item_lengths(key, part):
    key = jax.random.fold_in(key, 13)
    values = jax.random.randint(key, (SLOTS * N_DP * N_FSDP,), ITEM // 2, ITEM + 1)
    return values.at[0].set(ITEM).astype(jnp.int32)


def draw_in_weight(key, part):
    key = jax.random.fold_in(key, 17)
    keys = jax.random.split(key, 2)
    position = jnp.arange(2 * E, dtype=jnp.float32) / (2 * E)
    common = jax.random.truncated_normal(keys[1], -4.0, 4.0, (1, 2 * E), jnp.float32) * 0.4
    base = jax.random.truncated_normal(keys[0], -4.0, 4.0, (D, 2 * E), jnp.float32)
    ramp = 0.6 + 1.2 * position
    return (base * ramp[None, :] + common) * D ** (-0.5)


def channel_rows(key, spread):
    keys = jax.random.split(key, 5)
    taps = jax.random.truncated_normal(keys[0], -4.0, 4.0, (CONV, E), jnp.float32) * spread
    bias = jax.random.uniform(keys[1], (1, E), jnp.float32, -0.3, 0.3)
    step0 = jnp.exp(jax.random.uniform(keys[2], (1, E), jnp.float32, math.log(0.001), math.log(0.1)))
    step_bias = jnp.log(jnp.expm1(step0))
    skip = jax.random.uniform(keys[3], (1, E), jnp.float32, 0.5, 1.5)
    decay_log = jnp.log(jax.random.uniform(keys[4], (N, E), jnp.float32, 1.0, 16.0))
    return jnp.concatenate([taps, bias, step_bias, skip, decay_log], axis=0)


def draw_chan_table(key, part):
    key = jax.random.fold_in(key, 19)
    return channel_rows(key, 0.5)


def draw_chan_average(key, part):
    key = jax.random.fold_in(key, 23)
    return channel_rows(key, 0.5)


def touch_ends(array, stream_key, smallest, largest):
    longest = array.shape.index(max(array.shape))
    spots = []
    for shift in (0, 1):
        where = [jax.random.randint(jax.random.fold_in(stream_key, axis), (), 0, length) for axis, length in enumerate(array.shape)]
        where[longest] = (where[longest] + shift) % array.shape[longest]
        spots.append(tuple(where))
    return array.at[spots[0]].set(smallest).at[spots[1]].set(largest)


def block_scale(key, shape, shards, least, largest):
    def one(dim, shards_of):
        steps = jax.random.uniform(jax.random.fold_in(jax.random.fold_in(key, 6), dim), (shards_of,), jnp.float32, least / len(shards), largest / len(shards))
        return jnp.repeat(jnp.exp(steps), shape[dim] // shards_of).reshape((-1,) + (1,) * (len(shape) - dim - 1))

    level = one(*shards[0])
    for cut in shards[1:]:
        level = level * one(*cut)
    return level


def normal_values(key, shape, width, reach, cuts=(), kind=jnp.bfloat16):
    values = width * jax.random.normal(key, shape, jnp.float32)
    if cuts:
        values = values * block_scale(key, shape, cuts, -0.22, 0.18)
    return jnp.clip(values, -reach, reach).astype(kind)


def setup_inputs(seed: int = 0) -> dict:
    arg_keys = jax.random.split(jax.random.key(seed), 30)
    act = normal_values(arg_keys[0], (TOKENS, D), 1.0, 6.0, ((0, 32),))
    cotangent = normal_values(arg_keys[1], (TOKENS, D), 1.0, 6.0, ((0, 32),))
    item_counts = draw_item_counts(jax.random.fold_in(arg_keys[29], 71), 0)
    item_lengths = draw_item_lengths(jax.random.fold_in(arg_keys[29], 71), 0)
    time_steps = touch_ends(jax.random.randint(arg_keys[4], (ITEMS,), 0, 1000), jax.random.fold_in(arg_keys[4], 1), 0, 999).astype(jnp.int32)
    ada_weight = normal_values(arg_keys[5], (D, 3 * D), D ** -0.5, 0.15625, ((1, 32),), jnp.float32)
    ada_first = normal_values(arg_keys[6], (D, 3 * D), (0.111 / PARAMS ** 0.5), 0.00015258789, ((1, 32),), jnp.float32)
    ada_second = jnp.clip(jnp.exp(math.log(1.8188062167467933e-10) - 1.3862944 * jax.random.uniform(arg_keys[7], (D, 3 * D), jnp.float32) ** block_scale(arg_keys[7], (D, 3 * D), ((1, 32),), -0.2, 0.2)), 4.547015541866983e-11, 1.8188062167467933e-10)
    ada_average = normal_values(arg_keys[8], (D, 3 * D), D ** -0.5, 0.15625, ((1, 32),), jnp.float32)
    in_weight = draw_in_weight(jax.random.fold_in(arg_keys[29], 71), 0)
    in_first = normal_values(arg_keys[10], (D, 2 * E), (0.111 / PARAMS ** 0.5), 0.00015258789, ((1, 32),), jnp.float32)
    in_second = jnp.clip(jnp.exp(math.log(1.8188062167467933e-10) - 1.3862944 * jax.random.uniform(arg_keys[11], (D, 2 * E), jnp.float32) ** block_scale(arg_keys[11], (D, 2 * E), ((1, 32),), -0.2, 0.2)), 4.547015541866983e-11, 1.8188062167467933e-10)
    in_average = normal_values(arg_keys[12], (D, 2 * E), D ** -0.5, 0.15625, ((1, 32),), jnp.float32)
    x_weight = normal_values(arg_keys[13], (E, R + 2 * N), E ** -0.5, 0.109375, ((0, 32),), jnp.float32)
    x_first = normal_values(arg_keys[14], (E, R + 2 * N), (0.111 / PARAMS ** 0.5), 0.00015258789, ((0, 32),), jnp.float32)
    x_second = jnp.clip(jnp.exp(math.log(1.8188062167467933e-10) - 1.3862944 * jax.random.uniform(arg_keys[15], (E, R + 2 * N), jnp.float32) ** block_scale(arg_keys[15], (E, R + 2 * N), ((0, 32),), -0.2, 0.2)), 4.547015541866983e-11, 1.8188062167467933e-10)
    x_average = normal_values(arg_keys[16], (E, R + 2 * N), E ** -0.5, 0.109375, ((0, 32),), jnp.float32)
    dt_weight = normal_values(arg_keys[17], (R, E), R ** -0.5, 0.625, ((1, 32),), jnp.float32)
    dt_first = normal_values(arg_keys[18], (R, E), (0.111 / PARAMS ** 0.5), 0.00015258789, ((1, 32),), jnp.float32)
    dt_second = jnp.clip(jnp.exp(math.log(1.8188062167467933e-10) - 1.3862944 * jax.random.uniform(arg_keys[19], (R, E), jnp.float32) ** block_scale(arg_keys[19], (R, E), ((1, 32),), -0.2, 0.2)), 4.547015541866983e-11, 1.8188062167467933e-10)
    dt_average = normal_values(arg_keys[20], (R, E), R ** -0.5, 0.625, ((1, 32),), jnp.float32)
    chan_table = draw_chan_table(jax.random.fold_in(arg_keys[29], 71), 0)
    chan_first = normal_values(arg_keys[22], (CH, E), (0.111 / PARAMS ** 0.5), 0.00015258789, ((1, 32),), jnp.float32)
    chan_second = jnp.clip(jnp.exp(math.log(1.8188062167467933e-10) - 1.3862944 * jax.random.uniform(arg_keys[23], (CH, E), jnp.float32) ** block_scale(arg_keys[23], (CH, E), ((1, 32),), -0.2, 0.2)), 4.547015541866983e-11, 1.8188062167467933e-10)
    chan_average = draw_chan_average(jax.random.fold_in(arg_keys[29], 71), 0)
    out_weight = normal_values(arg_keys[25], (E, D), (E // 16) ** -0.5, 0.4375, ((0, 32),), jnp.float32)
    out_first = normal_values(arg_keys[26], (E, D), (0.111 / PARAMS ** 0.5), 0.00015258789, ((0, 32),), jnp.float32)
    out_second = jnp.clip(jnp.exp(math.log(1.8188062167467933e-10) - 1.3862944 * jax.random.uniform(arg_keys[27], (E, D), jnp.float32) ** block_scale(arg_keys[27], (E, D), ((0, 32),), -0.2, 0.2)), 4.547015541866983e-11, 1.8188062167467933e-10)
    out_average = normal_values(arg_keys[28], (E, D), (E // 16) ** -0.5, 0.4375, ((0, 32),), jnp.float32)
    return dict(act=act, cotangent=cotangent, item_counts=item_counts, item_lengths=item_lengths, time_steps=time_steps, ada_weight=ada_weight, ada_first=ada_first, ada_second=ada_second, ada_average=ada_average, in_weight=in_weight, in_first=in_first, in_second=in_second, in_average=in_average, x_weight=x_weight, x_first=x_first, x_second=x_second, x_average=x_average, dt_weight=dt_weight, dt_first=dt_first, dt_second=dt_second, dt_average=dt_average, chan_table=chan_table, chan_first=chan_first, chan_second=chan_second, chan_average=chan_average, out_weight=out_weight, out_first=out_first, out_second=out_second, out_average=out_average)


@jax.custom_vjp
def low(v):
    return lax.optimization_barrier(v.astype(jnp.bfloat16)).astype(jnp.float32)

@jax.custom_vjp
def low_back(v):
    return v

def low_keep(v):
    return (low(v), None)

def low_pass(kept, grad):
    return (grad,)

def back_keep(v):
    return (v, None)

def back_low(kept, grad):
    return (low(grad),)
low.defvjp(low_keep, low_pass)
low_back.defvjp(back_keep, back_low)

def exact(left, right):
    return jnp.dot(left, right, precision=lax.Precision.HIGHEST, preferred_element_type=jnp.float32)

def embed_time(steps):
    half = D // 2
    freqs = jnp.exp(-math.log(10000.0) * jnp.arange(half, dtype=jnp.float32) / half)
    angles = steps.astype(jnp.float32)[:, None] * freqs[None, :]
    return jax.nn.silu(jnp.concatenate([jnp.cos(angles), jnp.sin(angles)], axis=1))

def modulate(x, mod):
    mean = lax.optimization_barrier(jnp.mean(x, axis=2, keepdims=True))
    centered = x - mean
    var = lax.optimization_barrier(jnp.mean(centered * centered, axis=2, keepdims=True))
    normed = centered * lax.rsqrt(var + 1e-06)
    return normed * (1.0 + mod[:, None, D:2 * D]) + mod[:, None, :D]

def mix_conv(xs, chan):
    padded = jnp.pad(xs, ((0, 0), (CONV - 1, 0), (0, 0)))
    pre = chan[CONV][None, None, :]
    for k in range(CONV):
        pre = pre + padded[:, k:k + ITEM, :] * chan[k][None, None, :]
    return jax.nn.silu(pre)

def finish(x, o, mod):
    return x + mod[:, None, 2 * D:] * o

def selective(u, dtp, bc, z, chan):
    count = u.shape[0]
    blocks = ITEM // BLOCK
    step = jax.nn.softplus(dtp + chan[CONV + 1])
    a_neg = -jnp.exp(chan[CONV + 3:])

    def split(v):
        return jnp.moveaxis(v.reshape(count, blocks, BLOCK, v.shape[-1]), 1, 0)

    @jax.checkpoint
    def block(state, pieces):

        def advance(carry, one):
            u_now, step_now, b_now, c_now = one
            carry = jnp.exp(step_now[:, None, :] * a_neg[None]) * carry + b_now[:, :, None] * (step_now * u_now)[:, None, :]
            return (carry, lax.optimization_barrier(jnp.sum(carry * c_now[:, :, None], axis=1)))
        moved = tuple((jnp.moveaxis(p, 1, 0) for p in pieces))
        state, outs = lax.scan(advance, state, moved)
        return (state, jnp.moveaxis(outs, 0, 1))
    start = jnp.zeros((count, N, E), jnp.float32)
    _, outs = lax.scan(block, start, (split(u), split(step), split(bc[..., :N]), split(bc[..., N:])))
    y = jnp.moveaxis(outs, 0, 1).reshape(count, ITEM, E) + chan[CONV + 2] * u
    return y * jax.nn.silu(z)

def forward(params, x, steps):
    ada, w_in, w_x, w_dt, chan, w_out = params
    chan = low(chan)
    count = x.shape[0]
    cond = low(embed_time(steps))
    mod = low_back(exact(cond, low(ada)))
    h = modulate(x, mod)
    xz = low_back(exact(low(h).reshape(-1, D), low(w_in))).reshape(count, ITEM, 2 * E)
    u = mix_conv(xz[..., :E], chan)
    proj = low_back(exact(low(u).reshape(-1, E), low(w_x))).reshape(count, ITEM, R + 2 * N)
    dtp = low_back(exact(low(proj[..., :R]).reshape(-1, R), low(w_dt))).reshape(count, ITEM, E)
    yg = selective(u, dtp, proj[..., R:], xz[..., E:], chan)
    o = low_back(exact(low(yg).reshape(-1, E), low(w_out))).reshape(count, ITEM, D)
    return finish(x, o, mod)

def adamw(weight, first, second, average, grad, factor, learn_rate, weight_decay):
    ema_keep = min(0.9999, (1.0 + STEP) / (10.0 + STEP))
    grad = grad * factor
    first = 0.9 * first + 0.1 * grad
    second = 0.999 * second + 0.001 * grad * grad
    first_hat = first / (1.0 - 0.9 ** STEP)
    second_hat = second / (1.0 - 0.999 ** STEP)
    weight = weight - learn_rate * (first_hat / (jnp.sqrt(second_hat) + 1e-08) + weight_decay * weight)
    average = ema_keep * average + (1.0 - ema_keep) * weight
    return (first, second, weight, average)

def reference(act, cotangent, item_counts, item_lengths, time_steps, ada_weight, ada_first, ada_second, ada_average, in_weight, in_first, in_second, in_average, x_weight, x_first, x_second, x_average, dt_weight, dt_first, dt_second, dt_average, chan_table, chan_first, chan_second, chan_average, out_weight, out_first, out_second, out_average):
    devices = N_DP * N_FSDP
    params = (ada_weight, in_weight, x_weight, dt_weight, chan_table, out_weight)
    live_items = jnp.arange(SLOTS, dtype=jnp.int32)[None, :] < item_counts[:, None]
    live_rows = jnp.arange(ITEM, dtype=jnp.int32)[None, None, :] < item_lengths.reshape(devices, SLOTS)[:, :, None]
    live = (live_items[:, :, None] & live_rows).astype(jnp.float32)
    x_all = act.astype(jnp.float32).reshape(devices, SLOTS, ITEM, D)
    cot_all = cotangent.astype(jnp.float32).reshape(devices, SLOTS, ITEM, D)
    steps_all = time_steps.reshape(devices, SLOTS)

    def per_device(acc, pieces):
        x_now, cot_now, steps_now, live_now = pieces
        out_now, pull = jax.vjp(lambda ws, xv: forward(ws, xv, steps_now), params, x_now)
        grads, dx_now = pull(cot_now * live_now[..., None])
        acc = tuple((a + g for a, g in zip(acc, grads)))
        return (acc, (out_now, dx_now))
    zeros = tuple((jnp.zeros_like(p) for p in params))
    grads, (outs, dxs) = lax.scan(per_device, zeros, (x_all, cot_all, steps_all, live))
    total = jnp.float32(0.0)
    for g in grads:
        total = total + jnp.sum(g * g)
    grad_norm = jnp.sqrt(total)
    factor = jnp.minimum(1.0, 1.0 / (grad_norm + 1e-06))
    states = ((ada_weight, ada_first, ada_second, ada_average), (in_weight, in_first, in_second, in_average), (x_weight, x_first, x_second, x_average), (dt_weight, dt_first, dt_second, dt_average), (chan_table, chan_first, chan_second, chan_average), (out_weight, out_first, out_second, out_average))
    settings = ((0.03, 0.1), (0.03, 0.1), (0.03, 0.1), (0.03, 0.1), (0.5, 0.0), (0.03, 0.1))
    results = []
    for (w, m, v, a), g, (learn_rate, weight_decay) in zip(states, grads, settings):
        results.extend(adamw(w, m, v, a, g, factor, learn_rate, weight_decay))
    final = outs.reshape(-1, D)
    act_grad = dxs.reshape(-1, D)
    return (final, act_grad, grad_norm, results[0], results[1], results[2], results[3], results[4], results[5], results[6], results[7], results[8], results[9], results[10], results[11], results[12], results[13], results[14], results[15], results[16], results[17], results[18], results[19], results[20], results[21], results[22], results[23])
```

```python
import math

import jax
import jax.numpy as jnp
from jax import lax
from jax.experimental import pallas as pl
from jax.experimental.pallas import tpu as pltpu
from jax.sharding import PartitionSpec as P

D = 1536
E = 3072
N = 16
R = 96
CONV = 4
ITEM = 256
STEP = 10
SUB = 8
LANE = 128
ALL = ("dp", "fsdp")
LOG2E = math.log2(math.e)
LN2 = math.log(2.0)
F32 = jnp.float32
BF = jnp.bfloat16
VMEM_LIMIT = 40 * 1024 * 1024
SCAN_BLOCK = 64


def softplus(v):
    return jnp.maximum(v, 0.0) + jnp.log1p(jnp.exp(-jnp.abs(v)))


def scan_forward_body(u_ref, dtp_ref, bc_ref, rate_ref, row_ref, y_ref, states_ref, carry, parts):
    groups = u_ref.shape[0] // SUB
    chunks = u_ref.shape[1] // LANE

    @pl.when(pl.program_id(1) == 0)
    def _():
        carry[...] = jnp.zeros_like(carry)

    def group(g, _):
        base = pl.multiple_of(g * SUB, SUB)
        u8 = u_ref[pl.ds(base, SUB), :]
        step8 = softplus(dtp_ref[pl.ds(base, SUB), :] + row_ref[0:1, :])
        drive8 = step8 * u8
        bc = bc_ref[g]
        states = [carry[:, c * LANE : (c + 1) * LANE] for c in range(chunks)]
        for j in range(SUB):
            b = jnp.broadcast_to(bc[:N, j : j + 1], (N, LANE))
            cc = jnp.broadcast_to(bc[N:, j : j + 1], (N, LANE))
            at = pl.multiple_of((base + j) * N, N)
            for c in range(chunks):
                lanes = slice(c * LANE, (c + 1) * LANE)
                step = jnp.broadcast_to(step8[j : j + 1, lanes], (N, LANE))
                drive = jnp.broadcast_to(drive8[j : j + 1, lanes], (N, LANE))
                s = jnp.exp2(step * rate_ref[:, lanes]) * states[c] + b * drive
                states[c] = s
                states_ref[pl.ds(at, N), lanes] = s
                p = cc * s
                parts[c, j * SUB : (j + 1) * SUB, :] = p[:SUB] + p[SUB:]
        for c in range(chunks):
            lanes = slice(c * LANE, (c + 1) * LANE)
            carry[:, lanes] = states[c]
            total = row_ref[1:2, lanes] * u8[:, lanes]
            for n in range(SUB):
                total = total + parts[c, pl.ds(n, SUB, stride=SUB), :]
            y_ref[pl.ds(base, SUB), lanes] = total
        return 0

    lax.fori_loop(0, groups, group, 0)


def scan_forward(u, dtp, bc, rate, rows, item, block=SCAN_BLOCK):
    total, width = u.shape
    items = total // item
    steps = item // block
    chunks = width // LANE
    tok = pl.BlockSpec((block, width), lambda i, t: (i * steps + t, 0))
    whole = lambda r: pl.BlockSpec((r, width), lambda i, t: (0, 0))
    return pl.pallas_call(
        scan_forward_body,
        grid=(items, steps),
        in_specs=[tok, tok, pl.BlockSpec((block // SUB, 2 * N, SUB), lambda i, t: (i * steps + t, 0, 0)), whole(N), whole(2)],
        out_specs=[tok, pl.BlockSpec((block * N, width), lambda i, t: (i * steps + t, 0))],
        out_shape=[jax.ShapeDtypeStruct((total, width), F32), jax.ShapeDtypeStruct((total * N, width), F32)],
        scratch_shapes=[pltpu.VMEM((N, width), F32), pltpu.VMEM((chunks, SUB * SUB, LANE), F32)],
        compiler_params=pltpu.CompilerParams(vmem_limit_bytes=VMEM_LIMIT),
        cost_estimate=pl.CostEstimate(flops=8*total*N*width, bytes_accessed=4*total*width*(N+3), transcendentals=total*N*width),
        name="scan_forward",
    )(u, dtp, bc, rate, rows)


def scan_backward_body(u_ref, dtp_ref, dy_ref, bc_ref, states_ref, before_ref, rate_ref, row_ref,
                       du_ref, ddtp_ref, dbc_ref, drate_ref, drow_ref, carry, parts, parts2, sums):
    groups = u_ref.shape[0] // SUB
    chunks = u_ref.shape[1] // LANE
    first = pl.program_id(1) == pl.num_programs(1) - 1

    @pl.when(pl.program_id(1) == 0)
    def _():
        carry[...] = jnp.zeros_like(carry)

    @pl.when((pl.program_id(0) == 0) & (pl.program_id(1) == 0))
    def _():
        drate_ref[...] = jnp.zeros_like(drate_ref)
        drow_ref[...] = jnp.zeros_like(drow_ref)

    def group(k, _):
        g = groups - 1 - k
        base = pl.multiple_of(g * SUB, SUB)
        u8 = u_ref[pl.ds(base, SUB), :]
        pre8 = dtp_ref[pl.ds(base, SUB), :] + row_ref[0:1, :]
        step8 = softplus(pre8)
        drive8 = step8 * u8
        dy8 = dy_ref[pl.ds(base, SUB), :]
        bc = bc_ref[g]
        grads = [carry[:, c * LANE : (c + 1) * LANE] for c in range(chunks)]
        drate = [drate_ref[:, c * LANE : (c + 1) * LANE] for c in range(chunks)]
        for j in reversed(range(SUB)):
            b = jnp.broadcast_to(bc[:N, j : j + 1], (N, LANE))
            cc = jnp.broadcast_to(bc[N:, j : j + 1], (N, LANE))
            at = pl.multiple_of((base + j) * N, N)
            db = jnp.zeros((N, LANE), F32)
            dc = jnp.zeros((N, LANE), F32)
            for c in range(chunks):
                lanes = slice(c * LANE, (c + 1) * LANE)
                step = jnp.broadcast_to(step8[j : j + 1, lanes], (N, LANE))
                drive = jnp.broadcast_to(drive8[j : j + 1, lanes], (N, LANE))
                dy = jnp.broadcast_to(dy8[j : j + 1, lanes], (N, LANE))
                now = states_ref[pl.ds(at, N), lanes]
                if j > 0:
                    prev = states_ref[pl.ds(at - N, N), lanes]
                else:
                    prev = states_ref[pl.ds(pl.multiple_of(jnp.maximum(at - N, 0), N), N), lanes]
                    edge = jnp.where(first, 0.0, before_ref[:, lanes])
                    prev = jnp.where(g == 0, edge, prev)
                rate = rate_ref[:, lanes]
                grad = cc * dy + grads[c]
                dc = dc + now * dy
                db = db + grad * drive
                p = grad * b
                parts[c, j * SUB : (j + 1) * SUB, :] = p[:SUB] + p[SUB:]
                grad = grad * jnp.exp2(step * rate)
                grads[c] = grad
                q = grad * prev
                p = q * rate
                parts2[c, j * SUB : (j + 1) * SUB, :] = p[:SUB] + p[SUB:]
                drate[c] = drate[c] + q * step
            sums[pl.ds(at, N), :] = db
            sums[pl.ds(pl.multiple_of(groups * SUB * N + at, N), N), :] = dc
        for c in range(chunks):
            lanes = slice(c * LANE, (c + 1) * LANE)
            carry[:, lanes] = grads[c]
            drate_ref[:, lanes] = drate[c]
            x = parts[c, pl.ds(0, SUB, stride=SUB), :]
            r = parts2[c, pl.ds(0, SUB, stride=SUB), :]
            for n in range(1, SUB):
                x = x + parts[c, pl.ds(n, SUB, stride=SUB), :]
                r = r + parts2[c, pl.ds(n, SUB, stride=SUB), :]
            dy = dy8[:, lanes]
            u = u8[:, lanes]
            du_ref[pl.ds(base, SUB), lanes] = step8[:, lanes] * x + row_ref[1:2, lanes] * dy
            ddtp = (u * x + LN2 * r) * jax.nn.sigmoid(pre8[:, lanes])
            ddtp_ref[pl.ds(base, SUB), lanes] = ddtp
            drow_ref[:SUB, lanes] += ddtp
            drow_ref[SUB:, lanes] += dy * u
        return 0

    lax.fori_loop(0, groups, group, 0)
    dbc_ref[...] = lax.dot_general(jnp.ones((SUB, LANE), F32), sums[...], (((1,), (1,)), ((), ())),
                                   precision=lax.Precision.HIGHEST, preferred_element_type=F32)


def scan_backward(u, dtp, dy, bc, states, rate, rows, item, block=SCAN_BLOCK):
    total, width = u.shape
    items = total // item
    steps = item // block
    chunks = width // LANE
    at = lambda i, t: i * steps + steps - 1 - t
    tok = pl.BlockSpec((block, width), lambda i, t: (at(i, t), 0))
    whole = lambda r: pl.BlockSpec((r, width), lambda i, t: (0, 0))
    return pl.pallas_call(
        scan_backward_body,
        grid=(items, steps),
        in_specs=[tok, tok, tok, pl.BlockSpec((block // SUB, 2 * N, SUB), lambda i, t: (at(i, t), 0, 0)),
                  pl.BlockSpec((block * N, width), lambda i, t: (at(i, t), 0)),
                  pl.BlockSpec((N, width), lambda i, t: (jnp.maximum(at(i, t) * block - 1, 0), 0)),
                  whole(N), whole(2)],
        out_specs=[tok, tok, pl.BlockSpec((SUB, 2 * block * N), lambda i, t: (0, at(i, t))), whole(N), whole(2 * SUB)],
        out_shape=[jax.ShapeDtypeStruct((total, width), F32), jax.ShapeDtypeStruct((total, width), F32),
                   jax.ShapeDtypeStruct((SUB, 2 * total * N), F32), jax.ShapeDtypeStruct((N, width), F32), jax.ShapeDtypeStruct((2 * SUB, width), F32)],
        scratch_shapes=[pltpu.VMEM((N, width), F32), pltpu.VMEM((chunks, SUB * SUB, LANE), F32), pltpu.VMEM((chunks, SUB * SUB, LANE), F32),
                        pltpu.VMEM((2 * block * N, LANE), F32)],
        compiler_params=pltpu.CompilerParams(vmem_limit_bytes=VMEM_LIMIT),
        cost_estimate=pl.CostEstimate(flops=16*total*N*width, bytes_accessed=4*total*width*(N+5), transcendentals=total*N*width),
        name="scan_backward",
    )(u, dtp, dy, bc, states, states, rate, rows)


def product(left, right):
    return jnp.dot(left, right, preferred_element_type=F32)


def left_outer(left, right):
    return lax.dot_general(left, right, (((0,), (0,)), ((), ())), preferred_element_type=F32)


def right_inner(left, right):
    return lax.dot_general(left, right, (((1,), (1,)), ((), ())), preferred_element_type=F32)


def embed_time(steps):
    half = D // 2
    freqs = jnp.exp(-math.log(10000.0) * jnp.arange(half, dtype=F32) / half)
    angles = steps.astype(F32)[:, None] * freqs[None, :]
    return jax.nn.silu(jnp.concatenate([jnp.cos(angles), jnp.sin(angles)], axis=1))


def normalize(x):
    mean = jnp.mean(x, axis=2, keepdims=True)
    centered = x - mean
    var = jnp.mean(centered * centered, axis=2, keepdims=True)
    scale = lax.rsqrt(var + 1e-06)
    return centered * scale, scale


def group_bits(size):
    return [1 << k for k in reversed(range(size.bit_length() - 1))]


def swap(v, bit, size):
    return lax.ppermute(v, "fsdp", [(i, i ^ bit) for i in range(size)])


def group_gather(v, size):
    for bit in group_bits(size):
        v = jnp.concatenate([v, swap(v, bit, size)], axis=0)
    return v


def group_scatter(v, size):
    for bit in reversed(group_bits(size)):
        half = v.shape[0] // 2
        v = v[:half] + swap(v[half:].astype(BF), bit, size).astype(F32)
    return v


def group_sum(v, size):
    count = v.shape[0]
    for k, bit in enumerate(group_bits(size)):
        other = swap(v, bit, size)
        span = 1 << k
        other = jnp.flip(other.reshape((count // (2 * span), 2, span) + v.shape[1:]), 1).reshape(v.shape)
        v = v + other
    return v


def exchange(v):
    return lax.all_to_all(v, ALL, 0, 0, tiled=True)


def on_device(sizes, *args):
    (
        act, cotangent, item_counts, item_lengths, time_steps,
        ada_weight, ada_first, ada_second, ada_average,
        in_weight, in_first, in_second, in_average,
        x_weight, x_first, x_second, x_average,
        dt_weight, dt_first, dt_second, dt_average,
        chan_table, chan_first, chan_second, chan_average,
        out_weight, out_first, out_second, out_average,
    ) = args
    n_dp, n_fsdp = sizes
    devices = n_dp * n_fsdp
    count = item_lengths.shape[0]
    items = count * n_fsdp
    tokens = items * ITEM
    width = E // n_fsdp
    ada_cols = ada_weight.shape[1]
    f = lax.axis_index("fsdp")
    d = lax.axis_index("dp")
    offsets = [0]
    for bit in group_bits(n_fsdp):
        offsets = offsets + [o ^ bit for o in offsets]

    rows = jnp.concatenate(
        [out_weight.astype(BF), x_weight.astype(BF), dt_weight.astype(BF).T, chan_table.astype(BF).T], axis=1
    )
    used = rows.shape[1]
    rows = jnp.pad(rows, ((0, 0), (0, -used % LANE)))
    forth = []
    for b in range(devices):
        i, j = divmod(b, 2)
        k, g = divmod(i, n_fsdp)
        forth.append((b, (2 * k + j) * n_fsdp + g))
    in_full = lax.all_gather(in_weight.astype(BF).T, "dp", axis=0, tiled=True)
    rows_full = lax.all_gather(lax.ppermute(rows, ALL, forth), "dp", axis=0, tiled=True)
    out_full = rows_full[:, :D]
    x_full = rows_full[:, D : D + R + 2 * N]
    dt_full = rows_full[:, D + R + 2 * N : D + 2 * R + 2 * N]
    chan = rows_full[:, D + 2 * R + 2 * N : used].astype(F32).T

    live_items = jnp.arange(count, dtype=jnp.int32) < item_counts[0]
    live_rows = jnp.arange(ITEM, dtype=jnp.int32)[None, :] < item_lengths[:, None]
    live = live_items[:, None] & live_rows
    dfinal_own = jnp.where(live[..., None], cotangent.reshape(count, ITEM, D), jnp.zeros((), BF))
    x_all = group_gather(act.reshape(count, ITEM, D), n_fsdp)
    dfinal_all = group_gather(dfinal_own, n_fsdp)

    steps_all = exchange(jnp.broadcast_to(time_steps[None], (devices, count))).reshape(-1)
    cond_all = embed_time(steps_all).astype(BF)
    mod_cols = product(cond_all, ada_weight.astype(BF)).reshape(n_dp, 1, items, ada_cols)
    mod_cols = jnp.broadcast_to(mod_cols, (n_dp, n_fsdp, items, ada_cols)).reshape(devices, items, ada_cols)
    mod = jnp.swapaxes(exchange(mod_cols), 0, 1).reshape(n_fsdp, count, 3 * D)
    mod = jnp.take(mod, jnp.array(offsets, jnp.int32) ^ f, axis=0).reshape(items, 1, 3 * D)
    shift, scale, gate = mod[..., :D], mod[..., D : 2 * D], mod[..., 2 * D :]

    normed, _ = normalize(x_all.astype(F32))
    h_low = (normed * (1.0 + scale) + shift).astype(BF).reshape(tokens, D)
    do_low = (gate * dfinal_all.astype(F32)).astype(BF).reshape(tokens, D)

    xz = right_inner(h_low, in_full)
    xs = xz[:, :width].reshape(items, ITEM, width)
    z = xz[:, width:]
    xs_pad = jnp.pad(xs, ((0, 0), (CONV - 1, 0), (0, 0)))
    pre = chan[CONV]
    for k in range(CONV):
        pre = pre + xs_pad[:, k : k + ITEM, :] * chan[k]
    u = jax.nn.silu(pre).reshape(tokens, width)
    u_low = u.astype(BF)
    proj = group_sum(product(u_low, x_full).reshape(n_fsdp, count * ITEM, R + 2 * N), n_fsdp).reshape(tokens, R + 2 * N)
    rank_low = proj[:, :R].astype(BF)
    dtp = right_inner(rank_low, dt_full)
    a_neg = -jnp.exp(chan[CONV + 3 :])
    rate = a_neg * LOG2E
    pair = chan[CONV + 1 : CONV + 3]
    bc = jnp.swapaxes(proj[:, R:].reshape(tokens // SUB, SUB, 2 * N), 1, 2)
    y, states = scan_forward(u, dtp, bc, rate, pair, ITEM)

    dyg = right_inner(do_low, out_full)
    z_sig = jax.nn.sigmoid(z)
    z_act = z * z_sig
    mixed_low = (y * z_act).astype(BF)
    dy = dyg * z_act
    dz_low = (dyg * y * (z_sig + z_act * (1.0 - z_sig))).astype(BF)
    o_own = group_scatter(product(mixed_low, out_full).reshape(items, ITEM, D), n_fsdp)
    grad_out = left_outer(mixed_low, do_low).astype(BF)

    du_scan, ddtp, dbc, drate, drow = scan_backward(u, dtp, dy, bc, states, rate, pair, ITEM)
    ddtp_low = ddtp.astype(BF)
    dbc = jnp.swapaxes(dbc[0].reshape(-1, 2, SCAN_BLOCK, N), 1, 2).reshape(tokens, 2 * N)
    drank = product(ddtp_low, dt_full)
    dproj = group_sum(jnp.concatenate([drank, dbc], axis=1).reshape(n_fsdp, count * ITEM, R + 2 * N), n_fsdp)
    dproj_low = dproj.reshape(tokens, R + 2 * N).astype(BF)
    grad_dt = left_outer(ddtp_low, rank_low)
    grad_x = left_outer(u_low, dproj_low)
    du = (du_scan + right_inner(dproj_low, x_full)).reshape(items, ITEM, width)
    sig = jax.nn.sigmoid(pre)
    dpre = du * (sig + pre * sig * (1.0 - sig))
    dpre_pad = jnp.pad(dpre, ((0, 0), (0, CONV - 1), (0, 0)))
    dxs = dpre_pad[:, CONV - 1 :] * chan[0]
    for k in range(1, CONV):
        dxs = dxs + dpre_pad[:, CONV - 1 - k : CONV - 1 - k + ITEM] * chan[k]
    grad_taps = [jnp.sum(dpre * xs_pad[:, k : k + ITEM], axis=(0, 1)) for k in range(CONV)]
    grad_bias = jnp.sum(dpre, axis=(0, 1))
    dxz_low = jnp.concatenate([dxs.reshape(tokens, width).astype(BF), dz_low], axis=1)
    grad_in = left_outer(dxz_low, h_low).astype(BF)
    grad_chan = jnp.concatenate(
        [
            jnp.stack(grad_taps + [grad_bias, jnp.sum(drow[:SUB], axis=0), jnp.sum(drow[SUB:], axis=0)]),
            drate * a_neg,
        ],
        axis=0,
    )
    small = jnp.concatenate([grad_x, grad_dt, grad_chan.T], axis=1)
    small = jnp.pad(small, ((0, 0), (0, -small.shape[1] % LANE))).astype(BF)

    back = [(t, s) for s, t in forth]
    out_share = lax.ppermute(lax.psum_scatter(grad_out, "dp", scatter_dimension=0, tiled=True), ALL, back).astype(F32)
    in_share = lax.psum_scatter(grad_in, "dp", scatter_dimension=0, tiled=True).astype(F32).T
    small = lax.ppermute(lax.psum_scatter(small, "dp", scatter_dimension=0, tiled=True), ALL, back).astype(F32)
    x_share = small[:, : R + 2 * N]
    dt_share = small[:, R + 2 * N : 2 * R + 2 * N].T
    chan_share = small[:, 2 * R + 2 * N : 2 * R + 2 * N + chan_table.shape[0]].T

    dh = group_scatter(product(dxz_low, in_full).reshape(items, ITEM, D), n_fsdp)
    x = act.astype(F32).reshape(count, ITEM, D)
    normed, inverse = normalize(x)
    dfinal = dfinal_own.astype(F32)
    final = x + gate[:count] * o_own
    dmod = jnp.concatenate(
        [jnp.sum(dh, axis=1), jnp.sum(dh * normed, axis=1), jnp.sum(dfinal * o_own, axis=1)], axis=1
    ).astype(BF)
    dn = dh * (1.0 + scale[:count])
    act_grad = dfinal + inverse * (
        dn - jnp.mean(dn, axis=2, keepdims=True) - normed * jnp.mean(dn * normed, axis=2, keepdims=True)
    )
    dmod_all = exchange(jnp.swapaxes(dmod.reshape(count, devices, ada_cols), 0, 1)).reshape(devices * count, ada_cols)
    ada_share = left_outer(cond_all, dmod_all)

    shares = (ada_share, in_share, x_share, dt_share, chan_share, out_share)
    local = F32(0.0)
    for g in shares:
        local = local + jnp.sum(g * g)
    total = jnp.sum(exchange(jnp.broadcast_to(local, (devices, LANE)))[:, 0])
    grad_norm = jnp.sqrt(total)
    factor = jnp.minimum(1.0, 1.0 / (grad_norm + 1e-06))
    ema_keep = min(0.9999, (1.0 + STEP) / (10.0 + STEP))
    states = (
        (ada_weight, ada_first, ada_second, ada_average),
        (in_weight, in_first, in_second, in_average),
        (x_weight, x_first, x_second, x_average),
        (dt_weight, dt_first, dt_second, dt_average),
        (chan_table, chan_first, chan_second, chan_average),
        (out_weight, out_first, out_second, out_average),
    )
    settings = ((0.03, 0.1), (0.03, 0.1), (0.03, 0.1), (0.03, 0.1), (0.5, 0.0), (0.03, 0.1))
    results = []
    for (weight, first, second, average), g, (learn_rate, weight_decay) in zip(states, shares, settings):
        clipped = g * factor
        first = 0.9 * first + 0.1 * clipped
        second = 0.999 * second + 0.001 * clipped * clipped
        first_hat = first / (1.0 - 0.9**STEP)
        second_hat = second / (1.0 - 0.999**STEP)
        weight = weight - learn_rate * (
            first_hat / (jnp.sqrt(second_hat) + 1e-08) + weight_decay * weight
        )
        average = ema_keep * average + (1.0 - ema_keep) * weight
        results.extend([first, second, weight, average])
    return (final.reshape(count * ITEM, D), act_grad.reshape(count * ITEM, D), grad_norm, *results)


def solution(mesh):
    sizes = (mesh.shape["dp"], mesh.shape["fsdp"])
    first, second = P(ALL, None), P(None, ALL)
    weights = [second] * 8 + [first] * 4 + [second] * 8 + [first] * 4
    return jax.shard_map(
        lambda *args: on_device(sizes, *args),
        mesh=mesh,
        in_specs=(first, first, P(ALL), P(ALL), P(ALL), *weights),
        out_specs=(first, first, P(), *weights),
        check_vma=False,
    )
```

```python
import math

import jax
import jax.numpy as jnp
from jax import lax
from jax.experimental import pallas as pl
from jax.experimental.pallas import tpu as pltpu
from jax.sharding import PartitionSpec as P

D = 1536
E = 3072
N = 16
R = 96
CONV = 4
CH = 7 + N
ITEM = 256
STEP = 10
SUB = 8
LANE = 128
BIAS, STEP_BIAS, SKIP, RATE = CONV, CONV + 1, CONV + 2, CONV + 3
TABLE = 32
SMALL = 2 * LANE
ALL = ("dp", "fsdp")
LOG2E = math.log2(math.e)
LN2 = math.log(2.0)
F32 = jnp.float32
BF = jnp.bfloat16
VMEM_LIMIT = 60 * 1024 * 1024
SCAN_BLOCK = 64
PITCH = ITEM + SUB


def product(left, right):
    return jnp.dot(left, right, preferred_element_type=F32)


def left_outer(left, right):
    return lax.dot_general(left, right, (((0,), (0,)), ((), ())), preferred_element_type=F32)


def right_inner(left, right):
    return lax.dot_general(left, right, (((1,), (1,)), ((), ())), preferred_element_type=F32)


def softplus(v):
    return jnp.maximum(v, 0.0) + jnp.log1p(jnp.exp(-jnp.abs(v)))


def shape(rows, columns, dtype=F32):
    return jax.ShapeDtypeStruct((rows, columns), dtype)


def item_rows(v):
    return pl.BlockSpec((ITEM, v.shape[1]), lambda i: (i, 0))


def fixed(v):
    return pl.BlockSpec(v.shape, lambda i: (0, 0))


ANYWHERE = pl.BlockSpec(memory_space=pl.ANY)
PARAMS = pltpu.CompilerParams(vmem_limit_bytes=VMEM_LIMIT)


def cost(us):
    return pl.CostEstimate(flops=int(us * 1e9), bytes_accessed=int(us * 1e6), transcendentals=0)


def hold_body(v_ref, *refs):
    pass


def hold(v, *after):
    return pl.pallas_call(
        hold_body,
        in_specs=[ANYWHERE] * (1 + len(after)),
        out_specs=ANYWHERE,
        out_shape=jax.ShapeDtypeStruct(v.shape, v.dtype),
        input_output_aliases={0: 0},
        name="hold",
    )(v, *after)


def joined(blocks):
    return blocks if blocks[0].shape[0] % 16 == 0 else [jnp.concatenate(blocks, axis=0)]


def parted(blocks, count):
    if len(blocks) == count:
        return list(blocks)
    rows = blocks[0].shape[0] // count
    return [blocks[0][q * rows : (q + 1) * rows] for q in range(count)]


def delayed(v, k):
    if k == 0:
        return v
    row = lax.broadcasted_iota(jnp.int32, v.shape, 0)
    moved = pltpu.roll(v, k % v.shape[0], axis=0)
    return jnp.where(row >= k if k > 0 else row < v.shape[0] + k, moved, 0.0)


def convolved(xs, table):
    pre = table[BIAS : BIAS + 1, :]
    for k in range(CONV):
        pre = pre + delayed(xs, CONV - 1 - k) * table[k : k + 1, :]
    return pre


def mix_body(blocks_count, h_ref, *refs):
    blocks = refs[: blocks_count]
    xs_ref, u_ref, low_ref, proj_ref, stream_ref, x_ref, dt_ref, table_ref, tail = refs[-9:]

    @pl.when(pl.program_id(0) == 0)
    def _():
        at = 0
        for block in blocks:
            rows = slice(at, at + block.shape[0])
            stream_ref[rows, :] = block[:, :D]
            x_ref[rows, :] = block[:, D : D + LANE]
            tail[rows, :] = block[:, D + LANE :].astype(F32)
            at += block.shape[0]
        lane = lax.broadcasted_iota(jnp.int32, tail.shape, 1)
        dt_ref[...] = jnp.where(lane < R, tail[...], 0.0).astype(BF)
        table_ref[...] = tail[...].T[R:, :]

    xs = right_inner(h_ref[...], stream_ref[...])
    xs_ref[...] = xs
    pre = convolved(xs, table_ref)
    u = pre * jax.nn.sigmoid(pre)
    u_ref[...] = u
    low = u.astype(BF)
    low_ref[...] = low
    proj_ref[...] = product(low, x_ref[...])


def mix(h, blocks, after):
    tokens = h.shape[0]
    blocks = joined(blocks)
    width = sum(b.shape[0] for b in blocks)
    out_shape = [
        shape(tokens, width), shape(tokens, width), shape(tokens, width, BF), shape(tokens, LANE),
        shape(width, D, BF), shape(width, LANE, BF), shape(width, LANE, BF), shape(TABLE, width),
    ]
    return pl.pallas_call(
        lambda *refs: mix_body(len(blocks), *refs),
        grid=(tokens // ITEM,),
        in_specs=[item_rows(h)] + [fixed(b) for b in blocks] + [ANYWHERE] * len(after),
        out_specs=[item_rows(v) for v in out_shape[:4]] + [fixed(v) for v in out_shape[4:]],
        out_shape=out_shape,
        scratch_shapes=[pltpu.VMEM((width, LANE), F32)],
        compiler_params=PARAMS,
        cost_estimate=cost(6),
        name="mix",
    )(h, *blocks, *after)


def gates_body(count, h_ref, do_ref, y_ref, *refs):
    blocks, grads = refs[:count], refs[count + 4 : 2 * count + 4]
    dy_ref, dz_ref, o_ref, gate_ref = refs[count : count + 4]
    out_w, grad_gate, grad_out = refs[2 * count + 4 :]

    @pl.when(pl.program_id(0) == 0)
    def _():
        at = 0
        for block in blocks:
            rows = slice(at, at + block.shape[0])
            gate_ref[rows, :] = block[:, :D]
            out_w[rows, :] = block[:, D:]
            at += block.shape[0]
        grad_gate[...] = jnp.zeros_like(grad_gate)
        grad_out[...] = jnp.zeros_like(grad_out)

    h, do, y = h_ref[...], do_ref[...], y_ref[...]
    z = right_inner(h, gate_ref[...])
    dyg = right_inner(do, out_w[...])
    sig = jax.nn.sigmoid(z)
    act = z * sig
    dy_ref[...] = dyg * act
    mixed = (y * act).astype(BF)
    dz = (dyg * y * (sig + act * (1.0 - sig))).astype(BF)
    dz_ref[...] = dz
    o_ref[...] = product(mixed, out_w[...]).astype(BF)
    grad_gate[...] += left_outer(dz, h)
    grad_out[...] += left_outer(mixed, do)

    @pl.when(pl.program_id(0) == pl.num_programs(0) - 1)
    def _():
        at = 0
        for grad in grads:
            rows = slice(at, at + grad.shape[0])
            grad[:, :D] = grad_gate[rows, :].astype(BF)
            grad[:, D:] = grad_out[rows, :].astype(BF)
            at += grad.shape[0]


def gates(h, do, y, blocks):
    tokens, width = y.shape
    parts = len(blocks)
    blocks = joined(blocks)
    out_shape = [shape(tokens, width), shape(tokens, width, BF), shape(tokens, D, BF), shape(width, D, BF)]
    grads = [shape(*b.shape, BF) for b in blocks]
    once = lambda v: pl.BlockSpec(v.shape, lambda i: (0, 0), pipeline_mode=pl.Buffered(1))
    dy, dz, o, gate_full, *grads = pl.pallas_call(
        lambda *refs: gates_body(len(blocks), *refs),
        grid=(tokens // ITEM,),
        in_specs=[item_rows(h), item_rows(do), item_rows(y)] + [once(b) for b in blocks],
        out_specs=[item_rows(v) for v in out_shape[:3]] + [fixed(out_shape[3])] + [fixed(v) for v in grads],
        out_shape=out_shape + grads,
        scratch_shapes=[pltpu.VMEM((width, D), BF), pltpu.VMEM((width, D), F32), pltpu.VMEM((width, D), F32)],
        compiler_params=PARAMS,
        cost_estimate=cost(14),
        name="gates",
    )(h, do, y, *blocks)
    return dy, dz, o, gate_full, parted(grads, parts)


def mix_back_body(calls, count, h_ref, xs_ref, du_ref, ddtp_ref, low_ref, proj_ref, dproj_ref, x_ref, table_ref, *refs):
    drates, drows = refs[:calls], refs[calls : 2 * calls]
    dxs_ref, *grads = refs[-5 - count : -4]
    grad_stream, grad_x, grad_tail, rows = refs[-4:]

    @pl.when(pl.program_id(0) == 0)
    def _():
        grad_stream[...] = jnp.zeros_like(grad_stream)
        grad_x[...] = jnp.zeros_like(grad_x)
        grad_tail[...] = jnp.zeros_like(grad_tail)
        rows[...] = jnp.zeros_like(rows)

    dproj = dproj_ref[...].astype(BF)
    xs = xs_ref[...]
    pre = convolved(xs, table_ref)
    sig = jax.nn.sigmoid(pre)
    dpre = (du_ref[...] + right_inner(dproj, x_ref[...])) * (sig + pre * sig * (1.0 - sig))
    dxs = jnp.zeros_like(dpre)
    for k in range(CONV):
        back = CONV - 1 - k
        dxs = dxs + delayed(dpre, -back) * table_ref[k : k + 1, :]
        rows[R + k : R + k + 1, :] += jnp.sum(dpre * delayed(xs, back), axis=0, keepdims=True)
    rows[R + BIAS : R + BIAS + 1, :] += jnp.sum(dpre, axis=0, keepdims=True)
    low = dxs.astype(BF)
    dxs_ref[...] = low
    grad_stream[...] += left_outer(low, h_ref[...])
    grad_x[...] += left_outer(low_ref[...], dproj)
    lane = lax.broadcasted_iota(jnp.int32, dproj.shape, 1)
    rank = jnp.where(lane < R, proj_ref[...], 0.0).astype(BF)
    grad_tail[...] += left_outer(ddtp_ref[...], rank)

    @pl.when(pl.program_id(0) == pl.num_programs(0) - 1)
    def _():
        drow = sum(r[...] for r in drows)
        rows[R + STEP_BIAS : R + STEP_BIAS + 1, :] = jnp.sum(drow[:SUB], axis=0, keepdims=True)
        rows[R + SKIP : R + SKIP + 1, :] = jnp.sum(drow[SUB:], axis=0, keepdims=True)
        rows[R + RATE : R + CH, :] = sum(r[...] for r in drates) * -jnp.exp(table_ref[RATE:CH, :])
        grad_tail[...] += rows[...].T
        at = 0
        for grad in grads:
            part = slice(at, at + grad.shape[0])
            grad[:, :D] = grad_stream[part, :].astype(BF)
            grad[:, D : D + LANE] = grad_x[part, :].astype(BF)
            grad[:, D + LANE :] = grad_tail[part, :].astype(BF)
            at += grad.shape[0]


def mix_back(h, xs, du, ddtp, low, proj, dproj, x_full, table, drates, drows, parts, after):
    tokens, width = xs.shape
    block_rows = width // parts
    blocks = [shape(block_rows, D + SMALL, BF)] * parts if block_rows % 16 == 0 else [shape(width, D + SMALL, BF)]
    dxs_shape = shape(tokens, width, BF)
    calls = len(drates)
    dxs, *grads = pl.pallas_call(
        lambda *refs: mix_back_body(calls, len(blocks), *refs),
        grid=(tokens // ITEM,),
        in_specs=[item_rows(v) for v in (h, xs, du, ddtp, low, proj, dproj)]
        + [fixed(v) for v in (x_full, table, *drates, *drows)]
        + [ANYWHERE] * len(after),
        out_specs=[item_rows(dxs_shape)] + [fixed(v) for v in blocks],
        out_shape=[dxs_shape] + blocks,
        scratch_shapes=[
            pltpu.VMEM((width, D), F32), pltpu.VMEM((width, LANE), F32), pltpu.VMEM((width, LANE), F32),
            pltpu.VMEM((LANE, width), F32),
        ],
        compiler_params=PARAMS,
        cost_estimate=cost(8),
        name="mix_back",
    )(h, xs, du, ddtp, low, proj, dproj, x_full, table, *drates, *drows, *after)
    return dxs, parted(grads, parts)


def scan_prepare(proj_ref, dt_ref, table_ref, pre, rate, bc):
    pre[...] = right_inner(proj_ref[...].astype(BF), dt_ref[...]) + table_ref[STEP_BIAS : STEP_BIAS + 1, :]
    rate[...] = -jnp.exp(table_ref[RATE:CH, :]) * LOG2E
    turned = proj_ref[...].T
    for g in range(bc.shape[0]):
        bc[g, :, :SUB] = turned[R:, g * SUB : (g + 1) * SUB]


def scan_forward_body(u_ref, proj_ref, dt_ref, table_ref, *refs):
    y_ref, states_ref, pre, rate_ref, bc_ref, carry, parts = refs[-7:]
    groups = u_ref.shape[0] // SUB
    chunks = u_ref.shape[1] // LANE

    @pl.when(pl.program_id(1) == 0)
    def _():
        carry[...] = jnp.zeros_like(carry)

    scan_prepare(proj_ref, dt_ref, table_ref, pre, rate_ref, bc_ref)

    def group(g, _):
        base = pl.multiple_of(g * SUB, SUB)
        u8 = u_ref[pl.ds(base, SUB), :]
        step8 = softplus(pre[pl.ds(base, SUB), :])
        drive8 = step8 * u8
        bc = bc_ref[g]
        states = [carry[:, c * LANE : (c + 1) * LANE] for c in range(chunks)]
        for j in range(SUB):
            b = jnp.broadcast_to(bc[:N, j : j + 1], (N, LANE))
            cc = jnp.broadcast_to(bc[N:, j : j + 1], (N, LANE))
            at = pl.multiple_of((base + j) * N, N)
            for c in range(chunks):
                lanes = slice(c * LANE, (c + 1) * LANE)
                step = jnp.broadcast_to(step8[j : j + 1, lanes], (N, LANE))
                drive = jnp.broadcast_to(drive8[j : j + 1, lanes], (N, LANE))
                s = jnp.exp2(step * rate_ref[:, lanes]) * states[c] + b * drive
                states[c] = s
                states_ref[pl.ds(at, N), lanes] = s
                p = cc * s
                parts[c, j * SUB : (j + 1) * SUB, :] = p[:SUB] + p[SUB:]
        for c in range(chunks):
            lanes = slice(c * LANE, (c + 1) * LANE)
            carry[:, lanes] = states[c]
            total = table_ref[SKIP : SKIP + 1, lanes] * u8[:, lanes]
            for n in range(SUB):
                total = total + parts[c, pl.ds(n, SUB, stride=SUB), :]
            y_ref[pl.ds(base, SUB), lanes] = total
        return 0

    lax.fori_loop(0, groups, group, 0)


def scan_forward(begin, count, u, proj, dt, table, kept, after):
    total, width = u.shape
    block = SCAN_BLOCK
    steps = ITEM // block
    chunks = width // LANE
    at = lambda i, t: ((begin + i) * steps + t, 0)
    tok = pl.BlockSpec((block, width), at)
    whole = lambda v: pl.BlockSpec(v.shape, lambda i, t: (0, 0))
    extra = list(kept) + list(after)
    return pl.pallas_call(
        scan_forward_body,
        grid=(count, steps),
        in_specs=[tok, pl.BlockSpec((block, LANE), at), whole(dt), whole(table)] + [ANYWHERE] * len(extra),
        out_specs=[tok, pl.BlockSpec((block * N, width), at)],
        out_shape=[shape(total, width), shape(total * N, width)],
        scratch_shapes=[
            pltpu.VMEM((block, width), F32), pltpu.VMEM((N, width), F32), pltpu.VMEM((block // SUB, 2 * N, LANE), F32),
            pltpu.VMEM((N, width), F32), pltpu.VMEM((chunks, SUB * SUB, LANE), F32),
        ],
        input_output_aliases={4 + k: k for k in range(len(kept))},
        compiler_params=PARAMS,
        cost_estimate=cost(8 * count),
        name="scan_forward",
    )(u, proj, dt, table, *extra)


def scan_backward_body(u_ref, proj_ref, dy_ref, states_ref, before_ref, dt_ref, table_ref, *refs):
    du_ref, ddtp_ref, dproj_ref, drate_ref, drow_ref = refs[-15:-10]
    pre, rate_ref, bc_ref, ddtp, carry, parts, parts2, sums, stage, own = refs[-10:]
    block = u_ref.shape[0]
    groups = block // SUB
    chunks = u_ref.shape[1] // LANE
    back = pl.num_programs(1) - 1 - pl.program_id(1)
    first = back == 0

    @pl.when(pl.program_id(1) == 0)
    def _():
        carry[...] = jnp.zeros_like(carry)

    @pl.when((pl.program_id(0) == 0) & (pl.program_id(1) == 0))
    def _():
        drate_ref[...] = jnp.zeros_like(drate_ref)
        drow_ref[...] = jnp.zeros_like(drow_ref)

    scan_prepare(proj_ref, dt_ref, table_ref, pre, rate_ref, bc_ref)

    def group(k, _):
        g = groups - 1 - k
        base = pl.multiple_of(g * SUB, SUB)
        u8 = u_ref[pl.ds(base, SUB), :]
        pre8 = pre[pl.ds(base, SUB), :]
        step8 = softplus(pre8)
        drive8 = step8 * u8
        dy8 = dy_ref[pl.ds(base, SUB), :]
        bc = bc_ref[g]
        grads = [carry[:, c * LANE : (c + 1) * LANE] for c in range(chunks)]
        drate = [drate_ref[:, c * LANE : (c + 1) * LANE] for c in range(chunks)]
        for j in reversed(range(SUB)):
            b = jnp.broadcast_to(bc[:N, j : j + 1], (N, LANE))
            cc = jnp.broadcast_to(bc[N:, j : j + 1], (N, LANE))
            at = pl.multiple_of((base + j) * N, N)
            db = jnp.zeros((N, LANE), F32)
            dc = jnp.zeros((N, LANE), F32)
            for c in range(chunks):
                lanes = slice(c * LANE, (c + 1) * LANE)
                step = jnp.broadcast_to(step8[j : j + 1, lanes], (N, LANE))
                drive = jnp.broadcast_to(drive8[j : j + 1, lanes], (N, LANE))
                dy = jnp.broadcast_to(dy8[j : j + 1, lanes], (N, LANE))
                now = states_ref[pl.ds(at, N), lanes]
                if j > 0:
                    prev = states_ref[pl.ds(at - N, N), lanes]
                else:
                    prev = states_ref[pl.ds(pl.multiple_of(jnp.maximum(at - N, 0), N), N), lanes]
                    edge = jnp.where(first, 0.0, before_ref[:, lanes])
                    prev = jnp.where(g == 0, edge, prev)
                rate = rate_ref[:, lanes]
                grad = cc * dy + grads[c]
                dc = dc + now * dy
                db = db + grad * drive
                p = grad * b
                parts[c, j * SUB : (j + 1) * SUB, :] = p[:SUB] + p[SUB:]
                grad = grad * jnp.exp2(step * rate)
                grads[c] = grad
                q = grad * prev
                p = q * rate
                parts2[c, j * SUB : (j + 1) * SUB, :] = p[:SUB] + p[SUB:]
                drate[c] = drate[c] + q * step
            token = back * block + base + j
            sums[pl.ds(token, N, stride=PITCH), :] = db
            sums[pl.ds(N * PITCH + token, N, stride=PITCH), :] = dc
        for c in range(chunks):
            lanes = slice(c * LANE, (c + 1) * LANE)
            carry[:, lanes] = grads[c]
            drate_ref[:, lanes] = drate[c]
            x = parts[c, pl.ds(0, SUB, stride=SUB), :]
            r = parts2[c, pl.ds(0, SUB, stride=SUB), :]
            for n in range(1, SUB):
                x = x + parts[c, pl.ds(n, SUB, stride=SUB), :]
                r = r + parts2[c, pl.ds(n, SUB, stride=SUB), :]
            dy = dy8[:, lanes]
            u = u8[:, lanes]
            du_ref[pl.ds(base, SUB), lanes] = step8[:, lanes] * x + table_ref[SKIP : SKIP + 1, lanes] * dy
            d = (u * x + LN2 * r) * jax.nn.sigmoid(pre8[:, lanes])
            ddtp[pl.ds(base, SUB), lanes] = d
            drow_ref[:SUB, lanes] += d
            drow_ref[SUB:, lanes] += dy * u
        return 0

    lax.fori_loop(0, groups, group, 0)
    low = ddtp[...].astype(BF)
    ddtp_ref[...] = low
    own[pl.ds(pl.multiple_of(back * block, block), block), :] = product(low, dt_ref[...])

    @pl.when(first)
    def _():
        stage[...] = jnp.zeros_like(stage)
        ones = jnp.ones((SUB, LANE), BF)
        for n in range(2 * N):
            wide = sums[n * PITCH : n * PITCH + ITEM, :]
            high = wide.astype(BF)
            row = right_inner(ones, high) + right_inner(ones, (wide - high.astype(F32)).astype(BF))
            stage[R + n : R + n + 1, :] = row[:1]
        dproj_ref[...] = own[...] + stage[...].T


def scan_backward(begin, count, u, proj, dy, states, dt, table, kept, after):
    total, width = u.shape
    block = SCAN_BLOCK
    steps = ITEM // block
    chunks = width // LANE
    place = lambda i, t: (begin + i) * steps + steps - 1 - t
    at = lambda i, t: (place(i, t), 0)
    tok = pl.BlockSpec((block, width), at)
    whole = lambda v: pl.BlockSpec(v.shape, lambda i, t: (0, 0))
    extra = list(kept) + list(after)
    out_shape = [
        shape(total, width), shape(total, width, BF), shape(total, LANE), shape(N, width), shape(2 * SUB, width)
    ]
    return pl.pallas_call(
        scan_backward_body,
        grid=(count, steps),
        in_specs=[
            tok, pl.BlockSpec((block, LANE), at), tok,
            pl.BlockSpec((block * N, width), at),
            pl.BlockSpec((N, width), lambda i, t: (jnp.maximum(place(i, t) * block - 1, 0), 0)),
            whole(dt), whole(table),
        ]
        + [ANYWHERE] * len(extra),
        out_specs=[tok, tok, pl.BlockSpec((ITEM, LANE), lambda i, t: (begin + i, 0)), whole(out_shape[3]), whole(out_shape[4])],
        out_shape=out_shape,
        scratch_shapes=[
            pltpu.VMEM((block, width), F32), pltpu.VMEM((N, width), F32), pltpu.VMEM((block // SUB, 2 * N, LANE), F32),
            pltpu.VMEM((block, width), F32), pltpu.VMEM((N, width), F32),
            pltpu.VMEM((chunks, SUB * SUB, LANE), F32), pltpu.VMEM((chunks, SUB * SUB, LANE), F32),
            pltpu.VMEM((2 * N * PITCH, LANE), F32), pltpu.VMEM((LANE, ITEM), F32), pltpu.VMEM((ITEM, LANE), F32),
        ],
        input_output_aliases={7 + k: k for k in range(len(kept))},
        compiler_params=PARAMS,
        cost_estimate=cost(15 * count),
        name="scan_backward",
    )(u, proj, dy, states, states, dt, table, *extra)


def update_body(factor_ref, *refs):
    grads, states, outs = refs[:5], refs[5:29], refs[29:]
    factor = factor_ref[0, 0]
    ema_keep = min(0.9999, (1.0 + STEP) / (10.0 + STEP))

    def update(k, g):
        learn_rate, weight_decay = (0.5, 0.0) if k == 4 else (0.03, 0.1)
        weight, first, second, average = (states[4 * k + q][...] for q in range(4))
        clipped = g * factor
        first = 0.9 * first + 0.1 * clipped
        second = 0.999 * second + 0.001 * clipped * clipped
        first_hat = first / (1.0 - 0.9**STEP)
        second_hat = second / (1.0 - 0.999**STEP)
        weight = weight - learn_rate * (first_hat / (jnp.sqrt(second_hat) + 1e-08) + weight_decay * weight)
        average = ema_keep * average + (1.0 - ema_keep) * weight
        for q, v in enumerate((first, second, weight, average)):
            outs[4 * k + q][...] = v

    ada, wide, small, small_t, out = grads
    update(0, ada[...])
    update(1, wide[...])
    update(5, out[...])

    @pl.when(pl.program_id(0) == 0)
    def _():
        update(2, small[...])
        update(3, small_t[:R, :])
        update(4, small_t[R:CH + R, :])


def update_all(factor, ada, wide, small, small_t, out, states):
    part = 256
    right = lambda v: pl.BlockSpec((v.shape[0], part), lambda t: (0, t))
    kinds = [right, right, fixed, fixed, fixed, right]
    specs = [kind(v) for kind, group in zip(kinds, states) for v in group]
    flat = [v for group in states for v in group]
    return pl.pallas_call(
        update_body,
        grid=(D // part,),
        in_specs=[pl.BlockSpec(memory_space=pltpu.SMEM), right(ada), right(wide), fixed(small), fixed(small_t), right(out)]
        + specs,
        out_specs=specs,
        out_shape=[shape(*v.shape) for v in flat],
        compiler_params=PARAMS,
        cost_estimate=cost(11),
        name="update",
    )(factor.reshape(1, 1), ada, wide, small, small_t, out, *flat)


def embed_time(steps):
    half = D // 2
    freqs = jnp.exp(-math.log(10000.0) * jnp.arange(half, dtype=F32) / half)
    angles = steps.astype(F32)[:, None] * freqs[None, :]
    return jax.nn.silu(jnp.concatenate([jnp.cos(angles), jnp.sin(angles)], axis=1))


def normalize(x):
    mean = jnp.mean(x, axis=2, keepdims=True)
    centered = x - mean
    var = jnp.mean(centered * centered, axis=2, keepdims=True)
    scale = lax.rsqrt(var + 1e-06)
    return centered * scale, scale


def group_bits(size):
    return [1 << k for k in reversed(range(size.bit_length() - 1))]


def swap(v, bit, size):
    return lax.ppermute(v, "fsdp", [(i, i ^ bit) for i in range(size)])


def group_gather(v, size):
    for bit in group_bits(size):
        v = jnp.concatenate([v, swap(v, bit, size)], axis=0)
    return v


def group_scatter_steps(v, size, gate):
    for bit in reversed(group_bits(size)):
        half = v.shape[0] // 2
        away = v[half:].astype(BF)
        if gate:
            away = hold(away, *gate)
        v = v[:half].astype(F32) + swap(away, bit, size).astype(F32)
        yield v


def group_sum(v, size):
    bits = group_bits(size)
    half = v.shape[0] // 2
    total = v[:half] + swap(v[half:], bits[-1], size)
    for k, bit in enumerate(bits[:-1]):
        other = swap(total, bit, size)
        rows = other.shape[0] // (size // 2)
        total = total + jnp.concatenate(
            [other[(p ^ (1 << k)) * rows : ((p ^ (1 << k)) + 1) * rows] for p in range(size // 2)], axis=0
        )
    return jnp.concatenate([total, swap(total, bits[-1], size)], axis=0)


def ring_order(size):
    if size == 8:
        return [0, 2, 4, 6, 7, 5, 3, 1]
    return list(range(size))


def ring_move(v, way, size):
    order = ring_order(size)
    return lax.ppermute(v, "dp", [(order[p], order[(p + way) % size]) for p in range(size)])


def ring_gather_steps(v, size, gate):
    behind = ahead = v
    for _ in range(size // 2 - 1):
        if gate:
            behind, ahead = hold(behind, *gate), hold(ahead, *gate)
        behind, ahead = ring_move(behind, 1, size), ring_move(ahead, -1, size)
        yield [behind, ahead]
    cut = v.shape[0] // 2
    if gate:
        behind, ahead = hold(behind, *gate), hold(ahead, *gate)
    yield [jnp.concatenate([ring_move(behind[:cut], 1, size), ring_move(ahead[cut:], -1, size)], axis=0)]


def ring_scatter_steps(blocks, size, gate):
    cut = blocks[0].shape[0] // 2
    add = lambda a, b: (a.astype(F32) + b.astype(F32)).astype(BF)
    up, down = ring_move(blocks[-1][:cut], 1, size), ring_move(blocks[-1][cut:], -1, size)
    yield [up, down]
    for s in range(size // 2 - 1, 0, -1):
        ahead, behind = blocks[2 * s], blocks[2 * s - 1]
        if s == size // 2 - 1:
            ahead = jnp.concatenate([add(ahead[:cut], up), ahead[cut:]], axis=0)
            behind = jnp.concatenate([behind[:cut], add(behind[cut:], down)], axis=0)
        else:
            ahead, behind = add(ahead, up), add(behind, down)
        if gate:
            ahead, behind = hold(ahead, *gate), hold(behind, *gate)
        up, down = ring_move(ahead, 1, size), ring_move(behind, -1, size)
        yield [up, down]
    yield blocks[0].astype(F32) + up.astype(F32) + down.astype(F32)


def exchange(v):
    return lax.all_to_all(v, ALL, 0, 0, tiled=True)


def on_device(sizes, *args):
    (
        act, cotangent, item_counts, item_lengths, time_steps,
        ada_weight, ada_first, ada_second, ada_average,
        in_weight, in_first, in_second, in_average,
        x_weight, x_first, x_second, x_average,
        dt_weight, dt_first, dt_second, dt_average,
        chan_table, chan_first, chan_second, chan_average,
        out_weight, out_first, out_second, out_average,
    ) = args
    n_dp, n_fsdp = sizes
    devices = n_dp * n_fsdp
    count = item_lengths.shape[0]
    items = count * n_fsdp
    tokens = items * ITEM
    ada_cols = ada_weight.shape[1]
    f = lax.axis_index("fsdp")
    half = n_dp // 2
    low_half = lax.axis_index("dp") < half
    offsets = [0]
    for bit in group_bits(n_fsdp):
        offsets = offsets + [o ^ bit for o in offsets]

    forth = []
    for b in range(devices):
        i, j = divmod(b, 2)
        k, g = divmod(i, n_fsdp)
        forth.append((b, (k + half * j) * n_fsdp + g))
    back = [(t, s) for s, t in forth]
    across = [(q, (q + half) % n_dp) for q in range(n_dp)]
    wide = in_weight.astype(BF).T
    rows = wide.shape[0] // 2
    leaving = jnp.where(low_half, wide[rows:], wide[:rows])
    swapped = lax.ppermute(leaving, "dp", across)
    small = jnp.concatenate([x_weight.astype(BF), dt_weight.astype(BF).T, chan_table.astype(BF).T], axis=1)
    small = jnp.pad(small, ((0, 0), (0, SMALL - small.shape[1])))
    small = lax.ppermute(hold(small, leaving), ALL, forth)
    stream_own = jnp.concatenate([jnp.where(low_half, wide[:rows], swapped), small], axis=1)
    gate_own = jnp.where(low_half, swapped, wide[rows:])

    live_items = jnp.arange(count, dtype=jnp.int32) < item_counts[0]
    live_rows = jnp.arange(ITEM, dtype=jnp.int32)[None, :] < item_lengths[:, None]
    live = live_items[:, None] & live_rows
    dfinal_own = jnp.where(live[..., None], cotangent.reshape(count, ITEM, D), jnp.zeros((), BF))
    x_all = group_gather(act.reshape(count, ITEM, D), n_fsdp)
    dfinal_all = group_gather(hold(dfinal_own, x_all), n_fsdp)

    steps_all = exchange(hold(jnp.broadcast_to(time_steps[None], (devices, count)), leaving)).reshape(-1)
    cond_all = embed_time(steps_all).astype(BF)
    mod_cols = product(cond_all, ada_weight.astype(BF)).reshape(n_dp, 1, items, ada_cols)
    mod_cols = jnp.broadcast_to(mod_cols, (n_dp, n_fsdp, items, ada_cols)).reshape(devices, items, ada_cols)
    mod = jnp.swapaxes(exchange(hold(mod_cols, stream_own)), 0, 1).reshape(n_fsdp, count, 3 * D)
    mod = jnp.take(mod, jnp.array(offsets, jnp.int32) ^ f, axis=0).reshape(items, 1, 3 * D)
    shift, scale, gate = mod[..., :D], mod[..., D : 2 * D], mod[..., 2 * D :]

    normed, _ = normalize(x_all.astype(F32))
    h_low = (normed * (1.0 + scale) + shift).astype(BF).reshape(tokens, D)
    do_low = (gate * dfinal_all.astype(F32)).astype(BF).reshape(tokens, D)

    stream, gate_ring = [stream_own], []
    steps = ring_gather_steps(stream_own, n_dp, gate_ring)
    for s in range(half):
        stream += next(steps)
        if s == half - 3:
            gate_ring[:] = [x_all]
        if s == half - 2:
            gate_ring[:] = [h_low]
    out_own = lax.ppermute(hold(out_weight.astype(BF), stream[half - 1]), ALL, forth)
    rest_own = hold(jnp.concatenate([gate_own, out_own], axis=1), stream[-1])
    rest_steps = list(ring_gather_steps(rest_own, n_dp, []))
    rest = [rest_own] + sum(rest_steps, [])

    xs, u, u_low, proj, stream_full, x_full, dt_full, table = mix(h_low, stream, [rest_own])
    proj = group_sum(proj, n_fsdp)
    calls = 2
    part = items // calls
    kept = []
    for i in range(calls):
        kept = scan_forward(i * part, part, u, proj, dt_full, table, kept, rest_steps[half // 2 - 1 + i])
    y, states = kept

    dy, dz_low, o_part, gate_full, early = gates(h_low, do_low, y, rest)
    gate_early = []
    early_steps = ring_scatter_steps(early, n_dp, gate_early)
    o_steps = group_scatter_steps(o_part.reshape(items, ITEM, D), n_fsdp, gate_early)
    came = next(early_steps)
    o_own = next(o_steps)
    kept, drates, drows = [], [], []
    after = list(early)
    for i in range(calls):
        *kept, drate, drow = scan_backward(i * part, part, u, proj, dy, states, dt_full, table, kept, after)
        drates.append(drate)
        drows.append(drow)
        after = list(came)
        gate_early[:] = [drate]
        came = next(early_steps)
        o_own = next(o_steps, o_own)
    for o_own in o_steps:
        pass
    for early_sum in early_steps:
        pass
    du_scan, ddtp_low, dproj = kept

    dproj = group_sum(dproj, n_fsdp)
    dxs_low, late = mix_back(h_low, xs, du_scan, ddtp_low, u_low, proj, dproj, x_full, table, drates, drows, n_dp, [o_own])
    dh = (product(dxs_low, stream_full) + product(dz_low, gate_full)).reshape(items, ITEM, D)
    dh_steps = group_scatter_steps(dh, n_fsdp, [])
    gate_late = []
    late_steps = ring_scatter_steps(late, n_dp, gate_late)
    next(late_steps)
    dh = next(dh_steps)
    next(late_steps)
    gate_late[:] = [dh]
    for dh in dh_steps:
        pass
    for late_sum in late_steps:
        pass

    small = lax.ppermute(late_sum[:, D:].astype(BF), ALL, back).astype(F32)
    small_t = small[:, LANE:].T
    out_share = lax.ppermute(early_sum[:, D:].astype(BF), ALL, back).astype(F32)
    gate_sum = early_sum[:, :D].astype(BF)
    late_sum = hold(late_sum[:, :D].astype(BF), dh)
    gate_moved = lax.ppermute(gate_sum, "dp", [(q, q + half) for q in range(half)])
    late_moved = lax.ppermute(late_sum, "dp", [(q + half, q) for q in range(half)])
    in_share = jnp.concatenate(
        [jnp.where(low_half, late_sum, gate_moved), jnp.where(low_half, late_moved, gate_sum)], axis=0
    )
    in_share = in_share.astype(F32)

    x = act.astype(F32).reshape(count, ITEM, D)
    normed, inverse = normalize(x)
    dfinal = dfinal_own.astype(F32)
    final = x + gate[:count] * o_own
    dmod = jnp.concatenate(
        [jnp.sum(dh, axis=1), jnp.sum(dh * normed, axis=1), jnp.sum(dfinal * o_own, axis=1)], axis=1
    ).astype(BF)
    dn = dh * (1.0 + scale[:count])
    act_grad = dfinal + inverse * (
        dn - jnp.mean(dn, axis=2, keepdims=True) - normed * jnp.mean(dn * normed, axis=2, keepdims=True)
    )
    dmod_all = exchange(jnp.swapaxes(dmod.reshape(count, devices, ada_cols), 0, 1)).reshape(devices * count, ada_cols)
    ada_share = left_outer(dmod_all, cond_all)

    shares = (ada_share, in_share, small, out_share)
    local = F32(0.0)
    for g in shares:
        local = local + jnp.sum(g * g)
    total = jnp.sum(exchange(jnp.broadcast_to(local, (devices, LANE)))[:, 0])
    grad_norm = jnp.sqrt(total)
    factor = jnp.minimum(1.0, 1.0 / (grad_norm + 1e-06))
    results = update_all(
        factor, ada_share, in_share, small[:, :LANE], small_t, out_share,
        (
            (ada_weight.T, ada_first.T, ada_second.T, ada_average.T),
            (in_weight.T, in_first.T, in_second.T, in_average.T),
            (x_weight, x_first, x_second, x_average),
            (dt_weight, dt_first, dt_second, dt_average),
            (chan_table, chan_first, chan_second, chan_average),
            (out_weight, out_first, out_second, out_average),
        ),
    )
    results = [v.T for v in results[:8]] + list(results[8:])
    return (final.reshape(count * ITEM, D), act_grad.reshape(count * ITEM, D), grad_norm, *results)


def solution(mesh):
    sizes = (mesh.shape["dp"], mesh.shape["fsdp"])
    first, second = P(ALL, None), P(None, ALL)
    weights = [second] * 8 + [first] * 4 + [second] * 8 + [first] * 4
    return jax.shard_map(
        lambda *args: on_device(sizes, *args),
        mesh=mesh,
        in_specs=(first, first, P(ALL), P(ALL), P(ALL), *weights),
        out_specs=(first, first, P(), *weights),
        check_vma=False,
    )
```

```python
import math

import jax
import jax.numpy as jnp
from jax import lax
from jax.experimental import pallas as pl
from jax.experimental.layout import Layout, with_layout_constraint
from jax.experimental.pallas import tpu as pltpu
from jax.sharding import PartitionSpec as P

D = 1536
E = 3072
N = 16
R = 96
CONV = 4
CH = 7 + N
ITEM = 256
STEP = 10
SUB = 8
LANE = 128
BIAS, STEP_BIAS, SKIP, RATE = CONV, CONV + 1, CONV + 2, CONV + 3
TABLE = 32
SMALL = 2 * LANE
ALL = ("dp", "fsdp")
LOG2E = math.log2(math.e)
LN2 = math.log(2.0)
F32 = jnp.float32
BF = jnp.bfloat16
VMEM_LIMIT = 60 * 1024 * 1024
SCAN_BLOCK = 64
PITCH = ITEM + SUB


def product(left, right):
    return jnp.dot(left, right, preferred_element_type=F32)


def left_outer(left, right):
    return lax.dot_general(left, right, (((0,), (0,)), ((), ())), preferred_element_type=F32)


def right_inner(left, right):
    return lax.dot_general(left, right, (((1,), (1,)), ((), ())), preferred_element_type=F32)


def softplus(v):
    return jnp.maximum(v, 0.0) + jnp.log1p(jnp.exp(-jnp.abs(v)))


def shape(rows, columns, dtype=F32):
    return jax.ShapeDtypeStruct((rows, columns), dtype)


def item_rows(v):
    return pl.BlockSpec((ITEM, v.shape[1]), lambda i: (i, 0))


def halves(tokens):
    last = tokens // ITEM // 2 - 1
    near = pl.BlockSpec((ITEM, D), lambda i: (jnp.minimum(i, last), 0))
    return near, pl.BlockSpec((ITEM, D), lambda i: (jnp.maximum(i - last - 1, 0), 0))


def fixed(v):
    return pl.BlockSpec(v.shape, lambda i: (0, 0))


def once(v):
    return pl.BlockSpec(v.shape, lambda i: (0, 0), pipeline_mode=pl.Buffered(1))


ANYWHERE = pl.BlockSpec(memory_space=pl.ANY)
PARAMS = pltpu.CompilerParams(vmem_limit_bytes=VMEM_LIMIT)


def cost(us):
    return pl.CostEstimate(flops=int(us * 1e9), bytes_accessed=int(us * 1e6), transcendentals=0)


def hold_body(v_ref, *refs):
    pass


def hold(v, *after):
    return pl.pallas_call(
        hold_body,
        in_specs=[ANYWHERE] * (1 + len(after)),
        out_specs=ANYWHERE,
        out_shape=jax.ShapeDtypeStruct(v.shape, v.dtype),
        input_output_aliases={0: 0},
        name="hold",
    )(v, *after)


def ring_sizes(rows, size):
    return [rows] * (size - 1) + [rows // 2] * 2


def joined(blocks):
    return blocks if all(b.shape[0] % 16 == 0 for b in blocks) else [jnp.concatenate(blocks, axis=0)]


def parted(blocks, sizes):
    if len(blocks) == len(sizes):
        return list(blocks)
    ends = [sum(sizes[: k + 1]) for k in range(len(sizes))]
    return [blocks[0][end - size : end] for end, size in zip(ends, sizes)]


def pick(refs, item, held):
    for p, ref in enumerate(refs):
        @pl.when(item == p)
        def _(ref=ref):
            held[...] = ref[...]


def fold_body(near_ref, came_ref, *refs):
    keep_ref, away_ref = refs[-2:]
    half = keep_ref.shape[0]
    keep_ref[...] = near_ref[:half, :].astype(F32) + came_ref[:half, :].astype(F32)
    away_ref[...] = (near_ref[half:, :].astype(F32) + came_ref[half:, :].astype(F32)).astype(BF)


def fold(near, came, after):
    half = near.shape[0] // 2
    whole = pl.BlockSpec(memory_space=pltpu.VMEM)
    return pl.pallas_call(
        fold_body,
        in_specs=[whole, whole] + [ANYWHERE] * len(after),
        out_specs=[whole, whole],
        out_shape=[shape(half, near.shape[1]), shape(half, near.shape[1], BF)],
        compiler_params=PARAMS,
        cost_estimate=cost(2),
        name="fold",
    )(near, came, *after)


def ring_add_body(ahead_ref, behind_ref, up_ref, down_ref, *refs):
    up, down = up_ref.shape[0], down_ref.shape[0]
    rows = ahead_ref.shape[0]
    to_ahead, to_behind = refs[-2:]
    to_ahead[:up, :] = (ahead_ref[:up, :].astype(F32) + up_ref[...].astype(F32)).astype(BF)
    to_behind[rows - down :, :] = (behind_ref[rows - down :, :].astype(F32) + down_ref[...].astype(F32)).astype(BF)
    if up < rows:
        to_ahead[up:, :] = ahead_ref[up:, :]
        to_behind[: rows - down, :] = behind_ref[: rows - down, :]


def ring_add(ahead, behind, up, down, after):
    whole = pl.BlockSpec(memory_space=pltpu.VMEM)
    return pl.pallas_call(
        ring_add_body,
        in_specs=[whole] * 4 + [ANYWHERE] * len(after),
        out_specs=[whole, whole],
        out_shape=[shape(*ahead.shape, BF)] * 2,
        compiler_params=PARAMS,
        cost_estimate=cost(2),
        name="ring_add",
    )(ahead, behind, up, down, *after)


def delayed(v, k):
    if k == 0:
        return v
    row = lax.broadcasted_iota(jnp.int32, v.shape, 0)
    moved = pltpu.roll(v, k % v.shape[0], axis=0)
    return jnp.where(row >= k if k > 0 else row < v.shape[0] + k, moved, 0.0)


def convolved(xs, table):
    pre = table[BIAS : BIAS + 1, :]
    for k in range(CONV):
        pre = pre + delayed(xs, CONV - 1 - k) * table[k : k + 1, :]
    return pre


def mix_body(items, count, mod_ref, *refs):
    pieces, blocks = refs[:items], refs[items : items + count]
    h_ref, xs_ref, u_ref, low_ref, proj_ref, stream_ref, x_ref, dt_ref, table_ref, tail, held = refs[-11:]

    @pl.when(pl.program_id(0) == 0)
    def _():
        at = 0
        for block in blocks:
            rows = slice(at, at + block.shape[0])
            stream_ref[rows, :] = block[:, :D]
            x_ref[rows, :] = block[:, D : D + LANE]
            tail[rows, :] = block[:, D + LANE :].astype(F32)
            at += block.shape[0]
        lane = lax.broadcasted_iota(jnp.int32, tail.shape, 1)
        dt_ref[...] = jnp.where(lane < R, tail[...], 0.0).astype(BF)
        table_ref[...] = tail[...].T[R:, :]

    pick(pieces, pl.program_id(0), held)
    x = held[...].astype(F32)
    centered = x - jnp.mean(x, axis=1, keepdims=True)
    normed = centered * lax.rsqrt(jnp.mean(centered * centered, axis=1, keepdims=True) + 1e-06)
    mod = mod_ref[pl.ds(pl.program_id(0), 1), :]
    h = (normed * (1.0 + mod[:, D : 2 * D]) + mod[:, :D]).astype(BF)
    h_ref[...] = h
    xs = right_inner(h, stream_ref[...])
    xs_ref[...] = xs
    pre = convolved(xs, table_ref)
    u = pre * jax.nn.sigmoid(pre)
    u_ref[...] = u
    low = u.astype(BF)
    low_ref[...] = low
    proj_ref[...] = product(low, x_ref[...])


def mix(pieces, mod, blocks, after):
    items = len(pieces)
    tokens = items * ITEM
    blocks = joined(blocks)
    width = sum(b.shape[0] for b in blocks)
    out_shape = [
        shape(tokens, D, BF), shape(tokens, width), shape(tokens, width), shape(tokens, width, BF), shape(tokens, LANE),
        shape(width, D, BF), shape(width, LANE, BF), shape(width, LANE, BF), shape(TABLE, width),
    ]
    return pl.pallas_call(
        lambda *refs: mix_body(items, len(blocks), *refs),
        grid=(items,),
        in_specs=[fixed(mod)] + [once(v) for v in (*pieces, *blocks)] + [ANYWHERE] * len(after),
        out_specs=[item_rows(v) for v in out_shape[:5]] + [fixed(v) for v in out_shape[5:]],
        out_shape=out_shape,
        scratch_shapes=[pltpu.VMEM((width, LANE), F32), pltpu.VMEM((ITEM, D), BF)],
        compiler_params=PARAMS,
        cost_estimate=cost(11),
        name="mix",
    )(mod, *pieces, *blocks, *after)


def gates_body(items, count, h_ref, mod_ref, y_ref, *refs):
    pieces, blocks = refs[:items], refs[items : items + count]
    dy_ref, dz_ref, near_ref, far_ref, gate_ref, *grads = refs[items + count : -4]
    out_w, grad_gate, grad_out, held = refs[-4:]
    item = pl.program_id(0)

    @pl.when(pl.program_id(0) == 0)
    def _():
        at = 0
        for block in blocks:
            rows = slice(at, at + block.shape[0])
            gate_ref[rows, :] = block[:, :D]
            out_w[rows, :] = block[:, D:]
            at += block.shape[0]
        grad_gate[...] = jnp.zeros_like(grad_gate)
        grad_out[...] = jnp.zeros_like(grad_out)

    pick(pieces, item, held)
    h, y = h_ref[...], y_ref[...]
    do = (mod_ref[pl.ds(item, 1), 2 * D :] * held[...].astype(F32)).astype(BF)
    z = right_inner(h, gate_ref[...])
    dyg = right_inner(do, out_w[...])
    sig = jax.nn.sigmoid(z)
    act = z * sig
    dy_ref[...] = dyg * act
    mixed = (y * act).astype(BF)
    dz = (dyg * y * (sig + act * (1.0 - sig))).astype(BF)
    dz_ref[...] = dz
    o = product(mixed, out_w[...]).astype(BF)
    in_near = item < pl.num_programs(0) // 2

    @pl.when(in_near)
    def _():
        near_ref[...] = o

    @pl.when(jnp.logical_not(in_near))
    def _():
        far_ref[...] = o

    grad_gate[...] += left_outer(dz, h)
    grad_out[...] += left_outer(mixed, do)

    @pl.when(pl.program_id(0) == pl.num_programs(0) - 1)
    def _():
        at = 0
        for grad in grads:
            rows = slice(at, at + grad.shape[0])
            grad[:, :D] = grad_gate[rows, :].astype(BF)
            grad[:, D:] = grad_out[rows, :].astype(BF)
            at += grad.shape[0]


def gates(h, pieces, mod, y, blocks):
    tokens, width = y.shape
    sizes = [b.shape[0] for b in blocks]
    items = len(pieces)
    blocks = joined(blocks)
    out_shape = [
        shape(tokens, width), shape(tokens, width, BF), shape(tokens // 2, D, BF), shape(tokens // 2, D, BF), shape(width, D, BF)
    ]
    near, far = halves(tokens)
    grads = [shape(*b.shape, BF) for b in blocks]
    dy, dz, o_near, o_far, gate_full, *grads = pl.pallas_call(
        lambda *refs: gates_body(items, len(blocks), *refs),
        grid=(tokens // ITEM,),
        in_specs=[item_rows(h), fixed(mod), item_rows(y)] + [once(b) for b in (*pieces, *blocks)],
        out_specs=[item_rows(v) for v in out_shape[:2]] + [near, far, fixed(out_shape[4])] + [fixed(v) for v in grads],
        out_shape=out_shape + grads,
        scratch_shapes=[
            pltpu.VMEM((width, D), BF), pltpu.VMEM((width, D), F32), pltpu.VMEM((width, D), F32), pltpu.VMEM((ITEM, D), BF)
        ],
        compiler_params=PARAMS,
        cost_estimate=cost(24),
        name="gates",
    )(h, mod, y, *pieces, *blocks)
    return dy, dz, o_near, o_far, gate_full, parted(grads, sizes)


def mix_back_body(
    calls, count, h_ref, xs_ref, du_ref, ddtp_ref, low_ref, proj_ref, dproj_ref, dz_ref,
    x_ref, table_ref, stream_ref, gate_ref, *refs
):
    drates, drows = refs[:calls], refs[calls : 2 * calls]
    near_ref, far_ref, *grads = refs[-6 - count : -4]
    item = pl.program_id(0)
    grad_stream, grad_x, grad_tail, rows = refs[-4:]

    @pl.when(pl.program_id(0) == 0)
    def _():
        grad_stream[...] = jnp.zeros_like(grad_stream)
        grad_x[...] = jnp.zeros_like(grad_x)
        grad_tail[...] = jnp.zeros_like(grad_tail)
        rows[...] = jnp.zeros_like(rows)

    dproj = dproj_ref[...].astype(BF)
    xs = xs_ref[...]
    pre = convolved(xs, table_ref)
    sig = jax.nn.sigmoid(pre)
    dpre = (du_ref[...] + right_inner(dproj, x_ref[...])) * (sig + pre * sig * (1.0 - sig))
    dxs = jnp.zeros_like(dpre)
    for k in range(CONV):
        back = CONV - 1 - k
        dxs = dxs + delayed(dpre, -back) * table_ref[k : k + 1, :]
        rows[R + k : R + k + 1, :] += jnp.sum(dpre * delayed(xs, back), axis=0, keepdims=True)
    rows[R + BIAS : R + BIAS + 1, :] += jnp.sum(dpre, axis=0, keepdims=True)
    low = dxs.astype(BF)
    dh = product(low, stream_ref[...]) + product(dz_ref[...], gate_ref[...])
    in_near = item < pl.num_programs(0) // 2

    @pl.when(in_near)
    def _():
        near_ref[...] = dh

    @pl.when(jnp.logical_not(in_near))
    def _():
        far_ref[...] = dh.astype(BF)

    grad_stream[...] += left_outer(low, h_ref[...])
    grad_x[...] += left_outer(low_ref[...], dproj)
    lane = lax.broadcasted_iota(jnp.int32, dproj.shape, 1)
    rank = jnp.where(lane < R, proj_ref[...], 0.0).astype(BF)
    grad_tail[...] += left_outer(ddtp_ref[...], rank)

    @pl.when(pl.program_id(0) == pl.num_programs(0) - 1)
    def _():
        drow = sum(r[...] for r in drows)
        rows[R + STEP_BIAS : R + STEP_BIAS + 1, :] = jnp.sum(drow[:SUB], axis=0, keepdims=True)
        rows[R + SKIP : R + SKIP + 1, :] = jnp.sum(drow[SUB:], axis=0, keepdims=True)
        rows[R + RATE : R + CH, :] = sum(r[...] for r in drates) * -jnp.exp(table_ref[RATE:CH, :])
        grad_tail[...] += rows[...].T
        at = 0
        for grad in grads:
            part = slice(at, at + grad.shape[0])
            grad[:, :D] = grad_stream[part, :].astype(BF)
            grad[:, D : D + LANE] = grad_x[part, :].astype(BF)
            grad[:, D + LANE :] = grad_tail[part, :].astype(BF)
            at += grad.shape[0]


def mix_back(h, xs, du, ddtp, low, proj, dproj, dz, x_full, table, stream, gate, drates, drows, sizes, after):
    tokens, width = xs.shape
    aligned = all(size % 16 == 0 for size in sizes)
    blocks = [shape(size, D + SMALL, BF) for size in (sizes if aligned else [width])]
    near, far = halves(tokens)
    calls = len(drates)
    dh_near, dh_far, *grads = pl.pallas_call(
        lambda *refs: mix_back_body(calls, len(blocks), *refs),
        grid=(tokens // ITEM,),
        in_specs=[item_rows(v) for v in (h, xs, du, ddtp, low, proj, dproj, dz)]
        + [once(v) for v in (x_full, table, stream, gate, *drates, *drows)]
        + [ANYWHERE] * len(after),
        out_specs=[near, far] + [fixed(v) for v in blocks],
        out_shape=[shape(tokens // 2, D), shape(tokens // 2, D, BF)] + blocks,
        scratch_shapes=[
            pltpu.VMEM((width, D), F32), pltpu.VMEM((width, LANE), F32), pltpu.VMEM((width, LANE), F32),
            pltpu.VMEM((LANE, width), F32),
        ],
        compiler_params=PARAMS,
        cost_estimate=cost(19),
        name="mix_back",
    )(h, xs, du, ddtp, low, proj, dproj, dz, x_full, table, stream, gate, *drates, *drows, *after)
    return dh_near, dh_far, parted(grads, sizes)


def scan_prepare(proj_ref, dt_ref, table_ref, pre, rate, bc):
    pre[...] = right_inner(proj_ref[...].astype(BF), dt_ref[...]) + table_ref[STEP_BIAS : STEP_BIAS + 1, :]
    rate[...] = -jnp.exp(table_ref[RATE:CH, :]) * LOG2E
    turned = proj_ref[...].T
    for g in range(bc.shape[0]):
        bc[g, :, :SUB] = turned[R:, g * SUB : (g + 1) * SUB]


def scan_forward_body(u_ref, proj_ref, dt_ref, table_ref, *refs):
    y_ref, states_ref, pre, rate_ref, bc_ref, carry, parts = refs[-7:]
    groups = u_ref.shape[0] // SUB
    chunks = u_ref.shape[1] // LANE

    @pl.when(pl.program_id(1) == 0)
    def _():
        carry[...] = jnp.zeros_like(carry)

    scan_prepare(proj_ref, dt_ref, table_ref, pre, rate_ref, bc_ref)

    def group(g, _):
        base = pl.multiple_of(g * SUB, SUB)
        u8 = u_ref[pl.ds(base, SUB), :]
        step8 = softplus(pre[pl.ds(base, SUB), :])
        drive8 = step8 * u8
        bc = bc_ref[g]
        states = [carry[:, c * LANE : (c + 1) * LANE] for c in range(chunks)]
        for j in range(SUB):
            b = jnp.broadcast_to(bc[:N, j : j + 1], (N, LANE))
            cc = jnp.broadcast_to(bc[N:, j : j + 1], (N, LANE))
            at = pl.multiple_of((base + j) * N, N)
            for c in range(chunks):
                lanes = slice(c * LANE, (c + 1) * LANE)
                step = jnp.broadcast_to(step8[j : j + 1, lanes], (N, LANE))
                drive = jnp.broadcast_to(drive8[j : j + 1, lanes], (N, LANE))
                s = jnp.exp2(step * rate_ref[:, lanes]) * states[c] + b * drive
                states[c] = s
                states_ref[pl.ds(at, N), lanes] = s
                p = cc * s
                parts[c, j * SUB : (j + 1) * SUB, :] = p[:SUB] + p[SUB:]
        for c in range(chunks):
            lanes = slice(c * LANE, (c + 1) * LANE)
            carry[:, lanes] = states[c]
            total = table_ref[SKIP : SKIP + 1, lanes] * u8[:, lanes]
            for n in range(SUB):
                total = total + parts[c, pl.ds(n, SUB, stride=SUB), :]
            y_ref[pl.ds(base, SUB), lanes] = total
        return 0

    lax.fori_loop(0, groups, group, 0)


def scan_forward(begin, count, u, proj, dt, table, kept, after):
    total, width = u.shape
    block = SCAN_BLOCK
    steps = ITEM // block
    chunks = width // LANE
    at = lambda i, t: ((begin + i) * steps + t, 0)
    tok = pl.BlockSpec((block, width), at)
    whole = lambda v: pl.BlockSpec(v.shape, lambda i, t: (0, 0))
    extra = list(kept) + list(after)
    return pl.pallas_call(
        scan_forward_body,
        grid=(count, steps),
        in_specs=[tok, pl.BlockSpec((block, LANE), at), whole(dt), whole(table)] + [ANYWHERE] * len(extra),
        out_specs=[tok, pl.BlockSpec((block * N, width), at)],
        out_shape=[shape(total, width), shape(total * N, width)],
        scratch_shapes=[
            pltpu.VMEM((block, width), F32), pltpu.VMEM((N, width), F32), pltpu.VMEM((block // SUB, 2 * N, LANE), F32),
            pltpu.VMEM((N, width), F32), pltpu.VMEM((chunks, SUB * SUB, LANE), F32),
        ],
        input_output_aliases={4 + k: k for k in range(len(kept))},
        compiler_params=PARAMS,
        cost_estimate=cost(8 * count),
        name="scan_forward",
    )(u, proj, dt, table, *extra)


def scan_backward_body(u_ref, proj_ref, dy_ref, states_ref, before_ref, dt_ref, table_ref, *refs):
    du_ref, ddtp_ref, dproj_ref, drate_ref, drow_ref = refs[-15:-10]
    pre, rate_ref, bc_ref, ddtp, carry, parts, parts2, sums, stage, own = refs[-10:]
    block = u_ref.shape[0]
    groups = block // SUB
    chunks = u_ref.shape[1] // LANE
    back = pl.num_programs(1) - 1 - pl.program_id(1)
    first = back == 0

    @pl.when(pl.program_id(1) == 0)
    def _():
        carry[...] = jnp.zeros_like(carry)

    @pl.when((pl.program_id(0) == 0) & (pl.program_id(1) == 0))
    def _():
        drate_ref[...] = jnp.zeros_like(drate_ref)
        drow_ref[...] = jnp.zeros_like(drow_ref)

    scan_prepare(proj_ref, dt_ref, table_ref, pre, rate_ref, bc_ref)

    def group(k, _):
        g = groups - 1 - k
        base = pl.multiple_of(g * SUB, SUB)
        u8 = u_ref[pl.ds(base, SUB), :]
        pre8 = pre[pl.ds(base, SUB), :]
        step8 = softplus(pre8)
        drive8 = step8 * u8
        dy8 = dy_ref[pl.ds(base, SUB), :]
        bc = bc_ref[g]
        grads = [carry[:, c * LANE : (c + 1) * LANE] for c in range(chunks)]
        drate = [drate_ref[:, c * LANE : (c + 1) * LANE] for c in range(chunks)]
        for j in reversed(range(SUB)):
            b = jnp.broadcast_to(bc[:N, j : j + 1], (N, LANE))
            cc = jnp.broadcast_to(bc[N:, j : j + 1], (N, LANE))
            at = pl.multiple_of((base + j) * N, N)
            db = jnp.zeros((N, LANE), F32)
            dc = jnp.zeros((N, LANE), F32)
            for c in range(chunks):
                lanes = slice(c * LANE, (c + 1) * LANE)
                step = jnp.broadcast_to(step8[j : j + 1, lanes], (N, LANE))
                drive = jnp.broadcast_to(drive8[j : j + 1, lanes], (N, LANE))
                dy = jnp.broadcast_to(dy8[j : j + 1, lanes], (N, LANE))
                now = states_ref[pl.ds(at, N), lanes]
                if j > 0:
                    prev = states_ref[pl.ds(at - N, N), lanes]
                else:
                    prev = states_ref[pl.ds(pl.multiple_of(jnp.maximum(at - N, 0), N), N), lanes]
                    edge = jnp.where(first, 0.0, before_ref[:, lanes])
                    prev = jnp.where(g == 0, edge, prev)
                rate = rate_ref[:, lanes]
                grad = cc * dy + grads[c]
                dc = dc + now * dy
                db = db + grad * drive
                p = grad * b
                parts[c, j * SUB : (j + 1) * SUB, :] = p[:SUB] + p[SUB:]
                grad = grad * jnp.exp2(step * rate)
                grads[c] = grad
                q = grad * prev
                p = q * rate
                parts2[c, j * SUB : (j + 1) * SUB, :] = p[:SUB] + p[SUB:]
                drate[c] = drate[c] + q * step
            token = back * block + base + j
            sums[pl.ds(token, N, stride=PITCH), :] = db
            sums[pl.ds(N * PITCH + token, N, stride=PITCH), :] = dc
        for c in range(chunks):
            lanes = slice(c * LANE, (c + 1) * LANE)
            carry[:, lanes] = grads[c]
            drate_ref[:, lanes] = drate[c]
            x = parts[c, pl.ds(0, SUB, stride=SUB), :]
            r = parts2[c, pl.ds(0, SUB, stride=SUB), :]
            for n in range(1, SUB):
                x = x + parts[c, pl.ds(n, SUB, stride=SUB), :]
                r = r + parts2[c, pl.ds(n, SUB, stride=SUB), :]
            dy = dy8[:, lanes]
            u = u8[:, lanes]
            du_ref[pl.ds(base, SUB), lanes] = step8[:, lanes] * x + table_ref[SKIP : SKIP + 1, lanes] * dy
            d = (u * x + LN2 * r) * jax.nn.sigmoid(pre8[:, lanes])
            ddtp[pl.ds(base, SUB), lanes] = d
            drow_ref[:SUB, lanes] += d
            drow_ref[SUB:, lanes] += dy * u
        return 0

    lax.fori_loop(0, groups, group, 0)
    low = ddtp[...].astype(BF)
    ddtp_ref[...] = low
    own[pl.ds(pl.multiple_of(back * block, block), block), :] = product(low, dt_ref[...])

    @pl.when(first)
    def _():
        stage[...] = jnp.zeros_like(stage)
        ones = jnp.ones((SUB, LANE), BF)
        for n in range(2 * N):
            wide = sums[n * PITCH : n * PITCH + ITEM, :]
            high = wide.astype(BF)
            row = right_inner(ones, high) + right_inner(ones, (wide - high.astype(F32)).astype(BF))
            stage[R + n : R + n + 1, :] = row[:1]
        dproj_ref[...] = own[...] + stage[...].T


def scan_backward(begin, count, u, proj, dy, states, dt, table, kept, after):
    total, width = u.shape
    block = SCAN_BLOCK
    steps = ITEM // block
    chunks = width // LANE
    place = lambda i, t: (begin + i) * steps + steps - 1 - t
    at = lambda i, t: (place(i, t), 0)
    tok = pl.BlockSpec((block, width), at)
    whole = lambda v: pl.BlockSpec(v.shape, lambda i, t: (0, 0))
    extra = list(kept) + list(after)
    out_shape = [
        shape(total, width), shape(total, width, BF), shape(total, LANE), shape(N, width), shape(2 * SUB, width)
    ]
    return pl.pallas_call(
        scan_backward_body,
        grid=(count, steps),
        in_specs=[
            tok, pl.BlockSpec((block, LANE), at), tok,
            pl.BlockSpec((block * N, width), at),
            pl.BlockSpec((N, width), lambda i, t: (jnp.maximum(place(i, t) * block - 1, 0), 0)),
            whole(dt), whole(table),
        ]
        + [ANYWHERE] * len(extra),
        out_specs=[tok, tok, pl.BlockSpec((ITEM, LANE), lambda i, t: (begin + i, 0)), whole(out_shape[3]), whole(out_shape[4])],
        out_shape=out_shape,
        scratch_shapes=[
            pltpu.VMEM((block, width), F32), pltpu.VMEM((N, width), F32), pltpu.VMEM((block // SUB, 2 * N, LANE), F32),
            pltpu.VMEM((block, width), F32), pltpu.VMEM((N, width), F32),
            pltpu.VMEM((chunks, SUB * SUB, LANE), F32), pltpu.VMEM((chunks, SUB * SUB, LANE), F32),
            pltpu.VMEM((2 * N * PITCH, LANE), F32), pltpu.VMEM((LANE, ITEM), F32), pltpu.VMEM((ITEM, LANE), F32),
        ],
        input_output_aliases={7 + k: k for k in range(len(kept))},
        compiler_params=PARAMS,
        cost_estimate=cost(15 * count),
        name="scan_backward",
    )(u, proj, dy, states, states, dt, table, *extra)


def update_body(factor_ref, *refs):
    grads, states, outs = refs[:5], refs[5:29], refs[29:]
    factor = factor_ref[0, 0]
    ema_keep = min(0.9999, (1.0 + STEP) / (10.0 + STEP))

    def update(k, g):
        learn_rate, weight_decay = (0.5, 0.0) if k == 4 else (0.03, 0.1)
        weight, first, second, average = (states[4 * k + q][...] for q in range(4))
        clipped = g * factor
        first = 0.9 * first + 0.1 * clipped
        second = 0.999 * second + 0.001 * clipped * clipped
        first_hat = first / (1.0 - 0.9**STEP)
        second_hat = second / (1.0 - 0.999**STEP)
        weight = weight - learn_rate * (first_hat / (jnp.sqrt(second_hat) + 1e-08) + weight_decay * weight)
        average = ema_keep * average + (1.0 - ema_keep) * weight
        for q, v in enumerate((first, second, weight, average)):
            outs[4 * k + q][...] = v

    ada, wide, small, small_t, out = grads
    update(0, ada[...])
    update(1, wide[...].astype(F32))
    update(5, out[...].astype(F32))

    @pl.when(pl.program_id(0) == 0)
    def _():
        update(2, small[...])
        update(3, small_t[:R, :])
        update(4, small_t[R:CH + R, :])


def update_all(factor, ada, wide, small, small_t, out, states):
    part = 256
    right = lambda v: pl.BlockSpec((v.shape[0], part), lambda t: (0, t))
    kinds = [right, right, fixed, fixed, fixed, right]
    specs = [kind(v) for kind, group in zip(kinds, states) for v in group]
    flat = [v for group in states for v in group]
    return pl.pallas_call(
        update_body,
        grid=(D // part,),
        in_specs=[pl.BlockSpec(memory_space=pltpu.SMEM), right(ada), right(wide), fixed(small), fixed(small_t), right(out)]
        + specs,
        out_specs=specs,
        out_shape=[shape(*v.shape) for v in flat],
        compiler_params=PARAMS,
        cost_estimate=cost(11),
        name="update",
    )(factor.reshape(1, 1), ada, wide, small, small_t, out, *flat)


def embed_time(steps):
    half = D // 2
    freqs = jnp.exp(-math.log(10000.0) * jnp.arange(half, dtype=F32) / half)
    angles = steps.astype(F32)[:, None] * freqs[None, :]
    return jax.nn.silu(jnp.concatenate([jnp.cos(angles), jnp.sin(angles)], axis=1))


def normalize(x):
    mean = jnp.mean(x, axis=2, keepdims=True)
    centered = x - mean
    var = jnp.mean(centered * centered, axis=2, keepdims=True)
    scale = lax.rsqrt(var + 1e-06)
    return centered * scale, scale


def group_bits(size):
    return [1 << k for k in reversed(range(size.bit_length() - 1))]


def moved(v, axes, pairs):
    return lax.ppermute(with_layout_constraint(v, Layout(tuple(range(v.ndim)))), axes, pairs)


def swap(v, bit, size):
    return moved(v, "fsdp", [(i, i ^ bit) for i in range(size)])


def tick(v, size):
    return swap(v[:16, :LANE], 1, size)


def group_gather(v, size):
    blocks = [v]
    for bit in group_bits(size):
        blocks += [swap(b, bit, size) for b in blocks]
    return blocks


def group_sum(v, size):
    bits = group_bits(size)
    half = v.shape[0] // 2
    other = swap(v[half:], bits[-1], size)
    total = v[:half] + other
    for k, bit in enumerate(bits[:-1]):
        other = swap(total, bit, size)
        rows = other.shape[0] // (size // 2)
        total = total + jnp.concatenate(
            [other[(p ^ (1 << k)) * rows : ((p ^ (1 << k)) + 1) * rows] for p in range(size // 2)], axis=0
        )
    return jnp.concatenate([total, swap(total, bits[-1], size)], axis=0), other


def ring_order(size):
    if size == 8:
        return [0, 2, 4, 6, 7, 5, 3, 1]
    return list(range(size))


def ring_move(v, way, size):
    order = ring_order(size)
    return moved(v, "dp", [(order[p], order[(p + way) % size]) for p in range(size)])


def ring_gather_steps(v, size, split):
    behind = ahead = v
    for _ in range(size // 2 - 1):
        behind, ahead = ring_move(behind, 1, size), ring_move(ahead, -1, size)
        yield [behind, ahead]
    cut = v.shape[0] // 2
    if split:
        yield [ring_move(behind[:cut], 1, size), ring_move(ahead[cut:], -1, size)]
    else:
        yield [ring_move(behind, 1, size)]


def ring_partial(blocks, step, came, after):
    size = len(blocks) - 1
    if step == 0:
        return blocks[-2:]
    away = size // 2 - step
    ahead, behind = blocks[2 * away], blocks[2 * away - 1]
    if all(v.shape[0] % 16 == 0 for v in came):
        return ring_add(ahead, behind, *came, after)
    add = lambda a, b: (a.astype(F32) + b.astype(F32)).astype(BF)
    up, down = came
    if step == 1:
        cut = up.shape[0]
        return [
            jnp.concatenate([add(ahead[:cut], up), ahead[cut:]], axis=0),
            jnp.concatenate([behind[:-cut], add(behind[-cut:], down)], axis=0),
        ]
    return [add(ahead, up), add(behind, down)]


def ring_send(partial):
    size = lax.axis_size("dp")
    return [ring_move(partial[0], 1, size), ring_move(partial[1], -1, size)]


def ring_last(blocks, came):
    return blocks[0].astype(F32) + came[0].astype(F32) + came[1].astype(F32)


def exchange(v):
    return lax.all_to_all(v, ALL, 0, 0, tiled=True)


def on_device(sizes, *args):
    (
        act, cotangent, item_counts, item_lengths, time_steps,
        ada_weight, ada_first, ada_second, ada_average,
        in_weight, in_first, in_second, in_average,
        x_weight, x_first, x_second, x_average,
        dt_weight, dt_first, dt_second, dt_average,
        chan_table, chan_first, chan_second, chan_average,
        out_weight, out_first, out_second, out_average,
    ) = args
    n_dp, n_fsdp = sizes
    devices = n_dp * n_fsdp
    count = item_lengths.shape[0]
    items = count * n_fsdp
    tokens = items * ITEM
    ada_cols = ada_weight.shape[1]
    f = lax.axis_index("fsdp")
    half = n_dp // 2
    low_half = lax.axis_index("dp") < half
    offsets = [0]
    for bit in group_bits(n_fsdp):
        offsets = offsets + [o ^ bit for o in offsets]

    forth = []
    for b in range(devices):
        i, j = divmod(b, 2)
        k, g = divmod(i, n_fsdp)
        forth.append((b, (k + half * j) * n_fsdp + g))
    back = [(t, s) for s, t in forth]
    across = [(q, (q + half) % n_dp) for q in range(n_dp)]
    wide = in_weight.astype(BF).T
    rows = wide.shape[0] // 2
    leaving = jnp.where(low_half, wide[rows:], wide[:rows])
    swapped = moved(leaving, "dp", across)
    small = jnp.concatenate([x_weight.astype(BF), dt_weight.astype(BF).T, chan_table.astype(BF).T], axis=1)
    small = jnp.pad(small, ((0, 0), (0, SMALL - small.shape[1])))
    small = moved(hold(small, leaving), ALL, forth)
    stream_own = jnp.concatenate([jnp.where(low_half, wide[:rows], swapped), small], axis=1)
    gate_own = jnp.where(low_half, swapped, wide[rows:])

    live_items = jnp.arange(count, dtype=jnp.int32) < item_counts[0]
    live_rows = jnp.arange(ITEM, dtype=jnp.int32)[None, :] < item_lengths[:, None]
    live = live_items[:, None] & live_rows
    dfinal_own = jnp.where(live[..., None], cotangent.reshape(count, ITEM, D), jnp.zeros((), BF))
    x_all = group_gather(act.reshape(count * ITEM, D), n_fsdp)

    steps_all = exchange(hold(jnp.broadcast_to(time_steps[None], (devices, count)), leaving)).reshape(-1)
    cond_all = embed_time(steps_all).astype(BF)
    mod_cols = product(cond_all, ada_weight.astype(BF)).reshape(n_dp, 1, items, ada_cols)
    mod_cols = jnp.broadcast_to(mod_cols, (n_dp, n_fsdp, items, ada_cols)).reshape(devices, items, ada_cols)
    mod = exchange(hold(mod_cols, tick(stream_own, n_fsdp)))
    dfinal_all = group_gather(hold(dfinal_own.reshape(count * ITEM, D), mod), n_fsdp)
    mod = jnp.swapaxes(mod, 0, 1).reshape(n_fsdp, count, 3 * D)
    mod = jnp.take(mod, jnp.array(offsets, jnp.int32) ^ f, axis=0).reshape(items, 3 * D)

    stream = [stream_own]
    for came in ring_gather_steps(stream_own, n_dp, False):
        stream += came
    out_own = moved(hold(out_weight.astype(BF), stream[half - 1]), ALL, forth)
    rest_own = hold(jnp.concatenate([gate_own, out_own], axis=1), tick(stream[-2], n_fsdp))
    rest_steps = list(ring_gather_steps(rest_own, n_dp, True))
    rest = [rest_own] + sum(rest_steps, [])

    h_low, xs, u, u_low, proj, stream_full, x_full, dt_full, table = mix(x_all, mod, stream, [rest_own, *dfinal_all])
    proj, _ = group_sum(hold(proj, *rest_steps[0]), n_fsdp)
    calls = 2
    part = items // calls
    kept = []
    for i in range(calls):
        kept = scan_forward(i * part, part, u, proj, dt_full, table, kept, rest_steps[half // 2 - 1 + i])
    y, states = kept

    dy, dz_low, o_own, o_far, gate_full, early = gates(h_low, dfinal_all, mod, y, rest)
    bits = group_bits(n_fsdp)[::-1]
    kept, drates, drows, came, o_came = [], [], [], None, None
    for i in range(calls):
        partial = ring_partial(early, i, came, drates[-1:])
        came = ring_send(partial)
        *kept, drate, drow = scan_backward(
            i * part, part, u, proj, dy, states, dt_full, table, kept, [*partial, *([] if i else [o_far])]
        )
        drates.append(drate)
        drows.append(drow)
        if i == 0:
            o_came = swap(o_far, bits[0], n_fsdp)
    beside = came
    partial = ring_partial(early, calls, came, drates[-1:])
    came = ring_send(partial)
    du_scan, ddtp_low, dproj = kept

    dproj, other = group_sum(hold(dproj, *beside), n_fsdp)
    for bit in bits[1:]:
        o_own, o_far = fold(o_own, o_came, [other])
        o_came = swap(o_far, bit, n_fsdp)
    o_own = o_own.astype(F32) + o_came.astype(F32)
    dh, dh_far, late = mix_back(
        h_low, xs, du_scan, ddtp_low, u_low, proj, dproj, dz_low, x_full, table, stream_full, gate_full,
        drates, drows, ring_sizes(rows, n_dp), [o_far, *partial]
    )
    dh_far, *late[-2:] = [hold(v, *came, o_came) for v in (dh_far, *late[-2:])]
    for i in range(calls + 1, half):
        came = ring_send(ring_partial(early, i, came, late[-1:]))
    early_sum = ring_last(early, came)
    last_early, came, dh_came = came, None, None
    for i in range(half):
        if 0 < i < len(bits):
            dh, dh_far = fold(dh, dh_came, [])
        after = [dh_far] if i == 1 else last_early if i == 2 else [dh_came] if i == half - 1 else []
        came = ring_send(ring_partial(late, i, came, after))
        if i < len(bits):
            dh_came = swap(dh_far, bits[i], n_fsdp)
    dh = dh + dh_came.astype(F32)
    late_sum = ring_last(late, came)
    squares = jnp.sum(early_sum * early_sum) + jnp.sum(late_sum * late_sum)
    small = moved(late_sum[:, D:].astype(BF), ALL, back).astype(F32)
    small_t = small[:, LANE:].T
    late_sum = late_sum[:, :D].astype(BF)
    gate_sum = early_sum[:, :D].astype(BF)
    gate_moved = moved(hold(gate_sum, late_sum), "dp", [(q, q + half) for q in range(half)])
    out_share = moved(hold(early_sum[:, D:].astype(BF), late_sum), ALL, back)
    late_moved = moved(late_sum, "dp", [(q + half, q) for q in range(half)])
    in_share = jnp.concatenate(
        [jnp.where(low_half, late_sum, gate_moved), jnp.where(low_half, late_moved, gate_sum)], axis=0
    )
    dh, o_own = dh.reshape(count, ITEM, D), o_own.reshape(count, ITEM, D)

    x = act.astype(F32).reshape(count, ITEM, D)
    normed, inverse = normalize(x)
    dfinal = dfinal_own.astype(F32)
    scale, gate = mod[:count, None, D : 2 * D], mod[:count, None, 2 * D :]
    final = x + gate * o_own
    dmod = jnp.concatenate(
        [jnp.sum(dh, axis=1), jnp.sum(dh * normed, axis=1), jnp.sum(dfinal * o_own, axis=1)], axis=1
    ).astype(BF)
    dn = dh * (1.0 + scale)
    act_grad = dfinal + inverse * (
        dn - jnp.mean(dn, axis=2, keepdims=True) - normed * jnp.mean(dn * normed, axis=2, keepdims=True)
    )
    dmod = hold(dmod, late_sum)
    dmod_all = exchange(jnp.swapaxes(dmod.reshape(count, devices, ada_cols), 0, 1)).reshape(devices * count, ada_cols)
    ada_share = left_outer(dmod_all, cond_all)

    local = squares + jnp.sum(ada_share * ada_share)
    total = jnp.sum(exchange(jnp.broadcast_to(local, (devices, LANE)))[:, 0])
    grad_norm = jnp.sqrt(total)
    factor = jnp.minimum(1.0, 1.0 / (grad_norm + 1e-06))
    results = update_all(
        factor, ada_share, in_share, small[:, :LANE], small_t, out_share,
        (
            (ada_weight.T, ada_first.T, ada_second.T, ada_average.T),
            (in_weight.T, in_first.T, in_second.T, in_average.T),
            (x_weight, x_first, x_second, x_average),
            (dt_weight, dt_first, dt_second, dt_average),
            (chan_table, chan_first, chan_second, chan_average),
            (out_weight, out_first, out_second, out_average),
        ),
    )
    results = [v.T for v in results[:8]] + list(results[8:])
    return (final.reshape(count * ITEM, D), act_grad.reshape(count * ITEM, D), grad_norm, *results)


def solution(mesh):
    sizes = (mesh.shape["dp"], mesh.shape["fsdp"])
    first, second = P(ALL, None), P(None, ALL)
    weights = [second] * 8 + [first] * 4 + [second] * 8 + [first] * 4
    return jax.shard_map(
        lambda *args: on_device(sizes, *args),
        mesh=mesh,
        in_specs=(first, first, P(ALL), P(ALL), P(ALL), *weights),
        out_specs=(first, first, P(), *weights),
        check_vma=False,
    )
```

```python
import math

import jax
import jax.numpy as jnp
from jax import lax
from jax.experimental import pallas as pl
from jax.experimental.layout import Layout, with_layout_constraint
from jax.experimental.pallas import tpu as pltpu
from jax.sharding import PartitionSpec as P

D = 1536
E = 3072
N = 16
R = 96
CONV = 4
CH = 7 + N
ITEM = 256
STEP = 10
SUB = 8
LANE = 128
BIAS, STEP_BIAS, SKIP, RATE = CONV, CONV + 1, CONV + 2, CONV + 3
TABLE = 32
SMALL = 2 * LANE
ALL = ("dp", "fsdp")
LOG2E = math.log2(math.e)
LN2 = math.log(2.0)
F32 = jnp.float32
BF = jnp.bfloat16
VMEM_LIMIT = 60 * 1024 * 1024
SCAN_BLOCK = 64
PITCH = ITEM + SUB


def product(left, right):
    return jnp.dot(left, right, preferred_element_type=F32)


def left_outer(left, right):
    return lax.dot_general(left, right, (((0,), (0,)), ((), ())), preferred_element_type=F32)


def right_inner(left, right):
    return lax.dot_general(left, right, (((1,), (1,)), ((), ())), preferred_element_type=F32)


def softplus(v):
    return jnp.maximum(v, 0.0) + jnp.log1p(jnp.exp(-jnp.abs(v)))


def shape(rows, columns, dtype=F32):
    return jax.ShapeDtypeStruct((rows, columns), dtype)


def item_rows(v):
    return pl.BlockSpec((ITEM, v.shape[1]), lambda i: (i, 0))


def halves(tokens):
    last = tokens // ITEM // 2 - 1
    near = pl.BlockSpec((ITEM, D), lambda i: (jnp.minimum(i, last), 0))
    return near, pl.BlockSpec((ITEM, D), lambda i: (jnp.maximum(i - last - 1, 0), 0))


def fixed(v):
    return pl.BlockSpec(v.shape, lambda i: (0, 0))


def once(v):
    return pl.BlockSpec(v.shape, lambda i: (0, 0), pipeline_mode=pl.Buffered(1))


ANYWHERE = pl.BlockSpec(memory_space=pl.ANY)
PARAMS = pltpu.CompilerParams(vmem_limit_bytes=VMEM_LIMIT)


def cost(us):
    return pl.CostEstimate(flops=int(us * 1e9), bytes_accessed=int(us * 1e6), transcendentals=0)


def hold_body(v_ref, *refs):
    pass


def hold(v, *after):
    return pl.pallas_call(
        hold_body,
        in_specs=[ANYWHERE] * (1 + len(after)),
        out_specs=ANYWHERE,
        out_shape=jax.ShapeDtypeStruct(v.shape, v.dtype),
        input_output_aliases={0: 0},
        name="hold",
    )(v, *after)


def ring_sizes(rows, size):
    return [rows] * (size - 1) + [rows // 2] * 2


def joined(blocks):
    return blocks if all(b.shape[0] % 16 == 0 for b in blocks) else [jnp.concatenate(blocks, axis=0)]


def parted(blocks, sizes):
    if len(blocks) == len(sizes):
        return list(blocks)
    ends = [sum(sizes[: k + 1]) for k in range(len(sizes))]
    return [blocks[0][end - size : end] for end, size in zip(ends, sizes)]


def pick(refs, item, held):
    for p, ref in enumerate(refs):
        @pl.when(item == p)
        def _(ref=ref):
            held[...] = ref[...]


def fold_body(near_ref, came_ref, *refs):
    keep_ref, away_ref = refs[-2:]
    half = keep_ref.shape[0]
    keep_ref[...] = near_ref[:half, :].astype(F32) + came_ref[:half, :].astype(F32)
    away_ref[...] = (near_ref[half:, :].astype(F32) + came_ref[half:, :].astype(F32)).astype(BF)


def fold(near, came, after):
    half = near.shape[0] // 2
    whole = pl.BlockSpec(memory_space=pltpu.VMEM)
    return pl.pallas_call(
        fold_body,
        in_specs=[whole, whole] + [ANYWHERE] * len(after),
        out_specs=[whole, whole],
        out_shape=[shape(half, near.shape[1]), shape(half, near.shape[1], BF)],
        compiler_params=PARAMS,
        cost_estimate=cost(2),
        name="fold",
    )(near, came, *after)


def ring_add_body(ahead_ref, behind_ref, up_ref, down_ref, *refs):
    up, down = up_ref.shape[0], down_ref.shape[0]
    rows = ahead_ref.shape[0]
    to_ahead, to_behind = refs[-2:]
    to_ahead[:up, :] = (ahead_ref[:up, :].astype(F32) + up_ref[...].astype(F32)).astype(BF)
    to_behind[rows - down :, :] = (behind_ref[rows - down :, :].astype(F32) + down_ref[...].astype(F32)).astype(BF)
    if up < rows:
        to_ahead[up:, :] = ahead_ref[up:, :]
        to_behind[: rows - down, :] = behind_ref[: rows - down, :]


def ring_add(ahead, behind, up, down, after):
    whole = pl.BlockSpec(memory_space=pltpu.VMEM)
    return pl.pallas_call(
        ring_add_body,
        in_specs=[whole] * 4 + [ANYWHERE] * len(after),
        out_specs=[whole, whole],
        out_shape=[shape(*ahead.shape, BF)] * 2,
        compiler_params=PARAMS,
        cost_estimate=cost(2),
        name="ring_add",
    )(ahead, behind, up, down, *after)


def delayed(v, k):
    if k == 0:
        return v
    row = lax.broadcasted_iota(jnp.int32, v.shape, 0)
    moved = pltpu.roll(v, k % v.shape[0], axis=0)
    return jnp.where(row >= k if k > 0 else row < v.shape[0] + k, moved, 0.0)


def convolved(xs, table):
    pre = table[BIAS : BIAS + 1, :]
    for k in range(CONV):
        pre = pre + delayed(xs, CONV - 1 - k) * table[k : k + 1, :]
    return pre


def mix_body(items, count, mod_ref, *refs):
    pieces, blocks = refs[:items], refs[items : items + count]
    h_ref, xs_ref, u_ref, low_ref, proj_ref, stream_ref, x_ref, dt_ref, table_ref, tail, held = refs[-11:]

    @pl.when(pl.program_id(0) == 0)
    def _():
        at = 0
        for block in blocks:
            rows = slice(at, at + block.shape[0])
            stream_ref[rows, :] = block[:, :D]
            x_ref[rows, :] = block[:, D : D + LANE]
            tail[rows, :] = block[:, D + LANE :].astype(F32)
            at += block.shape[0]
        lane = lax.broadcasted_iota(jnp.int32, tail.shape, 1)
        dt_ref[...] = jnp.where(lane < R, tail[...], 0.0).astype(BF)
        table_ref[...] = tail[...].T[R:, :]

    pick(pieces, pl.program_id(0), held)
    x = held[...].astype(F32)
    centered = x - jnp.mean(x, axis=1, keepdims=True)
    normed = centered * lax.rsqrt(jnp.mean(centered * centered, axis=1, keepdims=True) + 1e-06)
    mod = mod_ref[pl.ds(pl.program_id(0), 1), :]
    h = (normed * (1.0 + mod[:, D : 2 * D]) + mod[:, :D]).astype(BF)
    h_ref[...] = h
    xs = right_inner(h, stream_ref[...])
    xs_ref[...] = xs
    pre = convolved(xs, table_ref)
    u = pre * jax.nn.sigmoid(pre)
    u_ref[...] = u
    low = u.astype(BF)
    low_ref[...] = low
    proj_ref[...] = product(low, x_ref[...])


def mix(pieces, mod, blocks, after):
    items = len(pieces)
    tokens = items * ITEM
    blocks = joined(blocks)
    width = sum(b.shape[0] for b in blocks)
    out_shape = [
        shape(tokens, D, BF), shape(tokens, width), shape(tokens, width), shape(tokens, width, BF), shape(tokens, LANE),
        shape(width, D, BF), shape(width, LANE, BF), shape(width, LANE, BF), shape(TABLE, width),
    ]
    return pl.pallas_call(
        lambda *refs: mix_body(items, len(blocks), *refs),
        grid=(items,),
        in_specs=[fixed(mod)] + [once(v) for v in (*pieces, *blocks)] + [ANYWHERE] * len(after),
        out_specs=[item_rows(v) for v in out_shape[:5]] + [fixed(v) for v in out_shape[5:]],
        out_shape=out_shape,
        scratch_shapes=[pltpu.VMEM((width, LANE), F32), pltpu.VMEM((ITEM, D), BF)],
        compiler_params=PARAMS,
        cost_estimate=cost(11),
        name="mix",
    )(mod, *pieces, *blocks, *after)


def gates_body(items, count, h_ref, mod_ref, y_ref, *refs):
    here = pl.ds(pl.multiple_of(pl.program_id(0) * ITEM, ITEM), ITEM)
    pieces, blocks = refs[:items], refs[items : items + count]
    dy_ref, dz_ref, near_ref, far_ref, gate_ref, *grads = refs[items + count : -4]
    out_w, all_dz, all_mixed, all_do = refs[-4:]
    item = pl.program_id(0)

    @pl.when(pl.program_id(0) == 0)
    def _():
        at = 0
        for block in blocks:
            rows = slice(at, at + block.shape[0])
            gate_ref[rows, :] = block[:, :D]
            out_w[rows, :] = block[:, D:]
            at += block.shape[0]

    pick(pieces, item, all_do.at[here])
    h, y = h_ref[here, :], y_ref[...]
    do = (mod_ref[pl.ds(item, 1), 2 * D :] * all_do[here, :].astype(F32)).astype(BF)
    all_do[here, :] = do
    z = right_inner(h, gate_ref[...])
    dyg = right_inner(do, out_w[...])
    sig = jax.nn.sigmoid(z)
    act = z * sig
    dy_ref[...] = dyg * act
    mixed = (y * act).astype(BF)
    dz = (dyg * y * (sig + act * (1.0 - sig))).astype(BF)
    dz_ref[...] = dz
    all_dz[here, :] = dz
    all_mixed[here, :] = mixed
    o = product(mixed, out_w[...]).astype(BF)
    in_near = item < pl.num_programs(0) // 2

    @pl.when(in_near)
    def _():
        near_ref[...] = o

    @pl.when(jnp.logical_not(in_near))
    def _():
        far_ref[...] = o

    @pl.when(pl.program_id(0) == pl.num_programs(0) - 1)
    def _():
        for lanes, left, right in ((slice(D), all_dz, h_ref), (slice(D, 2 * D), all_mixed, all_do)):
            total = left_outer(left[...], right[...]).astype(BF)
            at = 0
            for grad in grads:
                grad[:, lanes] = total[at : at + grad.shape[0], :]
                at += grad.shape[0]


def gates(h, pieces, mod, y, blocks):
    tokens, width = y.shape
    sizes = [b.shape[0] for b in blocks]
    items = len(pieces)
    blocks = joined(blocks)
    out_shape = [
        shape(tokens, width), shape(tokens, width, BF), shape(tokens // 2, D, BF), shape(tokens // 2, D, BF), shape(width, D, BF)
    ]
    near, far = halves(tokens)
    grads = [shape(*b.shape, BF) for b in blocks]
    dy, dz, o_near, o_far, gate_full, *grads = pl.pallas_call(
        lambda *refs: gates_body(items, len(blocks), *refs),
        grid=(tokens // ITEM,),
        in_specs=[once(h), fixed(mod), item_rows(y)] + [once(b) for b in (*pieces, *blocks)],
        out_specs=[item_rows(v) for v in out_shape[:2]] + [near, far, fixed(out_shape[4])] + [fixed(v) for v in grads],
        out_shape=out_shape + grads,
        scratch_shapes=[
            pltpu.VMEM((width, D), BF), pltpu.VMEM((tokens, width), BF), pltpu.VMEM((tokens, width), BF),
            pltpu.VMEM((tokens, D), BF),
        ],
        compiler_params=PARAMS,
        cost_estimate=cost(24),
        name="gates",
    )(h, mod, y, *pieces, *blocks)
    return dy, dz, o_near, o_far, gate_full, parted(grads, sizes)


def mix_back_body(
    calls, count, h_ref, xs_ref, du_ref, ddtp_ref, low_ref, proj_ref, dproj_ref, dz_ref,
    x_ref, table_ref, stream_ref, gate_ref, *refs
):
    drates, drows = refs[:calls], refs[calls : 2 * calls]
    near_ref, far_ref, *grads = refs[-6 - count : -4]
    item = pl.program_id(0)
    grad_stream, grad_x, grad_tail, rows = refs[-4:]

    @pl.when(pl.program_id(0) == 0)
    def _():
        grad_stream[...] = jnp.zeros_like(grad_stream)
        grad_x[...] = jnp.zeros_like(grad_x)
        grad_tail[...] = jnp.zeros_like(grad_tail)
        rows[...] = jnp.zeros_like(rows)

    dproj = dproj_ref[...].astype(BF)
    xs = xs_ref[...]
    pre = convolved(xs, table_ref)
    sig = jax.nn.sigmoid(pre)
    dpre = (du_ref[...] + right_inner(dproj, x_ref[...])) * (sig + pre * sig * (1.0 - sig))
    dxs = jnp.zeros_like(dpre)
    for k in range(CONV):
        back = CONV - 1 - k
        dxs = dxs + delayed(dpre, -back) * table_ref[k : k + 1, :]
        rows[R + k : R + k + 1, :] += jnp.sum(dpre * delayed(xs, back), axis=0, keepdims=True)
    rows[R + BIAS : R + BIAS + 1, :] += jnp.sum(dpre, axis=0, keepdims=True)
    low = dxs.astype(BF)
    dh = product(low, stream_ref[...]) + product(dz_ref[...], gate_ref[...])
    in_near = item < pl.num_programs(0) // 2

    @pl.when(in_near)
    def _():
        near_ref[...] = dh

    @pl.when(jnp.logical_not(in_near))
    def _():
        far_ref[...] = dh.astype(BF)

    grad_stream[...] += left_outer(low, h_ref[...])
    grad_x[...] += left_outer(low_ref[...], dproj)
    lane = lax.broadcasted_iota(jnp.int32, dproj.shape, 1)
    rank = jnp.where(lane < R, proj_ref[...], 0.0).astype(BF)
    grad_tail[...] += left_outer(ddtp_ref[...], rank)

    @pl.when(pl.program_id(0) == pl.num_programs(0) - 1)
    def _():
        drow = sum(r[...] for r in drows)
        rows[R + STEP_BIAS : R + STEP_BIAS + 1, :] = jnp.sum(drow[:SUB], axis=0, keepdims=True)
        rows[R + SKIP : R + SKIP + 1, :] = jnp.sum(drow[SUB:], axis=0, keepdims=True)
        rows[R + RATE : R + CH, :] = sum(r[...] for r in drates) * -jnp.exp(table_ref[RATE:CH, :])
        grad_tail[...] += rows[...].T
        at = 0
        for grad in grads:
            part = slice(at, at + grad.shape[0])
            grad[:, :D] = grad_stream[part, :].astype(BF)
            grad[:, D : D + LANE] = grad_x[part, :].astype(BF)
            grad[:, D + LANE :] = grad_tail[part, :].astype(BF)
            at += grad.shape[0]


def mix_back(h, xs, du, ddtp, low, proj, dproj, dz, x_full, table, stream, gate, drates, drows, sizes, after):
    tokens, width = xs.shape
    aligned = all(size % 16 == 0 for size in sizes)
    blocks = [shape(size, D + SMALL, BF) for size in (sizes if aligned else [width])]
    near, far = halves(tokens)
    calls = len(drates)
    dh_near, dh_far, *grads = pl.pallas_call(
        lambda *refs: mix_back_body(calls, len(blocks), *refs),
        grid=(tokens // ITEM,),
        in_specs=[item_rows(v) for v in (h, xs, du, ddtp, low, proj, dproj, dz)]
        + [once(v) for v in (x_full, table, stream, gate, *drates, *drows)]
        + [ANYWHERE] * len(after),
        out_specs=[near, far] + [fixed(v) for v in blocks],
        out_shape=[shape(tokens // 2, D), shape(tokens // 2, D, BF)] + blocks,
        scratch_shapes=[
            pltpu.VMEM((width, D), F32), pltpu.VMEM((width, LANE), F32), pltpu.VMEM((width, LANE), F32),
            pltpu.VMEM((LANE, width), F32),
        ],
        compiler_params=PARAMS,
        cost_estimate=cost(19),
        name="mix_back",
    )(h, xs, du, ddtp, low, proj, dproj, dz, x_full, table, stream, gate, *drates, *drows, *after)
    return dh_near, dh_far, parted(grads, sizes)


def scan_prepare(u_ref, proj_ref, dt_ref, table_ref, pre, step, drive, rate, bc):
    pre[...] = right_inner(proj_ref[...].astype(BF), dt_ref[...]) + table_ref[STEP_BIAS : STEP_BIAS + 1, :]
    step[...] = softplus(pre[...])
    drive[...] = step[...] * u_ref[...]
    rate[...] = -jnp.exp(table_ref[RATE:CH, :]) * LOG2E
    turned = proj_ref[...].T
    for g in range(bc.shape[0]):
        bc[g, :, :SUB] = turned[R:, g * SUB : (g + 1) * SUB]


def scan_forward_body(u_ref, proj_ref, dt_ref, table_ref, *refs):
    y_ref, states_ref, pre, step_ref, drive_ref, rate_ref, bc_ref, carry, parts = refs[-9:]
    groups = u_ref.shape[0] // SUB
    chunks = u_ref.shape[1] // LANE

    @pl.when(pl.program_id(1) == 0)
    def _():
        carry[...] = jnp.zeros_like(carry)

    scan_prepare(u_ref, proj_ref, dt_ref, table_ref, pre, step_ref, drive_ref, rate_ref, bc_ref)

    def group(g, _):
        base = pl.multiple_of(g * SUB, SUB)
        step8 = step_ref[pl.ds(base, SUB), :]
        drive8 = drive_ref[pl.ds(base, SUB), :]
        bc = bc_ref[g]
        states = [carry[:, c * LANE : (c + 1) * LANE] for c in range(chunks)]
        for j in range(SUB):
            b = jnp.broadcast_to(bc[:N, j : j + 1], (N, LANE))
            cc = jnp.broadcast_to(bc[N:, j : j + 1], (N, LANE))
            at = pl.multiple_of((base + j) * N, N)
            for c in range(chunks):
                lanes = slice(c * LANE, (c + 1) * LANE)
                step = jnp.broadcast_to(step8[j : j + 1, lanes], (N, LANE))
                drive = jnp.broadcast_to(drive8[j : j + 1, lanes], (N, LANE))
                s = jnp.exp2(step * rate_ref[:, lanes]) * states[c] + b * drive
                states[c] = s
                states_ref[pl.ds(at, N), lanes] = s
                p = cc * s
                parts[c, pl.ds(pl.multiple_of((base + j) * SUB, SUB), SUB), :] = p[:SUB] + p[SUB:]
        for c in range(chunks):
            lanes = slice(c * LANE, (c + 1) * LANE)
            carry[:, lanes] = states[c]
        return 0

    lax.fori_loop(0, groups, group, 0)
    for c in range(chunks):
        lanes = slice(c * LANE, (c + 1) * LANE)
        total = table_ref[SKIP : SKIP + 1, lanes] * u_ref[:, lanes]
        for n in range(SUB):
            total = total + parts[c, pl.ds(n, groups * SUB, stride=SUB), :]
        y_ref[:, lanes] = total


def scan_forward(begin, count, u, proj, dt, table, kept, after):
    total, width = u.shape
    block = SCAN_BLOCK
    steps = ITEM // block
    chunks = width // LANE
    at = lambda i, t: ((begin + i) * steps + t, 0)
    tok = pl.BlockSpec((block, width), at)
    whole = lambda v: pl.BlockSpec(v.shape, lambda i, t: (0, 0))
    extra = list(kept) + list(after)
    return pl.pallas_call(
        scan_forward_body,
        grid=(count, steps),
        in_specs=[tok, pl.BlockSpec((block, LANE), at), whole(dt), whole(table)] + [ANYWHERE] * len(extra),
        out_specs=[tok, pl.BlockSpec((block * N, width), at)],
        out_shape=[shape(total, width), shape(total * N, width)],
        scratch_shapes=[
            *[pltpu.VMEM((block, width), F32)] * 3, pltpu.VMEM((N, width), F32),
            pltpu.VMEM((block // SUB, 2 * N, LANE), F32),
            pltpu.VMEM((N, width), F32), pltpu.VMEM((chunks, block * SUB, LANE), F32),
        ],
        input_output_aliases={4 + k: k for k in range(len(kept))},
        compiler_params=PARAMS,
        cost_estimate=cost(8 * count),
        name="scan_forward",
    )(u, proj, dt, table, *extra)


def scan_backward_body(u_ref, proj_ref, dy_ref, states_ref, before_ref, dt_ref, table_ref, *refs):
    du_ref, ddtp_ref, dproj_ref, drate_ref, drow_ref = refs[-16:-11]
    pre, step_ref, drive_ref, rate_ref, bc_ref, carry, parts, parts2, sums, stage, own = refs[-11:]
    block = u_ref.shape[0]
    groups = block // SUB
    chunks = u_ref.shape[1] // LANE
    back = pl.num_programs(1) - 1 - pl.program_id(1)
    first = back == 0

    @pl.when(pl.program_id(1) == 0)
    def _():
        carry[...] = jnp.zeros_like(carry)

    @pl.when((pl.program_id(0) == 0) & (pl.program_id(1) == 0))
    def _():
        drate_ref[...] = jnp.zeros_like(drate_ref)
        drow_ref[...] = jnp.zeros_like(drow_ref)

    scan_prepare(u_ref, proj_ref, dt_ref, table_ref, pre, step_ref, drive_ref, rate_ref, bc_ref)

    def group(k, _):
        g = groups - 1 - k
        base = pl.multiple_of(g * SUB, SUB)
        step8 = step_ref[pl.ds(base, SUB), :]
        drive8 = drive_ref[pl.ds(base, SUB), :]
        dy8 = dy_ref[pl.ds(base, SUB), :]
        bc = bc_ref[g]
        grads = [carry[:, c * LANE : (c + 1) * LANE] for c in range(chunks)]
        drate = [drate_ref[:, c * LANE : (c + 1) * LANE] for c in range(chunks)]
        for j in reversed(range(SUB)):
            b = jnp.broadcast_to(bc[:N, j : j + 1], (N, LANE))
            cc = jnp.broadcast_to(bc[N:, j : j + 1], (N, LANE))
            at = pl.multiple_of((base + j) * N, N)
            db = jnp.zeros((N, LANE), F32)
            dc = jnp.zeros((N, LANE), F32)
            for c in range(chunks):
                lanes = slice(c * LANE, (c + 1) * LANE)
                step = jnp.broadcast_to(step8[j : j + 1, lanes], (N, LANE))
                drive = jnp.broadcast_to(drive8[j : j + 1, lanes], (N, LANE))
                dy = jnp.broadcast_to(dy8[j : j + 1, lanes], (N, LANE))
                now = states_ref[pl.ds(at, N), lanes]
                if j > 0:
                    prev = states_ref[pl.ds(at - N, N), lanes]
                else:
                    prev = states_ref[pl.ds(pl.multiple_of(jnp.maximum(at - N, 0), N), N), lanes]
                    edge = jnp.where(first, 0.0, before_ref[:, lanes])
                    prev = jnp.where(g == 0, edge, prev)
                rate = rate_ref[:, lanes]
                grad = cc * dy + grads[c]
                dc = dc + now * dy
                db = db + grad * drive
                p = grad * b
                parts[c, pl.ds(pl.multiple_of((base + j) * SUB, SUB), SUB), :] = p[:SUB] + p[SUB:]
                grad = grad * jnp.exp2(step * rate)
                grads[c] = grad
                q = grad * prev
                p = q * rate
                parts2[c, pl.ds(pl.multiple_of((base + j) * SUB, SUB), SUB), :] = p[:SUB] + p[SUB:]
                drate[c] = drate[c] + q * step
            token = back * block + base + j
            sums[pl.ds(token, N, stride=PITCH), :] = db
            sums[pl.ds(N * PITCH + token, N, stride=PITCH), :] = dc
        for c in range(chunks):
            lanes = slice(c * LANE, (c + 1) * LANE)
            carry[:, lanes] = grads[c]
            drate_ref[:, lanes] = drate[c]
        return 0

    lax.fori_loop(0, groups, group, 0)
    for c in range(chunks):
        lanes = slice(c * LANE, (c + 1) * LANE)
        x = parts[c, pl.ds(0, block, stride=SUB), :]
        r = parts2[c, pl.ds(0, block, stride=SUB), :]
        for n in range(1, SUB):
            x = x + parts[c, pl.ds(n, block, stride=SUB), :]
            r = r + parts2[c, pl.ds(n, block, stride=SUB), :]
        dy, u, step = dy_ref[:, lanes], u_ref[:, lanes], step_ref[:, lanes]
        du_ref[:, lanes] = step * x + table_ref[SKIP : SKIP + 1, lanes] * dy
        d = (u * x + LN2 * r) * jax.nn.sigmoid(pre[:, lanes])
        ddtp_ref[:, lanes] = d.astype(BF)
        drow_ref[:SUB, lanes] += jnp.sum(d.reshape(groups, SUB, LANE), axis=0)
        drow_ref[SUB:, lanes] += jnp.sum((dy * u).reshape(groups, SUB, LANE), axis=0)
    low = ddtp_ref[...]
    own[pl.ds(pl.multiple_of(back * block, block), block), :] = product(low, dt_ref[...])

    @pl.when(first)
    def _():
        stage[...] = jnp.zeros_like(stage)
        ones = jnp.ones((SUB, LANE), BF)
        for n in range(2 * N):
            wide = sums[n * PITCH : n * PITCH + ITEM, :]
            high = wide.astype(BF)
            row = right_inner(ones, high) + right_inner(ones, (wide - high.astype(F32)).astype(BF))
            stage[R + n : R + n + 1, :] = row[:1]
        dproj_ref[...] = own[...] + stage[...].T


def scan_backward(begin, count, u, proj, dy, states, dt, table, kept, after):
    total, width = u.shape
    block = SCAN_BLOCK
    steps = ITEM // block
    chunks = width // LANE
    place = lambda i, t: (begin + i) * steps + steps - 1 - t
    at = lambda i, t: (place(i, t), 0)
    tok = pl.BlockSpec((block, width), at)
    whole = lambda v: pl.BlockSpec(v.shape, lambda i, t: (0, 0))
    extra = list(kept) + list(after)
    out_shape = [
        shape(total, width), shape(total, width, BF), shape(total, LANE), shape(N, width), shape(2 * SUB, width)
    ]
    return pl.pallas_call(
        scan_backward_body,
        grid=(count, steps),
        in_specs=[
            tok, pl.BlockSpec((block, LANE), at), tok,
            pl.BlockSpec((block * N, width), at),
            pl.BlockSpec((N, width), lambda i, t: (jnp.maximum(place(i, t) * block - 1, 0), 0)),
            whole(dt), whole(table),
        ]
        + [ANYWHERE] * len(extra),
        out_specs=[tok, tok, pl.BlockSpec((ITEM, LANE), lambda i, t: (begin + i, 0)), whole(out_shape[3]), whole(out_shape[4])],
        out_shape=out_shape,
        scratch_shapes=[
            *[pltpu.VMEM((block, width), F32)] * 3, pltpu.VMEM((N, width), F32),
            pltpu.VMEM((block // SUB, 2 * N, LANE), F32), pltpu.VMEM((N, width), F32),
            *[pltpu.VMEM((chunks, block * SUB, LANE), F32)] * 2,
            pltpu.VMEM((2 * N * PITCH, LANE), F32), pltpu.VMEM((LANE, ITEM), F32), pltpu.VMEM((ITEM, LANE), F32),
        ],
        input_output_aliases={7 + k: k for k in range(len(kept))},
        compiler_params=PARAMS,
        cost_estimate=cost(15 * count),
        name="scan_backward",
    )(u, proj, dy, states, states, dt, table, *extra)


def update_body(factor_ref, *refs):
    grads, states, outs = refs[:5], refs[5:29], refs[29:]
    factor = factor_ref[0, 0]
    ema_keep = min(0.9999, (1.0 + STEP) / (10.0 + STEP))

    def update(k, g):
        learn_rate, weight_decay = (0.5, 0.0) if k == 4 else (0.03, 0.1)
        weight, first, second, average = (states[4 * k + q][...] for q in range(4))
        clipped = g * factor
        first = 0.9 * first + 0.1 * clipped
        second = 0.999 * second + 0.001 * clipped * clipped
        first_hat = first / (1.0 - 0.9**STEP)
        second_hat = second / (1.0 - 0.999**STEP)
        weight = weight - learn_rate * (first_hat / (jnp.sqrt(second_hat) + 1e-08) + weight_decay * weight)
        average = ema_keep * average + (1.0 - ema_keep) * weight
        for q, v in enumerate((first, second, weight, average)):
            outs[4 * k + q][...] = v

    ada, wide, small, small_t, out = grads
    update(0, ada[...])
    update(1, wide[...].astype(F32))
    update(5, out[...].astype(F32))

    @pl.when(pl.program_id(0) == 0)
    def _():
        update(2, small[...])
        update(3, small_t[:R, :])
        update(4, small_t[R:CH + R, :])


def update_all(factor, ada, wide, small, small_t, out, states):
    part = 256
    right = lambda v: pl.BlockSpec((v.shape[0], part), lambda t: (0, t))
    kinds = [right, right, fixed, fixed, fixed, right]
    specs = [kind(v) for kind, group in zip(kinds, states) for v in group]
    flat = [v for group in states for v in group]
    return pl.pallas_call(
        update_body,
        grid=(D // part,),
        in_specs=[pl.BlockSpec(memory_space=pltpu.SMEM), right(ada), right(wide), fixed(small), fixed(small_t), right(out)]
        + specs,
        out_specs=specs,
        out_shape=[shape(*v.shape) for v in flat],
        compiler_params=PARAMS,
        cost_estimate=cost(11),
        name="update",
    )(factor.reshape(1, 1), ada, wide, small, small_t, out, *flat)


def embed_time(steps):
    half = D // 2
    freqs = jnp.exp(-math.log(10000.0) * jnp.arange(half, dtype=F32) / half)
    angles = steps.astype(F32)[:, None] * freqs[None, :]
    return jax.nn.silu(jnp.concatenate([jnp.cos(angles), jnp.sin(angles)], axis=1))


def normalize(x):
    mean = jnp.mean(x, axis=2, keepdims=True)
    centered = x - mean
    var = jnp.mean(centered * centered, axis=2, keepdims=True)
    scale = lax.rsqrt(var + 1e-06)
    return centered * scale, scale


def group_bits(size):
    return [1 << k for k in reversed(range(size.bit_length() - 1))]


def moved(v, axes, pairs):
    return lax.ppermute(with_layout_constraint(v, Layout(tuple(range(v.ndim)))), axes, pairs)


def swap(v, bit, size):
    return moved(v, "fsdp", [(i, i ^ bit) for i in range(size)])


def tick(v, size):
    return swap(v[:16, :LANE], 1, size)


def group_gather(v, size):
    blocks = [v]
    for bit in group_bits(size):
        blocks += [swap(b, bit, size) for b in blocks]
    return blocks


def group_sum(v, size):
    bits = group_bits(size)
    half = v.shape[0] // 2
    other = swap(v[half:], bits[-1], size)
    total = v[:half] + other
    for k, bit in enumerate(bits[:-1]):
        other = swap(total, bit, size)
        rows = other.shape[0] // (size // 2)
        total = total + jnp.concatenate(
            [other[(p ^ (1 << k)) * rows : ((p ^ (1 << k)) + 1) * rows] for p in range(size // 2)], axis=0
        )
    return jnp.concatenate([total, swap(total, bits[-1], size)], axis=0), other


def ring_order(size):
    if size == 8:
        return [0, 2, 4, 6, 7, 5, 3, 1]
    return list(range(size))


def ring_move(v, way, size):
    order = ring_order(size)
    return moved(v, "dp", [(order[p], order[(p + way) % size]) for p in range(size)])


def ring_gather_steps(v, size, split):
    behind = ahead = v
    for _ in range(size // 2 - 1):
        behind, ahead = ring_move(behind, 1, size), ring_move(ahead, -1, size)
        yield [behind, ahead]
    cut = v.shape[0] // 2
    if split:
        yield [ring_move(behind[:cut], 1, size), ring_move(ahead[cut:], -1, size)]
    else:
        yield [ring_move(behind, 1, size)]


def ring_partial(blocks, step, came, after):
    size = len(blocks) - 1
    if step == 0:
        return blocks[-2:]
    away = size // 2 - step
    ahead, behind = blocks[2 * away], blocks[2 * away - 1]
    if all(v.shape[0] % 16 == 0 for v in came):
        return ring_add(ahead, behind, *came, after)
    add = lambda a, b: (a.astype(F32) + b.astype(F32)).astype(BF)
    up, down = came
    if step == 1:
        cut = up.shape[0]
        return [
            jnp.concatenate([add(ahead[:cut], up), ahead[cut:]], axis=0),
            jnp.concatenate([behind[:-cut], add(behind[-cut:], down)], axis=0),
        ]
    return [add(ahead, up), add(behind, down)]


def ring_send(partial):
    size = lax.axis_size("dp")
    return [ring_move(partial[0], 1, size), ring_move(partial[1], -1, size)]


def ring_last(blocks, came):
    return blocks[0].astype(F32) + came[0].astype(F32) + came[1].astype(F32)


def exchange(v):
    return lax.all_to_all(v, ALL, 0, 0, tiled=True)


def on_device(sizes, *args):
    (
        act, cotangent, item_counts, item_lengths, time_steps,
        ada_weight, ada_first, ada_second, ada_average,
        in_weight, in_first, in_second, in_average,
        x_weight, x_first, x_second, x_average,
        dt_weight, dt_first, dt_second, dt_average,
        chan_table, chan_first, chan_second, chan_average,
        out_weight, out_first, out_second, out_average,
    ) = args
    n_dp, n_fsdp = sizes
    devices = n_dp * n_fsdp
    count = item_lengths.shape[0]
    items = count * n_fsdp
    tokens = items * ITEM
    ada_cols = ada_weight.shape[1]
    f = lax.axis_index("fsdp")
    half = n_dp // 2
    low_half = lax.axis_index("dp") < half
    offsets = [0]
    for bit in group_bits(n_fsdp):
        offsets = offsets + [o ^ bit for o in offsets]

    forth = []
    for b in range(devices):
        i, j = divmod(b, 2)
        k, g = divmod(i, n_fsdp)
        forth.append((b, (k + half * j) * n_fsdp + g))
    back = [(t, s) for s, t in forth]
    across = [(q, (q + half) % n_dp) for q in range(n_dp)]
    wide = in_weight.astype(BF).T
    rows = wide.shape[0] // 2
    leaving = jnp.where(low_half, wide[rows:], wide[:rows])
    swapped = moved(leaving, "dp", across)
    small = jnp.concatenate([x_weight.astype(BF), dt_weight.astype(BF).T, chan_table.astype(BF).T], axis=1)
    small = jnp.pad(small, ((0, 0), (0, SMALL - small.shape[1])))
    small = moved(hold(small, leaving), ALL, forth)
    stream_own = jnp.concatenate([jnp.where(low_half, wide[:rows], swapped), small], axis=1)
    gate_own = jnp.where(low_half, swapped, wide[rows:])

    live_items = jnp.arange(count, dtype=jnp.int32) < item_counts[0]
    live_rows = jnp.arange(ITEM, dtype=jnp.int32)[None, :] < item_lengths[:, None]
    live = live_items[:, None] & live_rows
    dfinal_own = jnp.where(live[..., None], cotangent.reshape(count, ITEM, D), jnp.zeros((), BF))
    x_all = group_gather(act.reshape(count * ITEM, D), n_fsdp)

    steps_all = exchange(hold(jnp.broadcast_to(time_steps[None], (devices, count)), leaving)).reshape(-1)
    cond_all = embed_time(steps_all).astype(BF)
    mod_cols = product(cond_all, ada_weight.astype(BF)).reshape(n_dp, 1, items, ada_cols)
    mod_cols = jnp.broadcast_to(mod_cols, (n_dp, n_fsdp, items, ada_cols)).reshape(devices, items, ada_cols)
    mod = exchange(hold(mod_cols, tick(stream_own, n_fsdp)))
    dfinal_all = group_gather(hold(dfinal_own.reshape(count * ITEM, D), mod), n_fsdp)
    mod = jnp.swapaxes(mod, 0, 1).reshape(n_fsdp, count, 3 * D)
    mod = jnp.take(mod, jnp.array(offsets, jnp.int32) ^ f, axis=0).reshape(items, 3 * D)

    stream = [stream_own]
    for came in ring_gather_steps(stream_own, n_dp, False):
        stream += came
    out_own = moved(hold(out_weight.astype(BF), stream[half - 1]), ALL, forth)
    rest_own = hold(jnp.concatenate([gate_own, out_own], axis=1), tick(stream[-2], n_fsdp))
    rest_steps = list(ring_gather_steps(rest_own, n_dp, True))
    rest = [rest_own] + sum(rest_steps, [])

    h_low, xs, u, u_low, proj, stream_full, x_full, dt_full, table = mix(x_all, mod, stream, [rest_own, *dfinal_all])
    proj, _ = group_sum(hold(proj, *rest_steps[0]), n_fsdp)
    calls = 2
    part = items // calls
    kept = []
    for i in range(calls):
        kept = scan_forward(i * part, part, u, proj, dt_full, table, kept, rest_steps[half // 2 - 1 + i])
    y, states = kept

    dy, dz_low, o_own, o_far, gate_full, early = gates(h_low, dfinal_all, mod, y, rest)
    bits = group_bits(n_fsdp)[::-1]
    kept, drates, drows, came, o_came = [], [], [], None, None
    for i, (begin, some) in enumerate(((0, 1), (1, items - 2), (items - 1, 1))):
        partial = ring_partial(early, i, came, drates[-1:])
        came = ring_send(partial)
        *kept, drate, drow = scan_backward(
            begin, some, u, proj, dy, states, dt_full, table, kept, [*partial, *([] if i else [o_far])]
        )
        drates.append(drate)
        drows.append(drow)
        if i == 0:
            o_came = swap(o_far, bits[0], n_fsdp)
    beside, calls = came, len(drates)
    leaving = ring_partial(early, calls, came, drates[-1:])
    came = ring_send(leaving)
    du_scan, ddtp_low, dproj = kept

    dproj, other = group_sum(hold(dproj, *beside), n_fsdp)
    for bit in bits[1:]:
        o_own, o_far = fold(o_own, o_came, [other])
        o_came = swap(o_far, bit, n_fsdp)
    o_own = o_own.astype(F32) + o_came.astype(F32)

    def to_owners(early_sum):
        sums = early_sum[:, :D].astype(BF), early_sum[:, D:].astype(BF)
        return sums, (moved(sums[0], "dp", [(q, q + half) for q in range(half)]), moved(sums[1], ALL, back))

    if half == calls + 1:
        early_sum = ring_last(early, came)
        leaving, arrived = to_owners(early_sum)
    else:
        arrived = came
    dh, dh_far, late = mix_back(
        h_low, xs, du_scan, ddtp_low, u_low, proj, dproj, dz_low, x_full, table, stream_full, gate_full,
        drates, drows, ring_sizes(rows, n_dp), [o_far, *leaving]
    )
    dh_far, *late[-2:] = [hold(v, *arrived, o_came) for v in (dh_far, *late[-2:])]
    came, dh_came = None, None
    for i in range(half):
        if 0 < i < len(bits):
            dh, dh_far = fold(dh, dh_came, [])
        after = [dh_far] if i == 1 else [dh_came] if i == half - 1 else []
        came = ring_send(ring_partial(late, i, came, after))
        if i < len(bits):
            dh_came = swap(dh_far, bits[i], n_fsdp)
    dh = dh + dh_came.astype(F32)
    late_sum = ring_last(late, came)
    if half == calls + 1:
        (gate_sum, _), (gate_moved, out_share) = leaving, arrived
    else:
        came = arrived
        for i in range(calls + 1, half):
            came = ring_send(ring_partial(early, i, came, [late_sum]))
        early_sum = ring_last(early, came)
        (gate_sum, _), (gate_moved, out_share) = to_owners(early_sum)
    squares = jnp.sum(early_sum * early_sum) + jnp.sum(late_sum * late_sum)
    small = moved(late_sum[:, D:].astype(BF), ALL, back).astype(F32)
    small_t = small[:, LANE:].T
    late_sum = late_sum[:, :D].astype(BF)
    late_moved = moved(late_sum, "dp", [(q + half, q) for q in range(half)])
    in_share = jnp.concatenate(
        [jnp.where(low_half, late_sum, gate_moved), jnp.where(low_half, late_moved, gate_sum)], axis=0
    )
    dh, o_own = dh.reshape(count, ITEM, D), o_own.reshape(count, ITEM, D)

    x = act.astype(F32).reshape(count, ITEM, D)
    normed, inverse = normalize(x)
    dfinal = dfinal_own.astype(F32)
    scale, gate = mod[:count, None, D : 2 * D], mod[:count, None, 2 * D :]
    final = x + gate * o_own
    dmod = jnp.concatenate(
        [jnp.sum(dh, axis=1), jnp.sum(dh * normed, axis=1), jnp.sum(dfinal * o_own, axis=1)], axis=1
    ).astype(BF)
    dn = dh * (1.0 + scale)
    act_grad = dfinal + inverse * (
        dn - jnp.mean(dn, axis=2, keepdims=True) - normed * jnp.mean(dn * normed, axis=2, keepdims=True)
    )
    dmod = hold(dmod, late_sum)
    dmod_all = exchange(jnp.swapaxes(dmod.reshape(count, devices, ada_cols), 0, 1)).reshape(devices * count, ada_cols)
    ada_share = left_outer(dmod_all, cond_all)

    local = squares + jnp.sum(ada_share * ada_share)
    total = jnp.sum(exchange(jnp.broadcast_to(local, (devices, LANE)))[:, 0])
    grad_norm = jnp.sqrt(total)
    factor = jnp.minimum(1.0, 1.0 / (grad_norm + 1e-06))
    results = update_all(
        factor, ada_share, in_share, small[:, :LANE], small_t, out_share,
        (
            (ada_weight.T, ada_first.T, ada_second.T, ada_average.T),
            (in_weight.T, in_first.T, in_second.T, in_average.T),
            (x_weight, x_first, x_second, x_average),
            (dt_weight, dt_first, dt_second, dt_average),
            (chan_table, chan_first, chan_second, chan_average),
            (out_weight, out_first, out_second, out_average),
        ),
    )
    results = [v.T for v in results[:8]] + list(results[8:])
    return (final.reshape(count * ITEM, D), act_grad.reshape(count * ITEM, D), grad_norm, *results)


def solution(mesh):
    sizes = (mesh.shape["dp"], mesh.shape["fsdp"])
    first, second = P(ALL, None), P(None, ALL)
    weights = [second] * 8 + [first] * 4 + [second] * 8 + [first] * 4
    return jax.shard_map(
        lambda *args: on_device(sizes, *args),
        mesh=mesh,
        in_specs=(first, first, P(ALL), P(ALL), P(ALL), *weights),
        out_specs=(first, first, P(), *weights),
        check_vma=False,
    )
```

```python
import math

import jax
import jax.numpy as jnp
from jax import lax
from jax.experimental import pallas as pl
from jax.experimental.layout import Layout, with_layout_constraint
from jax.experimental.pallas import tpu as pltpu
from jax.sharding import PartitionSpec as P

D = 1536
E = 3072
N = 16
R = 96
CONV = 4
CH = 7 + N
ITEM = 256
STEP = 10
SUB = 8
LANE = 128
BIAS, STEP_BIAS, SKIP, RATE = CONV, CONV + 1, CONV + 2, CONV + 3
TABLE = 32
SMALL = 2 * LANE
ALL = ("dp", "fsdp")
LOG2E = math.log2(math.e)
LN2 = math.log(2.0)
F32 = jnp.float32
BF = jnp.bfloat16
VMEM_LIMIT = 60 * 1024 * 1024
SCAN_BLOCK = 64
PITCH = ITEM + SUB


def product(left, right):
    return jnp.dot(left, right, preferred_element_type=F32)


def left_outer(left, right):
    return lax.dot_general(left, right, (((0,), (0,)), ((), ())), preferred_element_type=F32)


def right_inner(left, right):
    return lax.dot_general(left, right, (((1,), (1,)), ((), ())), preferred_element_type=F32)


def softplus(v):
    return jnp.maximum(v, 0.0) + jnp.log1p(jnp.exp(-jnp.abs(v)))


def shape(rows, columns, dtype=F32):
    return jax.ShapeDtypeStruct((rows, columns), dtype)


def item_rows(v):
    return pl.BlockSpec((ITEM, v.shape[1]), lambda i: (i, 0))


def halves(tokens):
    last = tokens // ITEM // 2 - 1
    near = pl.BlockSpec((ITEM, D), lambda i: (jnp.minimum(i, last), 0))
    return near, pl.BlockSpec((ITEM, D), lambda i: (jnp.maximum(i - last - 1, 0), 0))


def fixed(v):
    return pl.BlockSpec(v.shape, lambda i: (0, 0))


def once(v):
    return pl.BlockSpec(v.shape, lambda i: (0, 0), pipeline_mode=pl.Buffered(1))


ANYWHERE = pl.BlockSpec(memory_space=pl.ANY)
PARAMS = pltpu.CompilerParams(vmem_limit_bytes=VMEM_LIMIT)


def cost(us):
    return pl.CostEstimate(flops=int(us * 1e9), bytes_accessed=int(us * 1e6), transcendentals=0)


def hold_body(v_ref, *refs):
    pass


def hold(v, *after):
    return pl.pallas_call(
        hold_body,
        in_specs=[ANYWHERE] * (1 + len(after)),
        out_specs=ANYWHERE,
        out_shape=jax.ShapeDtypeStruct(v.shape, v.dtype),
        input_output_aliases={0: 0},
        name="hold",
    )(v, *after)


def ring_sizes(rows, size):
    return [rows] * (size - 1) + [rows // 2] * 2


def joined(blocks):
    return blocks if all(b.shape[0] % 16 == 0 for b in blocks) else [jnp.concatenate(blocks, axis=0)]


def parted(blocks, sizes):
    if len(blocks) == len(sizes):
        return list(blocks)
    ends = [sum(sizes[: k + 1]) for k in range(len(sizes))]
    return [blocks[0][end - size : end] for end, size in zip(ends, sizes)]


def pick(refs, item, held):
    for p, ref in enumerate(refs):
        @pl.when(item == p)
        def _(ref=ref):
            held[...] = ref[...]


def fold_body(near_ref, came_ref, *refs):
    keep_ref, away_ref = refs[-2:]
    half = keep_ref.shape[0]
    keep_ref[...] = near_ref[:half, :].astype(F32) + came_ref[:half, :].astype(F32)
    away_ref[...] = (near_ref[half:, :].astype(F32) + came_ref[half:, :].astype(F32)).astype(BF)


def fold(near, came, after):
    half = near.shape[0] // 2
    whole = pl.BlockSpec(memory_space=pltpu.VMEM)
    return pl.pallas_call(
        fold_body,
        in_specs=[whole, whole] + [ANYWHERE] * len(after),
        out_specs=[whole, whole],
        out_shape=[shape(half, near.shape[1]), shape(half, near.shape[1], BF)],
        compiler_params=PARAMS,
        cost_estimate=cost(2),
        name="fold",
    )(near, came, *after)


def ring_add_body(ahead_ref, behind_ref, up_ref, down_ref, *refs):
    up, down = up_ref.shape[0], down_ref.shape[0]
    rows = ahead_ref.shape[0]
    to_ahead, to_behind = refs[-2:]
    to_ahead[:up, :] = (ahead_ref[:up, :].astype(F32) + up_ref[...].astype(F32)).astype(BF)
    to_behind[rows - down :, :] = (behind_ref[rows - down :, :].astype(F32) + down_ref[...].astype(F32)).astype(BF)
    if up < rows:
        to_ahead[up:, :] = ahead_ref[up:, :]
        to_behind[: rows - down, :] = behind_ref[: rows - down, :]


def ring_add(ahead, behind, up, down, after):
    whole = pl.BlockSpec(memory_space=pltpu.VMEM)
    return pl.pallas_call(
        ring_add_body,
        in_specs=[whole] * 4 + [ANYWHERE] * len(after),
        out_specs=[whole, whole],
        out_shape=[shape(*ahead.shape, BF)] * 2,
        compiler_params=PARAMS,
        cost_estimate=cost(2),
        name="ring_add",
    )(ahead, behind, up, down, *after)


def delayed(v, k):
    if k == 0:
        return v
    row = lax.broadcasted_iota(jnp.int32, v.shape, 0)
    moved = pltpu.roll(v, k % v.shape[0], axis=0)
    return jnp.where(row >= k if k > 0 else row < v.shape[0] + k, moved, 0.0)


def convolved(xs, table):
    pre = table[BIAS : BIAS + 1, :]
    for k in range(CONV):
        pre = pre + delayed(xs, CONV - 1 - k) * table[k : k + 1, :]
    return pre


def mix_body(items, count, mod_ref, *refs):
    pieces, blocks = refs[:items], refs[items : items + count]
    h_ref, xs_ref, u_ref, low_ref, proj_ref, stream_ref, x_ref, dt_ref, table_ref, tail, held = refs[-11:]

    @pl.when(pl.program_id(0) == 0)
    def _():
        at = 0
        for block in blocks:
            rows = slice(at, at + block.shape[0])
            stream_ref[rows, :] = block[:, :D]
            x_ref[rows, :] = block[:, D : D + LANE]
            tail[rows, :] = block[:, D + LANE :].astype(F32)
            at += block.shape[0]
        lane = lax.broadcasted_iota(jnp.int32, tail.shape, 1)
        dt_ref[...] = jnp.where(lane < R, tail[...], 0.0).astype(BF)
        table_ref[...] = tail[...].T[R:, :]

    pick(pieces, pl.program_id(0), held)
    x = held[...].astype(F32)
    centered = x - jnp.mean(x, axis=1, keepdims=True)
    normed = centered * lax.rsqrt(jnp.mean(centered * centered, axis=1, keepdims=True) + 1e-06)
    mod = mod_ref[pl.ds(pl.program_id(0), 1), :]
    h = (normed * (1.0 + mod[:, D : 2 * D]) + mod[:, :D]).astype(BF)
    h_ref[...] = h
    xs = right_inner(h, stream_ref[...])
    xs_ref[...] = xs
    pre = convolved(xs, table_ref)
    u = pre * jax.nn.sigmoid(pre)
    u_ref[...] = u
    low = u.astype(BF)
    low_ref[...] = low
    proj_ref[...] = product(low, x_ref[...])


def mix(pieces, mod, blocks, after):
    items = len(pieces)
    tokens = items * ITEM
    blocks = joined(blocks)
    width = sum(b.shape[0] for b in blocks)
    out_shape = [
        shape(tokens, D, BF), shape(tokens, width), shape(tokens, width), shape(tokens, width, BF), shape(tokens, LANE),
        shape(width, D, BF), shape(width, LANE, BF), shape(width, LANE, BF), shape(TABLE, width),
    ]
    return pl.pallas_call(
        lambda *refs: mix_body(items, len(blocks), *refs),
        grid=(items,),
        in_specs=[fixed(mod)] + [once(v) for v in (*pieces, *blocks)] + [ANYWHERE] * len(after),
        out_specs=[item_rows(v) for v in out_shape[:5]] + [fixed(v) for v in out_shape[5:]],
        out_shape=out_shape,
        scratch_shapes=[pltpu.VMEM((width, LANE), F32), pltpu.VMEM((ITEM, D), BF)],
        compiler_params=PARAMS,
        cost_estimate=cost(11),
        name="mix",
    )(mod, *pieces, *blocks, *after)


def gates_body(items, count, h_ref, mod_ref, y_ref, *refs):
    here = pl.ds(pl.multiple_of(pl.program_id(0) * ITEM, ITEM), ITEM)
    pieces, blocks = refs[:items], refs[items : items + count]
    dy_ref, dz_ref, near_ref, far_ref, gate_ref, *grads = refs[items + count : -4]
    out_w, all_dz, all_mixed, all_do = refs[-4:]
    item = pl.program_id(0)

    @pl.when(pl.program_id(0) == 0)
    def _():
        at = 0
        for block in blocks:
            rows = slice(at, at + block.shape[0])
            gate_ref[rows, :] = block[:, :D]
            out_w[rows, :] = block[:, D:]
            at += block.shape[0]

    pick(pieces, item, all_do.at[here])
    h, y = h_ref[here, :], y_ref[...]
    do = (mod_ref[pl.ds(item, 1), 2 * D :] * all_do[here, :].astype(F32)).astype(BF)
    all_do[here, :] = do
    z = right_inner(h, gate_ref[...])
    dyg = right_inner(do, out_w[...])
    sig = jax.nn.sigmoid(z)
    act = z * sig
    dy_ref[...] = dyg * act
    mixed = (y * act).astype(BF)
    dz = (dyg * y * (sig + act * (1.0 - sig))).astype(BF)
    dz_ref[...] = dz
    all_dz[here, :] = dz
    all_mixed[here, :] = mixed
    o = product(mixed, out_w[...]).astype(BF)
    in_near = item < pl.num_programs(0) // 2

    @pl.when(in_near)
    def _():
        near_ref[...] = o

    @pl.when(jnp.logical_not(in_near))
    def _():
        far_ref[...] = o

    @pl.when(pl.program_id(0) == pl.num_programs(0) - 1)
    def _():
        for lanes, left, right in ((slice(D), all_dz, h_ref), (slice(D, 2 * D), all_mixed, all_do)):
            total = left_outer(left[...], right[...]).astype(BF)
            at = 0
            for grad in grads:
                grad[:, lanes] = total[at : at + grad.shape[0], :]
                at += grad.shape[0]


def gates(h, pieces, mod, y, blocks):
    tokens, width = y.shape
    sizes = [b.shape[0] for b in blocks]
    items = len(pieces)
    blocks = joined(blocks)
    out_shape = [
        shape(tokens, width), shape(tokens, width, BF), shape(tokens // 2, D, BF), shape(tokens // 2, D, BF), shape(width, D, BF)
    ]
    near, far = halves(tokens)
    grads = [shape(*b.shape, BF) for b in blocks]
    dy, dz, o_near, o_far, gate_full, *grads = pl.pallas_call(
        lambda *refs: gates_body(items, len(blocks), *refs),
        grid=(tokens // ITEM,),
        in_specs=[once(h), fixed(mod), item_rows(y)] + [once(b) for b in (*pieces, *blocks)],
        out_specs=[item_rows(v) for v in out_shape[:2]] + [near, far, fixed(out_shape[4])] + [fixed(v) for v in grads],
        out_shape=out_shape + grads,
        scratch_shapes=[
            pltpu.VMEM((width, D), BF), pltpu.VMEM((tokens, width), BF), pltpu.VMEM((tokens, width), BF),
            pltpu.VMEM((tokens, D), BF),
        ],
        compiler_params=PARAMS,
        cost_estimate=cost(24),
        name="gates",
    )(h, mod, y, *pieces, *blocks)
    return dy, dz, o_near, o_far, gate_full, parted(grads, sizes)


def mix_back_body(
    calls, count, h_ref, xs_ref, du_ref, ddtp_ref, low_ref, proj_ref, dproj_ref, dz_ref,
    x_ref, table_ref, stream_ref, gate_ref, *refs
):
    drates, drows = refs[:calls], refs[calls : 2 * calls]
    near_ref, far_ref, *grads = refs[-6 - count : -4]
    item = pl.program_id(0)
    grad_stream, grad_x, grad_tail, rows = refs[-4:]

    @pl.when(pl.program_id(0) == 0)
    def _():
        grad_stream[...] = jnp.zeros_like(grad_stream)
        grad_x[...] = jnp.zeros_like(grad_x)
        grad_tail[...] = jnp.zeros_like(grad_tail)
        rows[...] = jnp.zeros_like(rows)

    dproj = dproj_ref[...].astype(BF)
    xs = xs_ref[...]
    pre = convolved(xs, table_ref)
    sig = jax.nn.sigmoid(pre)
    dpre = (du_ref[...] + right_inner(dproj, x_ref[...])) * (sig + pre * sig * (1.0 - sig))
    dxs = jnp.zeros_like(dpre)
    for k in range(CONV):
        back = CONV - 1 - k
        dxs = dxs + delayed(dpre, -back) * table_ref[k : k + 1, :]
        rows[R + k : R + k + 1, :] += jnp.sum(dpre * delayed(xs, back), axis=0, keepdims=True)
    rows[R + BIAS : R + BIAS + 1, :] += jnp.sum(dpre, axis=0, keepdims=True)
    low = dxs.astype(BF)
    dh = product(low, stream_ref[...]) + product(dz_ref[...], gate_ref[...])
    in_near = item < pl.num_programs(0) // 2

    @pl.when(in_near)
    def _():
        near_ref[...] = dh

    @pl.when(jnp.logical_not(in_near))
    def _():
        far_ref[...] = dh.astype(BF)

    grad_stream[...] += left_outer(low, h_ref[...])
    grad_x[...] += left_outer(low_ref[...], dproj)
    lane = lax.broadcasted_iota(jnp.int32, dproj.shape, 1)
    rank = jnp.where(lane < R, proj_ref[...], 0.0).astype(BF)
    grad_tail[...] += left_outer(ddtp_ref[...], rank)

    @pl.when(pl.program_id(0) == pl.num_programs(0) - 1)
    def _():
        drow = sum(r[...] for r in drows)
        rows[R + STEP_BIAS : R + STEP_BIAS + 1, :] = jnp.sum(drow[:SUB], axis=0, keepdims=True)
        rows[R + SKIP : R + SKIP + 1, :] = jnp.sum(drow[SUB:], axis=0, keepdims=True)
        rows[R + RATE : R + CH, :] = sum(r[...] for r in drates) * -jnp.exp(table_ref[RATE:CH, :])
        grad_tail[...] += rows[...].T
        at = 0
        for grad in grads:
            part = slice(at, at + grad.shape[0])
            grad[:, :D] = grad_stream[part, :].astype(BF)
            grad[:, D : D + LANE] = grad_x[part, :].astype(BF)
            grad[:, D + LANE :] = grad_tail[part, :].astype(BF)
            at += grad.shape[0]


def mix_back(h, xs, du, ddtp, low, proj, dproj, dz, x_full, table, stream, gate, drates, drows, sizes, after):
    tokens, width = xs.shape
    aligned = all(size % 16 == 0 for size in sizes)
    blocks = [shape(size, D + SMALL, BF) for size in (sizes if aligned else [width])]
    near, far = halves(tokens)
    calls = len(drates)
    dh_near, dh_far, *grads = pl.pallas_call(
        lambda *refs: mix_back_body(calls, len(blocks), *refs),
        grid=(tokens // ITEM,),
        in_specs=[item_rows(v) for v in (h, xs, du, ddtp, low, proj, dproj, dz)]
        + [once(v) for v in (x_full, table, stream, gate, *drates, *drows)]
        + [ANYWHERE] * len(after),
        out_specs=[near, far] + [fixed(v) for v in blocks],
        out_shape=[shape(tokens // 2, D), shape(tokens // 2, D, BF)] + blocks,
        scratch_shapes=[
            pltpu.VMEM((width, D), F32), pltpu.VMEM((width, LANE), F32), pltpu.VMEM((width, LANE), F32),
            pltpu.VMEM((LANE, width), F32),
        ],
        compiler_params=PARAMS,
        cost_estimate=cost(19),
        name="mix_back",
    )(h, xs, du, ddtp, low, proj, dproj, dz, x_full, table, stream, gate, *drates, *drows, *after)
    return dh_near, dh_far, parted(grads, sizes)


def scan_prepare(u_ref, proj_ref, dt_ref, table_ref, pre, step, drive, rate, bc):
    pre[...] = right_inner(proj_ref[...].astype(BF), dt_ref[...]) + table_ref[STEP_BIAS : STEP_BIAS + 1, :]
    step[...] = softplus(pre[...])
    drive[...] = step[...] * u_ref[...]
    rate[...] = -jnp.exp(table_ref[RATE:CH, :]) * LOG2E
    turned = proj_ref[...].T
    for g in range(bc.shape[0]):
        bc[g, :, :SUB] = turned[R:, g * SUB : (g + 1) * SUB]


def scan_forward_body(u_ref, proj_ref, dt_ref, table_ref, *refs):
    y_ref, states_ref, pre, step_ref, drive_ref, rate_ref, bc_ref, carry, parts = refs[-9:]
    groups = u_ref.shape[0] // SUB
    chunks = u_ref.shape[1] // LANE

    @pl.when(pl.program_id(1) == 0)
    def _():
        carry[...] = jnp.zeros_like(carry)

    scan_prepare(u_ref, proj_ref, dt_ref, table_ref, pre, step_ref, drive_ref, rate_ref, bc_ref)

    def group(g, _):
        base = pl.multiple_of(g * SUB, SUB)
        step8 = step_ref[pl.ds(base, SUB), :]
        drive8 = drive_ref[pl.ds(base, SUB), :]
        bc = bc_ref[g]
        states = [carry[:, c * LANE : (c + 1) * LANE] for c in range(chunks)]
        for j in range(SUB):
            b = jnp.broadcast_to(bc[:N, j : j + 1], (N, LANE))
            cc = jnp.broadcast_to(bc[N:, j : j + 1], (N, LANE))
            at = pl.multiple_of((base + j) * N, N)
            for c in range(chunks):
                lanes = slice(c * LANE, (c + 1) * LANE)
                step = jnp.broadcast_to(step8[j : j + 1, lanes], (N, LANE))
                drive = jnp.broadcast_to(drive8[j : j + 1, lanes], (N, LANE))
                s = jnp.exp2(step * rate_ref[:, lanes]) * states[c] + b * drive
                states[c] = s
                states_ref[pl.ds(at, N), lanes] = s
                p = cc * s
                parts[c, pl.ds(pl.multiple_of((base + j) * SUB, SUB), SUB), :] = p[:SUB] + p[SUB:]
        for c in range(chunks):
            lanes = slice(c * LANE, (c + 1) * LANE)
            carry[:, lanes] = states[c]
        return 0

    lax.fori_loop(0, groups, group, 0)
    for c in range(chunks):
        lanes = slice(c * LANE, (c + 1) * LANE)
        total = table_ref[SKIP : SKIP + 1, lanes] * u_ref[:, lanes]
        for n in range(SUB):
            total = total + parts[c, pl.ds(n, groups * SUB, stride=SUB), :]
        y_ref[:, lanes] = total


def scan_forward(begin, count, u, proj, dt, table, kept, after):
    total, width = u.shape
    block = SCAN_BLOCK
    steps = ITEM // block
    chunks = width // LANE
    at = lambda i, t: ((begin + i) * steps + t, 0)
    tok = pl.BlockSpec((block, width), at)
    whole = lambda v: pl.BlockSpec(v.shape, lambda i, t: (0, 0))
    extra = list(kept) + list(after)
    return pl.pallas_call(
        scan_forward_body,
        grid=(count, steps),
        in_specs=[tok, pl.BlockSpec((block, LANE), at), whole(dt), whole(table)] + [ANYWHERE] * len(extra),
        out_specs=[tok, pl.BlockSpec((block * N, width), at)],
        out_shape=[shape(total, width), shape(total * N, width)],
        scratch_shapes=[
            *[pltpu.VMEM((block, width), F32)] * 3, pltpu.VMEM((N, width), F32),
            pltpu.VMEM((block // SUB, 2 * N, LANE), F32),
            pltpu.VMEM((N, width), F32), pltpu.VMEM((chunks, block * SUB, LANE), F32),
        ],
        input_output_aliases={4 + k: k for k in range(len(kept))},
        compiler_params=PARAMS,
        cost_estimate=cost(8 * count),
        name="scan_forward",
    )(u, proj, dt, table, *extra)


def scan_backward_body(u_ref, proj_ref, dy_ref, states_ref, before_ref, dt_ref, table_ref, *refs):
    du_ref, ddtp_ref, dproj_ref, drate_ref, drow_ref = refs[-16:-11]
    pre, step_ref, drive_ref, rate_ref, bc_ref, carry, parts, parts2, sums, stage, own = refs[-11:]
    block = u_ref.shape[0]
    groups = block // SUB
    chunks = u_ref.shape[1] // LANE
    back = pl.num_programs(1) - 1 - pl.program_id(1)
    first = back == 0

    @pl.when(pl.program_id(1) == 0)
    def _():
        carry[...] = jnp.zeros_like(carry)

    @pl.when((pl.program_id(0) == 0) & (pl.program_id(1) == 0))
    def _():
        drate_ref[...] = jnp.zeros_like(drate_ref)
        drow_ref[...] = jnp.zeros_like(drow_ref)

    scan_prepare(u_ref, proj_ref, dt_ref, table_ref, pre, step_ref, drive_ref, rate_ref, bc_ref)

    def group(k, _):
        g = groups - 1 - k
        base = pl.multiple_of(g * SUB, SUB)
        step8 = step_ref[pl.ds(base, SUB), :]
        drive8 = drive_ref[pl.ds(base, SUB), :]
        dy8 = dy_ref[pl.ds(base, SUB), :]
        bc = bc_ref[g]
        grads = [carry[:, c * LANE : (c + 1) * LANE] for c in range(chunks)]
        drate = [drate_ref[:, c * LANE : (c + 1) * LANE] for c in range(chunks)]
        for j in reversed(range(SUB)):
            b = jnp.broadcast_to(bc[:N, j : j + 1], (N, LANE))
            cc = jnp.broadcast_to(bc[N:, j : j + 1], (N, LANE))
            at = pl.multiple_of((base + j) * N, N)
            db = jnp.zeros((N, LANE), F32)
            dc = jnp.zeros((N, LANE), F32)
            for c in range(chunks):
                lanes = slice(c * LANE, (c + 1) * LANE)
                step = jnp.broadcast_to(step8[j : j + 1, lanes], (N, LANE))
                drive = jnp.broadcast_to(drive8[j : j + 1, lanes], (N, LANE))
                dy = jnp.broadcast_to(dy8[j : j + 1, lanes], (N, LANE))
                now = states_ref[pl.ds(at, N), lanes]
                if j > 0:
                    prev = states_ref[pl.ds(at - N, N), lanes]
                else:
                    prev = states_ref[pl.ds(pl.multiple_of(jnp.maximum(at - N, 0), N), N), lanes]
                    edge = jnp.where(first, 0.0, before_ref[:, lanes])
                    prev = jnp.where(g == 0, edge, prev)
                rate = rate_ref[:, lanes]
                grad = cc * dy + grads[c]
                dc = dc + now * dy
                db = db + grad * drive
                p = grad * b
                parts[c, pl.ds(pl.multiple_of((base + j) * SUB, SUB), SUB), :] = p[:SUB] + p[SUB:]
                grad = grad * jnp.exp2(step * rate)
                grads[c] = grad
                q = grad * prev
                p = q * rate
                parts2[c, pl.ds(pl.multiple_of((base + j) * SUB, SUB), SUB), :] = p[:SUB] + p[SUB:]
                drate[c] = drate[c] + q * step
            token = back * block + base + j
            sums[pl.ds(token, N, stride=PITCH), :] = db
            sums[pl.ds(N * PITCH + token, N, stride=PITCH), :] = dc
        for c in range(chunks):
            lanes = slice(c * LANE, (c + 1) * LANE)
            carry[:, lanes] = grads[c]
            drate_ref[:, lanes] = drate[c]
        return 0

    lax.fori_loop(0, groups, group, 0)
    for c in range(chunks):
        lanes = slice(c * LANE, (c + 1) * LANE)
        x = parts[c, pl.ds(0, block, stride=SUB), :]
        r = parts2[c, pl.ds(0, block, stride=SUB), :]
        for n in range(1, SUB):
            x = x + parts[c, pl.ds(n, block, stride=SUB), :]
            r = r + parts2[c, pl.ds(n, block, stride=SUB), :]
        dy, u, step = dy_ref[:, lanes], u_ref[:, lanes], step_ref[:, lanes]
        du_ref[:, lanes] = step * x + table_ref[SKIP : SKIP + 1, lanes] * dy
        d = (u * x + LN2 * r) * jax.nn.sigmoid(pre[:, lanes])
        ddtp_ref[:, lanes] = d.astype(BF)
        drow_ref[:SUB, lanes] += jnp.sum(d.reshape(groups, SUB, LANE), axis=0)
        drow_ref[SUB:, lanes] += jnp.sum((dy * u).reshape(groups, SUB, LANE), axis=0)
    low = ddtp_ref[...]
    own[pl.ds(pl.multiple_of(back * block, block), block), :] = product(low, dt_ref[...])

    @pl.when(first)
    def _():
        stage[...] = jnp.zeros_like(stage)
        ones = jnp.ones((SUB, LANE), BF)
        for n in range(2 * N):
            wide = sums[n * PITCH : n * PITCH + ITEM, :]
            high = wide.astype(BF)
            row = right_inner(ones, high) + right_inner(ones, (wide - high.astype(F32)).astype(BF))
            stage[R + n : R + n + 1, :] = row[:1]
        dproj_ref[...] = own[...] + stage[...].T


def scan_backward(begin, count, u, proj, dy, states, dt, table, kept, after):
    total, width = u.shape
    block = SCAN_BLOCK
    steps = ITEM // block
    chunks = width // LANE
    place = lambda i, t: (begin + i) * steps + steps - 1 - t
    at = lambda i, t: (place(i, t), 0)
    tok = pl.BlockSpec((block, width), at)
    whole = lambda v: pl.BlockSpec(v.shape, lambda i, t: (0, 0))
    extra = list(kept) + list(after)
    out_shape = [
        shape(total, width), shape(total, width, BF), shape(total, LANE), shape(N, width), shape(2 * SUB, width)
    ]
    return pl.pallas_call(
        scan_backward_body,
        grid=(count, steps),
        in_specs=[
            tok, pl.BlockSpec((block, LANE), at), tok,
            pl.BlockSpec((block * N, width), at),
            pl.BlockSpec((N, width), lambda i, t: (jnp.maximum(place(i, t) * block - 1, 0), 0)),
            whole(dt), whole(table),
        ]
        + [ANYWHERE] * len(extra),
        out_specs=[tok, tok, pl.BlockSpec((ITEM, LANE), lambda i, t: (begin + i, 0)), whole(out_shape[3]), whole(out_shape[4])],
        out_shape=out_shape,
        scratch_shapes=[
            *[pltpu.VMEM((block, width), F32)] * 3, pltpu.VMEM((N, width), F32),
            pltpu.VMEM((block // SUB, 2 * N, LANE), F32), pltpu.VMEM((N, width), F32),
            *[pltpu.VMEM((chunks, block * SUB, LANE), F32)] * 2,
            pltpu.VMEM((2 * N * PITCH, LANE), F32), pltpu.VMEM((LANE, ITEM), F32), pltpu.VMEM((ITEM, LANE), F32),
        ],
        input_output_aliases={7 + k: k for k in range(len(kept))},
        compiler_params=PARAMS,
        cost_estimate=cost(15 * count),
        name="scan_backward",
    )(u, proj, dy, states, states, dt, table, *extra)


def update_body(factor_ref, *refs):
    grads, states, outs = refs[:5], refs[5:29], refs[29:]
    factor = factor_ref[0, 0]
    ema_keep = min(0.9999, (1.0 + STEP) / (10.0 + STEP))

    def update(k, g):
        learn_rate, weight_decay = (0.5, 0.0) if k == 4 else (0.03, 0.1)
        weight, first, second, average = (states[4 * k + q][...] for q in range(4))
        clipped = g * factor
        first = 0.9 * first + 0.1 * clipped
        second = 0.999 * second + 0.001 * clipped * clipped
        first_hat = first / (1.0 - 0.9**STEP)
        second_hat = second / (1.0 - 0.999**STEP)
        weight = weight - learn_rate * (first_hat / (jnp.sqrt(second_hat) + 1e-08) + weight_decay * weight)
        average = ema_keep * average + (1.0 - ema_keep) * weight
        for q, v in enumerate((first, second, weight, average)):
            outs[4 * k + q][...] = v

    ada, wide, small, small_t, out = grads
    update(0, ada[...])
    update(1, wide[...].astype(F32))
    update(5, out[...].astype(F32))

    @pl.when(pl.program_id(0) == 0)
    def _():
        update(2, small[...])
        update(3, small_t[:R, :])
        update(4, small_t[R:CH + R, :])


def update_all(factor, ada, wide, small, small_t, out, states):
    part = 256
    right = lambda v: pl.BlockSpec((v.shape[0], part), lambda t: (0, t))
    kinds = [right, right, fixed, fixed, fixed, right]
    specs = [kind(v) for kind, group in zip(kinds, states) for v in group]
    flat = [v for group in states for v in group]
    return pl.pallas_call(
        update_body,
        grid=(D // part,),
        in_specs=[pl.BlockSpec(memory_space=pltpu.SMEM), right(ada), right(wide), fixed(small), fixed(small_t), right(out)]
        + specs,
        out_specs=specs,
        out_shape=[shape(*v.shape) for v in flat],
        compiler_params=PARAMS,
        cost_estimate=cost(11),
        name="update",
    )(factor.reshape(1, 1), ada, wide, small, small_t, out, *flat)


def embed_time(steps):
    half = D // 2
    freqs = jnp.exp(-math.log(10000.0) * jnp.arange(half, dtype=F32) / half)
    angles = steps.astype(F32)[:, None] * freqs[None, :]
    return jax.nn.silu(jnp.concatenate([jnp.cos(angles), jnp.sin(angles)], axis=1))


def normalize(x):
    mean = jnp.mean(x, axis=2, keepdims=True)
    centered = x - mean
    var = jnp.mean(centered * centered, axis=2, keepdims=True)
    scale = lax.rsqrt(var + 1e-06)
    return centered * scale, scale


def group_bits(size):
    return [1 << k for k in reversed(range(size.bit_length() - 1))]


def moved(v, axes, pairs):
    return lax.ppermute(with_layout_constraint(v, Layout(tuple(range(v.ndim)))), axes, pairs)


def swap(v, bit, size):
    return moved(v, "fsdp", [(i, i ^ bit) for i in range(size)])


def tick(v, size):
    return swap(v[:16, :LANE], 1, size)


def group_gather(v, size):
    blocks = [v]
    for bit in group_bits(size):
        blocks += [swap(b, bit, size) for b in blocks]
    return blocks


def group_sum(v, size):
    bits = group_bits(size)
    half = v.shape[0] // 2
    other = swap(v[half:], bits[-1], size)
    total = v[:half] + other
    for k, bit in enumerate(bits[:-1]):
        other = swap(total, bit, size)
        rows = other.shape[0] // (size // 2)
        total = total + jnp.concatenate(
            [other[(p ^ (1 << k)) * rows : ((p ^ (1 << k)) + 1) * rows] for p in range(size // 2)], axis=0
        )
    return jnp.concatenate([total, swap(total, bits[-1], size)], axis=0), other


def ring_order(size):
    if size == 8:
        return [0, 2, 4, 6, 7, 5, 3, 1]
    return list(range(size))


def ring_move(v, way, size):
    order = ring_order(size)
    return moved(v, "dp", [(order[p], order[(p + way) % size]) for p in range(size)])


def ring_gather_steps(v, size, split):
    behind = ahead = v
    for _ in range(size // 2 - 1):
        behind, ahead = ring_move(behind, 1, size), ring_move(ahead, -1, size)
        yield [behind, ahead]
    cut = v.shape[0] // 2
    if split:
        yield [ring_move(behind[:cut], 1, size), ring_move(ahead[cut:], -1, size)]
    else:
        yield [ring_move(behind, 1, size)]


def ring_partial(blocks, step, came, after):
    size = len(blocks) - 1
    if step == 0:
        return blocks[-2:]
    away = size // 2 - step
    ahead, behind = blocks[2 * away], blocks[2 * away - 1]
    if all(v.shape[0] % 16 == 0 for v in came):
        return ring_add(ahead, behind, *came, after)
    add = lambda a, b: (a.astype(F32) + b.astype(F32)).astype(BF)
    up, down = came
    if step == 1:
        cut = up.shape[0]
        return [
            jnp.concatenate([add(ahead[:cut], up), ahead[cut:]], axis=0),
            jnp.concatenate([behind[:-cut], add(behind[-cut:], down)], axis=0),
        ]
    return [add(ahead, up), add(behind, down)]


def ring_send(partial):
    size = lax.axis_size("dp")
    return [ring_move(partial[0], 1, size), ring_move(partial[1], -1, size)]


def ring_last(blocks, came):
    return blocks[0].astype(F32) + came[0].astype(F32) + came[1].astype(F32)


def exchange(v):
    return lax.all_to_all(v, ALL, 0, 0, tiled=True)


def on_device(sizes, *args):
    (
        act, cotangent, item_counts, item_lengths, time_steps,
        ada_weight, ada_first, ada_second, ada_average,
        in_weight, in_first, in_second, in_average,
        x_weight, x_first, x_second, x_average,
        dt_weight, dt_first, dt_second, dt_average,
        chan_table, chan_first, chan_second, chan_average,
        out_weight, out_first, out_second, out_average,
    ) = args
    n_dp, n_fsdp = sizes
    devices = n_dp * n_fsdp
    count = item_lengths.shape[0]
    items = count * n_fsdp
    tokens = items * ITEM
    ada_cols = ada_weight.shape[1]
    f = lax.axis_index("fsdp")
    half = n_dp // 2
    low_half = lax.axis_index("dp") < half
    offsets = [0]
    for bit in group_bits(n_fsdp):
        offsets = offsets + [o ^ bit for o in offsets]

    forth = []
    for b in range(devices):
        i, j = divmod(b, 2)
        k, g = divmod(i, n_fsdp)
        forth.append((b, (k + half * j) * n_fsdp + g))
    back = [(t, s) for s, t in forth]
    across = [(q, (q + half) % n_dp) for q in range(n_dp)]
    wide = in_weight.astype(BF).T
    rows = wide.shape[0] // 2
    leaving = jnp.where(low_half, wide[rows:], wide[:rows])
    swapped = moved(leaving, "dp", across)
    small = jnp.concatenate([x_weight.astype(BF), dt_weight.astype(BF).T, chan_table.astype(BF).T], axis=1)
    small = jnp.pad(small, ((0, 0), (0, SMALL - small.shape[1])))
    small = moved(hold(small, leaving), ALL, forth)
    stream_own = jnp.concatenate([jnp.where(low_half, wide[:rows], swapped), small], axis=1)
    gate_own = jnp.where(low_half, swapped, wide[rows:])

    live_items = jnp.arange(count, dtype=jnp.int32) < item_counts[0]
    live_rows = jnp.arange(ITEM, dtype=jnp.int32)[None, :] < item_lengths[:, None]
    live = live_items[:, None] & live_rows
    dfinal_own = jnp.where(live[..., None], cotangent.reshape(count, ITEM, D), jnp.zeros((), BF))
    x_all = group_gather(act.reshape(count * ITEM, D), n_fsdp)

    steps_all = exchange(hold(jnp.broadcast_to(time_steps[None], (devices, count)), leaving)).reshape(-1)
    cond_all = embed_time(steps_all).astype(BF)
    mod_cols = product(cond_all, ada_weight.astype(BF)).reshape(n_dp, 1, items, ada_cols)
    mod_cols = jnp.broadcast_to(mod_cols, (n_dp, n_fsdp, items, ada_cols)).reshape(devices, items, ada_cols)
    mod = exchange(hold(mod_cols, tick(stream_own, n_fsdp)))
    mod = jnp.swapaxes(mod, 0, 1).reshape(n_fsdp, count, 3 * D)
    mod = jnp.take(mod, jnp.array(offsets, jnp.int32) ^ f, axis=0).reshape(items, 3 * D)

    stream = [stream_own]
    for came in ring_gather_steps(stream_own, n_dp, False):
        stream += came
    dfinal_all = group_gather(hold(dfinal_own.reshape(count * ITEM, D), stream[2]), n_fsdp)
    out_own = moved(hold(out_weight.astype(BF), stream[half - 1]), ALL, forth)
    rest_own = hold(jnp.concatenate([gate_own, out_own], axis=1), tick(stream[-2], n_fsdp))
    rest_steps = list(ring_gather_steps(rest_own, n_dp, True))
    rest = [rest_own] + sum(rest_steps, [])

    h_low, xs, u, u_low, proj, stream_full, x_full, dt_full, table = mix(x_all, mod, stream, [rest_own, *dfinal_all])
    proj, _ = group_sum(hold(proj, *rest_steps[0]), n_fsdp)
    calls = 2
    part = items // calls
    kept = []
    for i in range(calls):
        kept = scan_forward(i * part, part, u, proj, dt_full, table, kept, rest_steps[half // 2 - 1 + i])
    y, states = kept

    dy, dz_low, o_own, o_far, gate_full, early = gates(h_low, dfinal_all, mod, y, rest)
    bits = group_bits(n_fsdp)[::-1]
    kept, drates, drows, came, o_came = [], [], [], None, None
    for i, (begin, some) in enumerate(((0, 1), (1, items - 2), (items - 1, 1))):
        partial = ring_partial(early, i, came, drates[-1:])
        came = ring_send(partial)
        *kept, drate, drow = scan_backward(
            begin, some, u, proj, dy, states, dt_full, table, kept, [*partial, *([] if i else [o_far])]
        )
        drates.append(drate)
        drows.append(drow)
        if i == 0:
            o_came = swap(o_far, bits[0], n_fsdp)
    beside, calls = came, len(drates)
    leaving = ring_partial(early, calls, came, drates[-1:])
    came = ring_send(leaving)
    du_scan, ddtp_low, dproj = kept

    dproj, other = group_sum(hold(dproj, *beside), n_fsdp)
    for bit in bits[1:]:
        o_own, o_far = fold(o_own, o_came, [other])
        o_came = swap(o_far, bit, n_fsdp)
    o_own = o_own.astype(F32) + o_came.astype(F32)

    def to_owners(early_sum):
        sums = early_sum[:, :D].astype(BF), early_sum[:, D:].astype(BF)
        return sums, (moved(sums[0], "dp", [(q, q + half) for q in range(half)]), moved(sums[1], ALL, back))

    if half == calls + 1:
        early_sum = ring_last(early, came)
        leaving, arrived = to_owners(early_sum)
    else:
        arrived = came
    dh, dh_far, late = mix_back(
        h_low, xs, du_scan, ddtp_low, u_low, proj, dproj, dz_low, x_full, table, stream_full, gate_full,
        drates, drows, ring_sizes(rows, n_dp), [o_far, *leaving]
    )
    dh_far, *late[-2:] = [hold(v, *arrived, o_came) for v in (dh_far, *late[-2:])]
    came, dh_came = None, None
    for i in range(half):
        if 0 < i < len(bits):
            dh, dh_far = fold(dh, dh_came, [])
        after = [dh_far] if i == 1 else [dh_came] if i == half - 1 else []
        came = ring_send(ring_partial(late, i, came, after))
        if i < len(bits):
            dh_came = swap(dh_far, bits[i], n_fsdp)
    dh = dh + dh_came.astype(F32)
    late_sum = ring_last(late, came)
    if half == calls + 1:
        (gate_sum, _), (gate_moved, out_share) = leaving, arrived
    else:
        came = arrived
        for i in range(calls + 1, half):
            came = ring_send(ring_partial(early, i, came, [late_sum]))
        early_sum = ring_last(early, came)
        (gate_sum, _), (gate_moved, out_share) = to_owners(early_sum)
    squares = jnp.sum(early_sum * early_sum) + jnp.sum(late_sum * late_sum)
    small = moved(late_sum[:, D:].astype(BF), ALL, back).astype(F32)
    small_t = small[:, LANE:].T
    late_sum = late_sum[:, :D].astype(BF)
    late_moved = moved(late_sum, "dp", [(q + half, q) for q in range(half)])
    in_share = jnp.concatenate(
        [jnp.where(low_half, late_sum, gate_moved), jnp.where(low_half, late_moved, gate_sum)], axis=0
    )
    dh, o_own = dh.reshape(count, ITEM, D), o_own.reshape(count, ITEM, D)

    x = act.astype(F32).reshape(count, ITEM, D)
    normed, inverse = normalize(x)
    dfinal = dfinal_own.astype(F32)
    scale, gate = mod[:count, None, D : 2 * D], mod[:count, None, 2 * D :]
    final = x + gate * o_own
    dmod = jnp.concatenate(
        [jnp.sum(dh, axis=1), jnp.sum(dh * normed, axis=1), jnp.sum(dfinal * o_own, axis=1)], axis=1
    ).astype(BF)
    dn = dh * (1.0 + scale)
    act_grad = dfinal + inverse * (
        dn - jnp.mean(dn, axis=2, keepdims=True) - normed * jnp.mean(dn * normed, axis=2, keepdims=True)
    )
    dmod = hold(dmod, late_sum)
    dmod_all = exchange(jnp.swapaxes(dmod.reshape(count, devices, ada_cols), 0, 1)).reshape(devices * count, ada_cols)
    ada_share = left_outer(dmod_all, cond_all)

    local = squares + jnp.sum(ada_share * ada_share)
    total = jnp.sum(exchange(jnp.broadcast_to(local, (devices, LANE)))[:, 0])
    grad_norm = jnp.sqrt(total)
    factor = jnp.minimum(1.0, 1.0 / (grad_norm + 1e-06))
    results = update_all(
        factor, ada_share, in_share, small[:, :LANE], small_t, out_share,
        (
            (ada_weight.T, ada_first.T, ada_second.T, ada_average.T),
            (in_weight.T, in_first.T, in_second.T, in_average.T),
            (x_weight, x_first, x_second, x_average),
            (dt_weight, dt_first, dt_second, dt_average),
            (chan_table, chan_first, chan_second, chan_average),
            (out_weight, out_first, out_second, out_average),
        ),
    )
    results = [v.T for v in results[:8]] + list(results[8:])
    return (final.reshape(count * ITEM, D), act_grad.reshape(count * ITEM, D), grad_norm, *results)


def solution(mesh):
    sizes = (mesh.shape["dp"], mesh.shape["fsdp"])
    first, second = P(ALL, None), P(None, ALL)
    weights = [second] * 8 + [first] * 4 + [second] * 8 + [first] * 4
    return jax.shard_map(
        lambda *args: on_device(sizes, *args),
        mesh=mesh,
        in_specs=(first, first, P(ALL), P(ALL), P(ALL), *weights),
        out_specs=(first, first, P(), *weights),
        check_vma=False,
    )
```

```python
import math

import jax
import jax.numpy as jnp
from jax import lax
from jax.experimental import pallas as pl
from jax.experimental.layout import Layout, with_layout_constraint
from jax.experimental.pallas import tpu as pltpu
from jax.sharding import PartitionSpec as P

D = 1536
E = 3072
N = 16
R = 96
CONV = 4
CH = 7 + N
ITEM = 256
STEP = 10
SUB = 8
LANE = 128
BIAS, STEP_BIAS, SKIP, RATE = CONV, CONV + 1, CONV + 2, CONV + 3
TABLE = 32
SMALL = 2 * LANE
ALL = ("dp", "fsdp")
LOG2E = math.log2(math.e)
LN2 = math.log(2.0)
F32 = jnp.float32
BF = jnp.bfloat16
VMEM_LIMIT = 60 * 1024 * 1024
SCAN_BLOCK = 64
PITCH = ITEM + SUB


def product(left, right):
    return jnp.dot(left, right, preferred_element_type=F32)


def left_outer(left, right):
    return lax.dot_general(left, right, (((0,), (0,)), ((), ())), preferred_element_type=F32)


def right_inner(left, right):
    return lax.dot_general(left, right, (((1,), (1,)), ((), ())), preferred_element_type=F32)


def softplus(v):
    return jnp.maximum(v, 0.0) + jnp.log1p(jnp.exp(-jnp.abs(v)))


def shape(rows, columns, dtype=F32):
    return jax.ShapeDtypeStruct((rows, columns), dtype)


def item_rows(v):
    return pl.BlockSpec((ITEM, v.shape[1]), lambda i: (i, 0))


def halves(tokens):
    last = tokens // ITEM // 2 - 1
    near = pl.BlockSpec((ITEM, D), lambda i: (jnp.minimum(i, last), 0))
    return near, pl.BlockSpec((ITEM, D), lambda i: (jnp.maximum(i - last - 1, 0), 0))


def fixed(v):
    return pl.BlockSpec(v.shape, lambda i: (0, 0))


def once(v):
    return pl.BlockSpec(v.shape, lambda i: (0, 0), pipeline_mode=pl.Buffered(1))


ANYWHERE = pl.BlockSpec(memory_space=pl.ANY)
PARAMS = pltpu.CompilerParams(vmem_limit_bytes=VMEM_LIMIT)


def cost(us):
    return pl.CostEstimate(flops=int(us * 1e9), bytes_accessed=int(us * 1e6), transcendentals=0)


def hold_body(v_ref, *refs):
    pass


def hold(v, *after):
    return pl.pallas_call(
        hold_body,
        in_specs=[ANYWHERE] * (1 + len(after)),
        out_specs=ANYWHERE,
        out_shape=jax.ShapeDtypeStruct(v.shape, v.dtype),
        input_output_aliases={0: 0},
        name="hold",
    )(v, *after)


def ring_sizes(rows, size):
    return [rows] * (size - 1) + [rows // 2] * 2


def joined(blocks):
    return blocks if all(b.shape[0] % 16 == 0 for b in blocks) else [jnp.concatenate(blocks, axis=0)]


def parted(blocks, sizes):
    if len(blocks) == len(sizes):
        return list(blocks)
    ends = [sum(sizes[: k + 1]) for k in range(len(sizes))]
    return [blocks[0][end - size : end] for end, size in zip(ends, sizes)]


def pick(refs, item, held):
    for p, ref in enumerate(refs):
        @pl.when(item == p)
        def _(ref=ref):
            held[...] = ref[...]


def fold_body(near_ref, came_ref, *refs):
    keep_ref, away_ref = refs[-2:]
    half = keep_ref.shape[0]
    keep_ref[...] = near_ref[:half, :].astype(F32) + came_ref[:half, :].astype(F32)
    away_ref[...] = (near_ref[half:, :].astype(F32) + came_ref[half:, :].astype(F32)).astype(BF)


def fold(near, came, after):
    half = near.shape[0] // 2
    whole = pl.BlockSpec(memory_space=pltpu.VMEM)
    return pl.pallas_call(
        fold_body,
        in_specs=[whole, whole] + [ANYWHERE] * len(after),
        out_specs=[whole, whole],
        out_shape=[shape(half, near.shape[1]), shape(half, near.shape[1], BF)],
        compiler_params=PARAMS,
        cost_estimate=cost(2),
        name="fold",
    )(near, came, *after)


def ring_add_body(ahead_ref, behind_ref, up_ref, down_ref, *refs):
    up, down = up_ref.shape[0], down_ref.shape[0]
    rows = ahead_ref.shape[0]
    to_ahead, to_behind = refs[-2:]
    to_ahead[:up, :] = (ahead_ref[:up, :].astype(F32) + up_ref[...].astype(F32)).astype(BF)
    to_behind[rows - down :, :] = (behind_ref[rows - down :, :].astype(F32) + down_ref[...].astype(F32)).astype(BF)
    if up < rows:
        to_ahead[up:, :] = ahead_ref[up:, :]
        to_behind[: rows - down, :] = behind_ref[: rows - down, :]


def ring_add(ahead, behind, up, down, after):
    whole = pl.BlockSpec(memory_space=pltpu.VMEM)
    return pl.pallas_call(
        ring_add_body,
        in_specs=[whole] * 4 + [ANYWHERE] * len(after),
        out_specs=[whole, whole],
        out_shape=[shape(*ahead.shape, BF)] * 2,
        compiler_params=PARAMS,
        cost_estimate=cost(2),
        name="ring_add",
    )(ahead, behind, up, down, *after)


def delayed(v, k):
    if k == 0:
        return v
    row = lax.broadcasted_iota(jnp.int32, v.shape, 0)
    moved = pltpu.roll(v, k % v.shape[0], axis=0)
    return jnp.where(row >= k if k > 0 else row < v.shape[0] + k, moved, 0.0)


def convolved(xs, table):
    pre = table[BIAS : BIAS + 1, :]
    for k in range(CONV):
        pre = pre + delayed(xs, CONV - 1 - k) * table[k : k + 1, :]
    return pre


def mix_body(items, count, mod_ref, *refs):
    pieces, blocks = refs[:items], refs[items : items + count]
    h_ref, xs_ref, u_ref, low_ref, proj_ref, stream_ref, x_ref, dt_ref, table_ref, tail, held = refs[-11:]

    @pl.when(pl.program_id(0) == 0)
    def _():
        at = 0
        for block in blocks:
            rows = slice(at, at + block.shape[0])
            stream_ref[rows, :] = block[:, :D]
            x_ref[rows, :] = block[:, D : D + LANE]
            tail[rows, :] = block[:, D + LANE :].astype(F32)
            at += block.shape[0]
        lane = lax.broadcasted_iota(jnp.int32, tail.shape, 1)
        dt_ref[...] = jnp.where(lane < R, tail[...], 0.0).astype(BF)
        table_ref[...] = tail[...].T[R:, :]

    pick(pieces, pl.program_id(0), held)
    x = held[...].astype(F32)
    centered = x - jnp.mean(x, axis=1, keepdims=True)
    normed = centered * lax.rsqrt(jnp.mean(centered * centered, axis=1, keepdims=True) + 1e-06)
    mod = mod_ref[pl.ds(pl.program_id(0), 1), :]
    h = (normed * (1.0 + mod[:, D : 2 * D]) + mod[:, :D]).astype(BF)
    h_ref[...] = h
    xs = right_inner(h, stream_ref[...])
    xs_ref[...] = xs
    pre = convolved(xs, table_ref)
    u = pre * jax.nn.sigmoid(pre)
    u_ref[...] = u
    low = u.astype(BF)
    low_ref[...] = low
    proj_ref[...] = product(low, x_ref[...])


def mix(pieces, mod, blocks, after):
    items = len(pieces)
    tokens = items * ITEM
    blocks = joined(blocks)
    width = sum(b.shape[0] for b in blocks)
    out_shape = [
        shape(tokens, D, BF), shape(tokens, width), shape(tokens, width), shape(tokens, width, BF), shape(tokens, LANE),
        shape(width, D, BF), shape(width, LANE, BF), shape(width, LANE, BF), shape(TABLE, width),
    ]
    return pl.pallas_call(
        lambda *refs: mix_body(items, len(blocks), *refs),
        grid=(items,),
        in_specs=[fixed(mod)] + [once(v) for v in (*pieces, *blocks)] + [ANYWHERE] * len(after),
        out_specs=[item_rows(v) for v in out_shape[:5]] + [fixed(v) for v in out_shape[5:]],
        out_shape=out_shape,
        scratch_shapes=[pltpu.VMEM((width, LANE), F32), pltpu.VMEM((ITEM, D), BF)],
        compiler_params=PARAMS,
        cost_estimate=cost(11),
        name="mix",
    )(mod, *pieces, *blocks, *after)


def gates_body(items, count, h_ref, mod_ref, y_ref, *refs):
    here = pl.ds(pl.multiple_of(pl.program_id(0) * ITEM, ITEM), ITEM)
    pieces, blocks = refs[:items], refs[items : items + count]
    dy_ref, dz_ref, near_ref, far_ref, gate_ref, *grads = refs[items + count : -4]
    out_w, all_dz, all_mixed, all_do = refs[-4:]
    item = pl.program_id(0)

    @pl.when(pl.program_id(0) == 0)
    def _():
        at = 0
        for block in blocks:
            rows = slice(at, at + block.shape[0])
            gate_ref[rows, :] = block[:, :D]
            out_w[rows, :] = block[:, D:]
            at += block.shape[0]

    pick(pieces, item, all_do.at[here])
    h, y = h_ref[here, :], y_ref[...]
    do = (mod_ref[pl.ds(item, 1), 2 * D :] * all_do[here, :].astype(F32)).astype(BF)
    all_do[here, :] = do
    z = right_inner(h, gate_ref[...])
    dyg = right_inner(do, out_w[...])
    sig = jax.nn.sigmoid(z)
    act = z * sig
    dy_ref[...] = dyg * act
    mixed = (y * act).astype(BF)
    dz = (dyg * y * (sig + act * (1.0 - sig))).astype(BF)
    dz_ref[...] = dz
    all_dz[here, :] = dz
    all_mixed[here, :] = mixed
    o = product(mixed, out_w[...]).astype(BF)
    in_near = item < pl.num_programs(0) // 2

    @pl.when(in_near)
    def _():
        near_ref[...] = o

    @pl.when(jnp.logical_not(in_near))
    def _():
        far_ref[...] = o

    @pl.when(pl.program_id(0) == pl.num_programs(0) - 1)
    def _():
        for lanes, left, right in ((slice(D), all_dz, h_ref), (slice(D, 2 * D), all_mixed, all_do)):
            total = left_outer(left[...], right[...]).astype(BF)
            at = 0
            for grad in grads:
                grad[:, lanes] = total[at : at + grad.shape[0], :]
                at += grad.shape[0]


def gates(h, pieces, mod, y, blocks):
    tokens, width = y.shape
    sizes = [b.shape[0] for b in blocks]
    items = len(pieces)
    blocks = joined(blocks)
    out_shape = [
        shape(tokens, width), shape(tokens, width, BF), shape(tokens // 2, D, BF), shape(tokens // 2, D, BF), shape(width, D, BF)
    ]
    near, far = halves(tokens)
    grads = [shape(*b.shape, BF) for b in blocks]
    dy, dz, o_near, o_far, gate_full, *grads = pl.pallas_call(
        lambda *refs: gates_body(items, len(blocks), *refs),
        grid=(tokens // ITEM,),
        in_specs=[once(h), fixed(mod), item_rows(y)] + [once(b) for b in (*pieces, *blocks)],
        out_specs=[item_rows(v) for v in out_shape[:2]] + [near, far, fixed(out_shape[4])] + [fixed(v) for v in grads],
        out_shape=out_shape + grads,
        scratch_shapes=[
            pltpu.VMEM((width, D), BF), pltpu.VMEM((tokens, width), BF), pltpu.VMEM((tokens, width), BF),
            pltpu.VMEM((tokens, D), BF),
        ],
        compiler_params=PARAMS,
        cost_estimate=cost(24),
        name="gates",
    )(h, mod, y, *pieces, *blocks)
    return dy, dz, o_near, o_far, gate_full, parted(grads, sizes)


def mix_back_body(
    calls, count, h_ref, xs_ref, du_ref, ddtp_ref, low_ref, proj_ref, dproj_ref, dz_ref,
    x_ref, table_ref, stream_ref, gate_ref, *refs
):
    drates, drows = refs[:calls], refs[calls : 2 * calls]
    near_ref, far_ref, *grads = refs[-6 - count : -4]
    item = pl.program_id(0)
    grad_stream, grad_x, grad_tail, rows = refs[-4:]

    @pl.when(pl.program_id(0) == 0)
    def _():
        grad_stream[...] = jnp.zeros_like(grad_stream)
        grad_x[...] = jnp.zeros_like(grad_x)
        grad_tail[...] = jnp.zeros_like(grad_tail)
        rows[...] = jnp.zeros_like(rows)

    dproj = dproj_ref[...].astype(BF)
    xs = xs_ref[...]
    pre = convolved(xs, table_ref)
    sig = jax.nn.sigmoid(pre)
    dpre = (du_ref[...] + right_inner(dproj, x_ref[...])) * (sig + pre * sig * (1.0 - sig))
    dxs = jnp.zeros_like(dpre)
    for k in range(CONV):
        back = CONV - 1 - k
        dxs = dxs + delayed(dpre, -back) * table_ref[k : k + 1, :]
        rows[R + k : R + k + 1, :] += jnp.sum(dpre * delayed(xs, back), axis=0, keepdims=True)
    rows[R + BIAS : R + BIAS + 1, :] += jnp.sum(dpre, axis=0, keepdims=True)
    low = dxs.astype(BF)
    dh = product(low, stream_ref[...]) + product(dz_ref[...], gate_ref[...])
    in_near = item < pl.num_programs(0) // 2

    @pl.when(in_near)
    def _():
        near_ref[...] = dh

    @pl.when(jnp.logical_not(in_near))
    def _():
        far_ref[...] = dh.astype(BF)

    grad_stream[...] += left_outer(low, h_ref[...])
    grad_x[...] += left_outer(low_ref[...], dproj)
    lane = lax.broadcasted_iota(jnp.int32, dproj.shape, 1)
    rank = jnp.where(lane < R, proj_ref[...], 0.0).astype(BF)
    grad_tail[...] += left_outer(ddtp_ref[...], rank)

    @pl.when(pl.program_id(0) == pl.num_programs(0) - 1)
    def _():
        drow = sum(r[...] for r in drows)
        rows[R + STEP_BIAS : R + STEP_BIAS + 1, :] = jnp.sum(drow[:SUB], axis=0, keepdims=True)
        rows[R + SKIP : R + SKIP + 1, :] = jnp.sum(drow[SUB:], axis=0, keepdims=True)
        rows[R + RATE : R + CH, :] = sum(r[...] for r in drates) * -jnp.exp(table_ref[RATE:CH, :])
        grad_tail[...] += rows[...].T
        at = 0
        for grad in grads:
            part = slice(at, at + grad.shape[0])
            grad[:, :D] = grad_stream[part, :].astype(BF)
            grad[:, D : D + LANE] = grad_x[part, :].astype(BF)
            grad[:, D + LANE :] = grad_tail[part, :].astype(BF)
            at += grad.shape[0]


def mix_back(h, xs, du, ddtp, low, proj, dproj, dz, x_full, table, stream, gate, drates, drows, sizes, after):
    tokens, width = xs.shape
    aligned = all(size % 16 == 0 for size in sizes)
    blocks = [shape(size, D + SMALL, BF) for size in (sizes if aligned else [width])]
    near, far = halves(tokens)
    calls = len(drates)
    dh_near, dh_far, *grads = pl.pallas_call(
        lambda *refs: mix_back_body(calls, len(blocks), *refs),
        grid=(tokens // ITEM,),
        in_specs=[item_rows(v) for v in (h, xs, du, ddtp, low, proj, dproj, dz)]
        + [once(v) for v in (x_full, table, stream, gate, *drates, *drows)]
        + [ANYWHERE] * len(after),
        out_specs=[near, far] + [fixed(v) for v in blocks],
        out_shape=[shape(tokens // 2, D), shape(tokens // 2, D, BF)] + blocks,
        scratch_shapes=[
            pltpu.VMEM((width, D), F32), pltpu.VMEM((width, LANE), F32), pltpu.VMEM((width, LANE), F32),
            pltpu.VMEM((LANE, width), F32),
        ],
        compiler_params=PARAMS,
        cost_estimate=cost(19),
        name="mix_back",
    )(h, xs, du, ddtp, low, proj, dproj, dz, x_full, table, stream, gate, *drates, *drows, *after)
    return dh_near, dh_far, parted(grads, sizes)


def scan_prepare(u_ref, proj_ref, dt_ref, table_ref, pre, step, drive, rate, bc):
    pre[...] = right_inner(proj_ref[...].astype(BF), dt_ref[...]) + table_ref[STEP_BIAS : STEP_BIAS + 1, :]
    step[...] = softplus(pre[...])
    drive[...] = step[...] * u_ref[...]
    rate[...] = -jnp.exp(table_ref[RATE:CH, :]) * LOG2E
    turned = proj_ref[...].T
    for g in range(bc.shape[0]):
        bc[g, :, :SUB] = turned[R:, g * SUB : (g + 1) * SUB]


def scan_forward_body(u_ref, proj_ref, dt_ref, table_ref, *refs):
    y_ref, states_ref, pre, step_ref, drive_ref, rate_ref, bc_ref, carry, parts = refs[-9:]
    groups = u_ref.shape[0] // SUB
    chunks = u_ref.shape[1] // LANE

    @pl.when(pl.program_id(1) == 0)
    def _():
        carry[...] = jnp.zeros_like(carry)

    scan_prepare(u_ref, proj_ref, dt_ref, table_ref, pre, step_ref, drive_ref, rate_ref, bc_ref)

    def group(g, _):
        base = pl.multiple_of(g * SUB, SUB)
        step8 = step_ref[pl.ds(base, SUB), :]
        drive8 = drive_ref[pl.ds(base, SUB), :]
        bc = bc_ref[g]
        states = [carry[:, c * LANE : (c + 1) * LANE] for c in range(chunks)]
        for j in range(SUB):
            b = jnp.broadcast_to(bc[:N, j : j + 1], (N, LANE))
            cc = jnp.broadcast_to(bc[N:, j : j + 1], (N, LANE))
            at = pl.multiple_of((base + j) * N, N)
            for c in range(chunks):
                lanes = slice(c * LANE, (c + 1) * LANE)
                step = jnp.broadcast_to(step8[j : j + 1, lanes], (N, LANE))
                drive = jnp.broadcast_to(drive8[j : j + 1, lanes], (N, LANE))
                s = jnp.exp2(step * rate_ref[:, lanes]) * states[c] + b * drive
                states[c] = s
                states_ref[pl.ds(at, N), lanes] = s
                p = cc * s
                parts[c, pl.ds(pl.multiple_of((base + j) * SUB, SUB), SUB), :] = p[:SUB] + p[SUB:]
        for c in range(chunks):
            lanes = slice(c * LANE, (c + 1) * LANE)
            carry[:, lanes] = states[c]
        return 0

    lax.fori_loop(0, groups, group, 0)
    for c in range(chunks):
        lanes = slice(c * LANE, (c + 1) * LANE)
        total = table_ref[SKIP : SKIP + 1, lanes] * u_ref[:, lanes]
        for n in range(SUB):
            total = total + parts[c, pl.ds(n, groups * SUB, stride=SUB), :]
        y_ref[:, lanes] = total


def scan_forward(begin, count, u, proj, dt, table, kept, after):
    total, width = u.shape
    block = SCAN_BLOCK
    steps = ITEM // block
    chunks = width // LANE
    at = lambda i, t: ((begin + i) * steps + t, 0)
    tok = pl.BlockSpec((block, width), at)
    whole = lambda v: pl.BlockSpec(v.shape, lambda i, t: (0, 0))
    extra = list(kept) + list(after)
    return pl.pallas_call(
        scan_forward_body,
        grid=(count, steps),
        in_specs=[tok, pl.BlockSpec((block, LANE), at), whole(dt), whole(table)] + [ANYWHERE] * len(extra),
        out_specs=[tok, pl.BlockSpec((block * N, width), at)],
        out_shape=[shape(total, width), shape(total * N, width)],
        scratch_shapes=[
            *[pltpu.VMEM((block, width), F32)] * 3, pltpu.VMEM((N, width), F32),
            pltpu.VMEM((block // SUB, 2 * N, LANE), F32),
            pltpu.VMEM((N, width), F32), pltpu.VMEM((chunks, (block + 1) * SUB, LANE), F32),
        ],
        input_output_aliases={4 + k: k for k in range(len(kept))},
        compiler_params=PARAMS,
        cost_estimate=cost(8 * count),
        name="scan_forward",
    )(u, proj, dt, table, *extra)


def scan_backward_body(u_ref, proj_ref, dy_ref, states_ref, before_ref, dt_ref, table_ref, *refs):
    du_ref, ddtp_ref, dproj_ref, drate_ref, drow_ref = refs[-16:-11]
    pre, step_ref, drive_ref, rate_ref, bc_ref, carry, parts, parts2, sums, stage, own = refs[-11:]
    block = u_ref.shape[0]
    groups = block // SUB
    chunks = u_ref.shape[1] // LANE
    back = pl.num_programs(1) - 1 - pl.program_id(1)
    first = back == 0

    @pl.when(pl.program_id(1) == 0)
    def _():
        carry[...] = jnp.zeros_like(carry)

    @pl.when((pl.program_id(0) == 0) & (pl.program_id(1) == 0))
    def _():
        drate_ref[...] = jnp.zeros_like(drate_ref)
        drow_ref[...] = jnp.zeros_like(drow_ref)

    scan_prepare(u_ref, proj_ref, dt_ref, table_ref, pre, step_ref, drive_ref, rate_ref, bc_ref)

    def group(k, _):
        g = groups - 1 - k
        base = pl.multiple_of(g * SUB, SUB)
        step8 = step_ref[pl.ds(base, SUB), :]
        drive8 = drive_ref[pl.ds(base, SUB), :]
        dy8 = dy_ref[pl.ds(base, SUB), :]
        bc = bc_ref[g]
        grads = [carry[:, c * LANE : (c + 1) * LANE] for c in range(chunks)]
        drate = [drate_ref[:, c * LANE : (c + 1) * LANE] for c in range(chunks)]
        for j in reversed(range(SUB)):
            b = jnp.broadcast_to(bc[:N, j : j + 1], (N, LANE))
            cc = jnp.broadcast_to(bc[N:, j : j + 1], (N, LANE))
            at = pl.multiple_of((base + j) * N, N)
            db = jnp.zeros((N, LANE), F32)
            dc = jnp.zeros((N, LANE), F32)
            for c in range(chunks):
                lanes = slice(c * LANE, (c + 1) * LANE)
                step = jnp.broadcast_to(step8[j : j + 1, lanes], (N, LANE))
                drive = jnp.broadcast_to(drive8[j : j + 1, lanes], (N, LANE))
                dy = jnp.broadcast_to(dy8[j : j + 1, lanes], (N, LANE))
                now = states_ref[pl.ds(at, N), lanes]
                if j > 0:
                    prev = states_ref[pl.ds(at - N, N), lanes]
                else:
                    prev = states_ref[pl.ds(pl.multiple_of(jnp.maximum(at - N, 0), N), N), lanes]
                    edge = jnp.where(first, 0.0, before_ref[:, lanes])
                    prev = jnp.where(g == 0, edge, prev)
                rate = rate_ref[:, lanes]
                grad = cc * dy + grads[c]
                dc = dc + now * dy
                db = db + grad * drive
                p = grad * b
                parts[c, pl.ds(pl.multiple_of((base + j) * SUB, SUB), SUB), :] = p[:SUB] + p[SUB:]
                grad = grad * jnp.exp2(step * rate)
                grads[c] = grad
                q = grad * prev
                p = q * rate
                parts2[c, pl.ds(pl.multiple_of((base + j) * SUB, SUB), SUB), :] = p[:SUB] + p[SUB:]
                drate[c] = drate[c] + q * step
            token = back * block + base + j
            sums[pl.ds(token, N, stride=PITCH), :] = db
            sums[pl.ds(N * PITCH + token, N, stride=PITCH), :] = dc
        for c in range(chunks):
            lanes = slice(c * LANE, (c + 1) * LANE)
            carry[:, lanes] = grads[c]
            drate_ref[:, lanes] = drate[c]
        return 0

    lax.fori_loop(0, groups, group, 0)
    for c in range(chunks):
        lanes = slice(c * LANE, (c + 1) * LANE)
        x = parts[c, pl.ds(0, block, stride=SUB), :]
        r = parts2[c, pl.ds(0, block, stride=SUB), :]
        for n in range(1, SUB):
            x = x + parts[c, pl.ds(n, block, stride=SUB), :]
            r = r + parts2[c, pl.ds(n, block, stride=SUB), :]
        dy, u, step = dy_ref[:, lanes], u_ref[:, lanes], step_ref[:, lanes]
        du_ref[:, lanes] = step * x + table_ref[SKIP : SKIP + 1, lanes] * dy
        d = (u * x + LN2 * r) * jax.nn.sigmoid(pre[:, lanes])
        ddtp_ref[:, lanes] = d.astype(BF)
        drow_ref[:SUB, lanes] += jnp.sum(d.reshape(groups, SUB, LANE), axis=0)
        drow_ref[SUB:, lanes] += jnp.sum((dy * u).reshape(groups, SUB, LANE), axis=0)
    low = ddtp_ref[...]
    own[pl.ds(pl.multiple_of(back * block, block), block), :] = product(low, dt_ref[...])

    @pl.when(first)
    def _():
        stage[...] = jnp.zeros_like(stage)
        ones = jnp.ones((SUB, LANE), BF)
        for n in range(2 * N):
            wide = sums[n * PITCH : n * PITCH + ITEM, :]
            high = wide.astype(BF)
            row = right_inner(ones, high) + right_inner(ones, (wide - high.astype(F32)).astype(BF))
            stage[R + n : R + n + 1, :] = row[:1]
        dproj_ref[...] = own[...] + stage[...].T


def scan_backward(begin, count, u, proj, dy, states, dt, table, kept, after):
    total, width = u.shape
    block = SCAN_BLOCK
    steps = ITEM // block
    chunks = width // LANE
    place = lambda i, t: (begin + i) * steps + steps - 1 - t
    at = lambda i, t: (place(i, t), 0)
    tok = pl.BlockSpec((block, width), at)
    whole = lambda v: pl.BlockSpec(v.shape, lambda i, t: (0, 0))
    extra = list(kept) + list(after)
    out_shape = [
        shape(total, width), shape(total, width, BF), shape(total, LANE), shape(N, width), shape(2 * SUB, width)
    ]
    return pl.pallas_call(
        scan_backward_body,
        grid=(count, steps),
        in_specs=[
            tok, pl.BlockSpec((block, LANE), at), tok,
            pl.BlockSpec((block * N, width), at),
            pl.BlockSpec((N, width), lambda i, t: (jnp.maximum(place(i, t) * block - 1, 0), 0)),
            whole(dt), whole(table),
        ]
        + [ANYWHERE] * len(extra),
        out_specs=[tok, tok, pl.BlockSpec((ITEM, LANE), lambda i, t: (begin + i, 0)), whole(out_shape[3]), whole(out_shape[4])],
        out_shape=out_shape,
        scratch_shapes=[
            *[pltpu.VMEM((block, width), F32)] * 3, pltpu.VMEM((N, width), F32),
            pltpu.VMEM((block // SUB, 2 * N, LANE), F32), pltpu.VMEM((N, width), F32),
            *[pltpu.VMEM((chunks, (block + 1) * SUB, LANE), F32)] * 2,
            pltpu.VMEM(((2 * N + 1) * PITCH, LANE), F32), pltpu.VMEM((LANE, ITEM), F32), pltpu.VMEM((ITEM, LANE), F32),
        ],
        input_output_aliases={7 + k: k for k in range(len(kept))},
        compiler_params=PARAMS,
        cost_estimate=cost(15 * count),
        name="scan_backward",
    )(u, proj, dy, states, states, dt, table, *extra)


def update_body(factor_ref, *refs):
    grads, states, outs = refs[:5], refs[5:29], refs[29:]
    factor = factor_ref[0, 0]
    ema_keep = min(0.9999, (1.0 + STEP) / (10.0 + STEP))

    def update(k, g):
        learn_rate, weight_decay = (0.5, 0.0) if k == 4 else (0.03, 0.1)
        weight, first, second, average = (states[4 * k + q][...] for q in range(4))
        clipped = g * factor
        first = 0.9 * first + 0.1 * clipped
        second = 0.999 * second + 0.001 * clipped * clipped
        first_hat = first / (1.0 - 0.9**STEP)
        second_hat = second / (1.0 - 0.999**STEP)
        weight = weight - learn_rate * (first_hat / (jnp.sqrt(second_hat) + 1e-08) + weight_decay * weight)
        average = ema_keep * average + (1.0 - ema_keep) * weight
        for q, v in enumerate((first, second, weight, average)):
            outs[4 * k + q][...] = v

    ada, wide, small, small_t, out = grads
    update(0, ada[...])
    update(1, wide[...].astype(F32))
    update(5, out[...].astype(F32))

    @pl.when(pl.program_id(0) == 0)
    def _():
        update(2, small[...])
        update(3, small_t[:R, :])
        update(4, small_t[R:CH + R, :])


def update_all(factor, ada, wide, small, small_t, out, states):
    part = 256
    right = lambda v: pl.BlockSpec((v.shape[0], part), lambda t: (0, t))
    kinds = [right, right, fixed, fixed, fixed, right]
    specs = [kind(v) for kind, group in zip(kinds, states) for v in group]
    flat = [v for group in states for v in group]
    return pl.pallas_call(
        update_body,
        grid=(D // part,),
        in_specs=[pl.BlockSpec(memory_space=pltpu.SMEM), right(ada), right(wide), fixed(small), fixed(small_t), right(out)]
        + specs,
        out_specs=specs,
        out_shape=[shape(*v.shape) for v in flat],
        compiler_params=PARAMS,
        cost_estimate=cost(11),
        name="update",
    )(factor.reshape(1, 1), ada, wide, small, small_t, out, *flat)


def embed_time(steps):
    half = D // 2
    freqs = jnp.exp(-math.log(10000.0) * jnp.arange(half, dtype=F32) / half)
    angles = steps.astype(F32)[:, None] * freqs[None, :]
    return jax.nn.silu(jnp.concatenate([jnp.cos(angles), jnp.sin(angles)], axis=1))


def normalize(x):
    mean = jnp.mean(x, axis=2, keepdims=True)
    centered = x - mean
    var = jnp.mean(centered * centered, axis=2, keepdims=True)
    scale = lax.rsqrt(var + 1e-06)
    return centered * scale, scale


def group_bits(size):
    return [1 << k for k in reversed(range(size.bit_length() - 1))]


def moved(v, axes, pairs):
    return lax.ppermute(with_layout_constraint(v, Layout(tuple(range(v.ndim)))), axes, pairs)


def swap(v, bit, size):
    return moved(v, "fsdp", [(i, i ^ bit) for i in range(size)])


def tick(v, size):
    return swap(v[:16, :LANE], 1, size)


def group_gather(v, size):
    blocks = [v]
    for bit in group_bits(size):
        blocks += [swap(b, bit, size) for b in blocks]
    return blocks


def group_sum(v, size):
    bits = group_bits(size)
    half = v.shape[0] // 2
    other = swap(v[half:], bits[-1], size)
    total = v[:half] + other
    for k, bit in enumerate(bits[:-1]):
        other = swap(total, bit, size)
        rows = other.shape[0] // (size // 2)
        total = total + jnp.concatenate(
            [other[(p ^ (1 << k)) * rows : ((p ^ (1 << k)) + 1) * rows] for p in range(size // 2)], axis=0
        )
    return jnp.concatenate([total, swap(total, bits[-1], size)], axis=0), other


def ring_order(size):
    if size == 8:
        return [0, 2, 4, 6, 7, 5, 3, 1]
    return list(range(size))


def ring_move(v, way, size):
    order = ring_order(size)
    return moved(v, "dp", [(order[p], order[(p + way) % size]) for p in range(size)])


def ring_gather_steps(v, size, split):
    behind = ahead = v
    for _ in range(size // 2 - 1):
        behind, ahead = ring_move(behind, 1, size), ring_move(ahead, -1, size)
        yield [behind, ahead]
    cut = v.shape[0] // 2
    if split:
        yield [ring_move(behind[:cut], 1, size), ring_move(ahead[cut:], -1, size)]
    else:
        yield [ring_move(behind, 1, size)]


def ring_partial(blocks, step, came, after):
    size = len(blocks) - 1
    if step == 0:
        return blocks[-2:]
    away = size // 2 - step
    ahead, behind = blocks[2 * away], blocks[2 * away - 1]
    if all(v.shape[0] % 16 == 0 for v in came):
        return ring_add(ahead, behind, *came, after)
    add = lambda a, b: (a.astype(F32) + b.astype(F32)).astype(BF)
    up, down = came
    if step == 1:
        cut = up.shape[0]
        return [
            jnp.concatenate([add(ahead[:cut], up), ahead[cut:]], axis=0),
            jnp.concatenate([behind[:-cut], add(behind[-cut:], down)], axis=0),
        ]
    return [add(ahead, up), add(behind, down)]


def ring_send(partial):
    size = lax.axis_size("dp")
    return [ring_move(partial[0], 1, size), ring_move(partial[1], -1, size)]


def ring_last(blocks, came):
    return blocks[0].astype(F32) + came[0].astype(F32) + came[1].astype(F32)


def exchange(v):
    return lax.all_to_all(v, ALL, 0, 0, tiled=True)


def on_device(sizes, *args):
    (
        act, cotangent, item_counts, item_lengths, time_steps,
        ada_weight, ada_first, ada_second, ada_average,
        in_weight, in_first, in_second, in_average,
        x_weight, x_first, x_second, x_average,
        dt_weight, dt_first, dt_second, dt_average,
        chan_table, chan_first, chan_second, chan_average,
        out_weight, out_first, out_second, out_average,
    ) = args
    n_dp, n_fsdp = sizes
    devices = n_dp * n_fsdp
    count = item_lengths.shape[0]
    items = count * n_fsdp
    tokens = items * ITEM
    ada_cols = ada_weight.shape[1]
    f = lax.axis_index("fsdp")
    half = n_dp // 2
    low_half = lax.axis_index("dp") < half
    offsets = [0]
    for bit in group_bits(n_fsdp):
        offsets = offsets + [o ^ bit for o in offsets]

    forth = []
    for b in range(devices):
        i, j = divmod(b, 2)
        k, g = divmod(i, n_fsdp)
        forth.append((b, (k + half * j) * n_fsdp + g))
    back = [(t, s) for s, t in forth]
    across = [(q, (q + half) % n_dp) for q in range(n_dp)]
    wide = in_weight.astype(BF).T
    rows = wide.shape[0] // 2
    leaving = jnp.where(low_half, wide[rows:], wide[:rows])
    swapped = moved(leaving, "dp", across)
    small = jnp.concatenate([x_weight.astype(BF), dt_weight.astype(BF).T, chan_table.astype(BF).T], axis=1)
    small = jnp.pad(small, ((0, 0), (0, SMALL - small.shape[1])))
    small = moved(hold(small, leaving), ALL, forth)
    stream_own = jnp.concatenate([jnp.where(low_half, wide[:rows], swapped), small], axis=1)
    gate_own = jnp.where(low_half, swapped, wide[rows:])

    live_items = jnp.arange(count, dtype=jnp.int32) < item_counts[0]
    live_rows = jnp.arange(ITEM, dtype=jnp.int32)[None, :] < item_lengths[:, None]
    live = live_items[:, None] & live_rows
    dfinal_own = jnp.where(live[..., None], cotangent.reshape(count, ITEM, D), jnp.zeros((), BF))
    x_all = group_gather(act.reshape(count * ITEM, D), n_fsdp)

    steps_all = exchange(hold(jnp.broadcast_to(time_steps[None], (devices, count)), leaving)).reshape(-1)
    cond_all = embed_time(steps_all).astype(BF)
    mod_cols = product(cond_all, ada_weight.astype(BF)).reshape(n_dp, 1, items, ada_cols)
    mod_cols = jnp.broadcast_to(mod_cols, (n_dp, n_fsdp, items, ada_cols)).reshape(devices, items, ada_cols)
    mod = exchange(hold(mod_cols, tick(stream_own, n_fsdp)))
    mod = jnp.swapaxes(mod, 0, 1).reshape(n_fsdp, count, 3 * D)
    mod = jnp.take(mod, jnp.array(offsets, jnp.int32) ^ f, axis=0).reshape(items, 3 * D)

    stream = [stream_own]
    for came in ring_gather_steps(stream_own, n_dp, False):
        stream += came
    dfinal_all = group_gather(hold(dfinal_own.reshape(count * ITEM, D), stream[2]), n_fsdp)
    out_own = moved(hold(out_weight.astype(BF), stream[half - 1]), ALL, forth)
    rest_own = hold(jnp.concatenate([gate_own, out_own], axis=1), tick(stream[-2], n_fsdp))
    rest_steps = list(ring_gather_steps(rest_own, n_dp, True))
    rest = [rest_own] + sum(rest_steps, [])

    h_low, xs, u, u_low, proj, stream_full, x_full, dt_full, table = mix(x_all, mod, stream, [rest_own, *dfinal_all])
    proj, _ = group_sum(hold(proj, *rest_steps[0]), n_fsdp)
    calls = 2
    part = items // calls
    kept = []
    for i in range(calls):
        kept = scan_forward(i * part, part, u, proj, dt_full, table, kept, rest_steps[half // 2 - 1 + i])
    y, states = kept

    dy, dz_low, o_own, o_far, gate_full, early = gates(h_low, dfinal_all, mod, y, rest)
    bits = group_bits(n_fsdp)[::-1]
    kept, drates, drows, came, o_came = [], [], [], None, None
    for i, (begin, some) in enumerate(((0, 1), (1, items - 2), (items - 1, 1))):
        partial = ring_partial(early, i, came, drates[-1:])
        came = ring_send(partial)
        *kept, drate, drow = scan_backward(
            begin, some, u, proj, dy, states, dt_full, table, kept, [*partial, *([] if i else [o_far])]
        )
        drates.append(drate)
        drows.append(drow)
        if i == 0:
            o_came = swap(o_far, bits[0], n_fsdp)
    beside, calls = came, len(drates)
    leaving = ring_partial(early, calls, came, drates[-1:])
    came = ring_send(leaving)
    du_scan, ddtp_low, dproj = kept

    dproj, other = group_sum(hold(dproj, *beside), n_fsdp)
    for bit in bits[1:]:
        o_own, o_far = fold(o_own, o_came, [other])
        o_came = swap(o_far, bit, n_fsdp)
    o_own = o_own.astype(F32) + o_came.astype(F32)

    def to_owners(early_sum):
        sums = early_sum[:, :D].astype(BF), early_sum[:, D:].astype(BF)
        return sums, (moved(sums[0], "dp", [(q, q + half) for q in range(half)]), moved(sums[1], ALL, back))

    if half == calls + 1:
        early_sum = ring_last(early, came)
        leaving, arrived = to_owners(early_sum)
    else:
        arrived = came
    dh, dh_far, late = mix_back(
        h_low, xs, du_scan, ddtp_low, u_low, proj, dproj, dz_low, x_full, table, stream_full, gate_full,
        drates, drows, ring_sizes(rows, n_dp), [o_far, *leaving]
    )
    dh_far, *late[-2:] = [hold(v, *arrived, o_came) for v in (dh_far, *late[-2:])]
    came, dh_came = None, None
    for i in range(half):
        if 0 < i < len(bits):
            dh, dh_far = fold(dh, dh_came, [])
        after = [dh_far] if i == 1 else [dh_came] if i == half - 1 else []
        came = ring_send(ring_partial(late, i, came, after))
        if i < len(bits):
            dh_came = swap(dh_far, bits[i], n_fsdp)
    dh = dh + dh_came.astype(F32)
    late_sum = ring_last(late, came)
    if half == calls + 1:
        (gate_sum, _), (gate_moved, out_share) = leaving, arrived
    else:
        came = arrived
        for i in range(calls + 1, half):
            came = ring_send(ring_partial(early, i, came, [late_sum]))
        early_sum = ring_last(early, came)
        (gate_sum, _), (gate_moved, out_share) = to_owners(early_sum)
    squares = jnp.sum(early_sum * early_sum) + jnp.sum(late_sum * late_sum)
    small = moved(late_sum[:, D:].astype(BF), ALL, back).astype(F32)
    small_t = small[:, LANE:].T
    late_sum = late_sum[:, :D].astype(BF)
    late_moved = moved(late_sum, "dp", [(q + half, q) for q in range(half)])
    in_share = jnp.concatenate(
        [jnp.where(low_half, late_sum, gate_moved), jnp.where(low_half, late_moved, gate_sum)], axis=0
    )
    dh, o_own = dh.reshape(count, ITEM, D), o_own.reshape(count, ITEM, D)

    x = act.astype(F32).reshape(count, ITEM, D)
    normed, inverse = normalize(x)
    dfinal = dfinal_own.astype(F32)
    scale, gate = mod[:count, None, D : 2 * D], mod[:count, None, 2 * D :]
    final = x + gate * o_own
    dmod = jnp.concatenate(
        [jnp.sum(dh, axis=1), jnp.sum(dh * normed, axis=1), jnp.sum(dfinal * o_own, axis=1)], axis=1
    ).astype(BF)
    dn = dh * (1.0 + scale)
    act_grad = dfinal + inverse * (
        dn - jnp.mean(dn, axis=2, keepdims=True) - normed * jnp.mean(dn * normed, axis=2, keepdims=True)
    )
    dmod = hold(dmod, late_sum)
    dmod_all = exchange(jnp.swapaxes(dmod.reshape(count, devices, ada_cols), 0, 1)).reshape(devices * count, ada_cols)
    ada_share = left_outer(dmod_all, cond_all)

    local = squares + jnp.sum(ada_share * ada_share)
    total = jnp.sum(exchange(jnp.broadcast_to(local, (devices, LANE)))[:, 0])
    grad_norm = jnp.sqrt(total)
    factor = jnp.minimum(1.0, 1.0 / (grad_norm + 1e-06))
    results = update_all(
        factor, ada_share, in_share, small[:, :LANE], small_t, out_share,
        (
            (ada_weight.T, ada_first.T, ada_second.T, ada_average.T),
            (in_weight.T, in_first.T, in_second.T, in_average.T),
            (x_weight, x_first, x_second, x_average),
            (dt_weight, dt_first, dt_second, dt_average),
            (chan_table, chan_first, chan_second, chan_average),
            (out_weight, out_first, out_second, out_average),
        ),
    )
    results = [v.T for v in results[:8]] + list(results[8:])
    return (final.reshape(count * ITEM, D), act_grad.reshape(count * ITEM, D), grad_norm, *results)


def solution(mesh):
    sizes = (mesh.shape["dp"], mesh.shape["fsdp"])
    first, second = P(ALL, None), P(None, ALL)
    weights = [second] * 8 + [first] * 4 + [second] * 8 + [first] * 4
    return jax.shard_map(
        lambda *args: on_device(sizes, *args),
        mesh=mesh,
        in_specs=(first, first, P(ALL), P(ALL), P(ALL), *weights),
        out_specs=(first, first, P(), *weights),
        check_vma=False,
    )
```
